32 devices in a mesh: dp: 4 (over y, core), seq: 8 (over z, x).
Axes of the slice: x: 2, y: 2, z: 4, core: 2. Of those that a mesh axis runs over, the one named last changes fastest.
Arguments:
- tokens: bfloat16 [8192, 640], P(('dp', 'seq')), may hold values from -6 to 6
- positions: int32 [8192], P(('dp', 'seq')), may hold values from 0 to 2047, as said below
- cotangent: bfloat16 [8192, 640], P(('dp', 'seq')), may hold values from -6 to 6
- w_query: bfloat16 [655360], P(('dp', 'seq')), may hold values from -0.25 to 0.25
- w_key: bfloat16 [163840], P(('dp', 'seq')), may hold values from -0.25 to 0.25
- w_value: bfloat16 [163840], P(('dp', 'seq')), may hold values from -0.25 to 0.25
- w_out: bfloat16 [655360], P(('dp', 'seq')), may hold values from -0.1875 to 0.1875
- w_gate: bfloat16 [1310720], P(('dp', 'seq')), may hold values from -0.25 to 0.25
- w_up: bfloat16 [1310720], P(('dp', 'seq')), may hold values from -0.25 to 0.25
- w_down: bfloat16 [1310720], P(('dp', 'seq')), may hold values from -0.125 to 0.125
- gains: bfloat16 [3072], P(('dp', 'seq')), may hold values from 0.099609375 to 1.8984375
Outputs:
- layer_out: bfloat16 [8192, 640], P(('dp', 'seq'))
- input_grad: float32 [8192, 640], P(('dp', 'seq'))
- grad_query: float32 [655360], P(('dp', 'seq'))
- grad_key: float32 [163840], P(('dp', 'seq'))
- grad_value: float32 [163840], P(('dp', 'seq'))
- grad_out: float32 [655360], P(('dp', 'seq'))
- grad_gate: float32 [1310720], P(('dp', 'seq'))
- grad_up: float32 [1310720], P(('dp', 'seq'))
- grad_down: float32 [1310720], P(('dp', 'seq'))
- grad_gains: float32 [3072], P(('dp', 'seq'))
The draws below stay inside these ranges and needn't reach their ends.
Inputs may be any that keep to these rules, and one draw needn't show every extreme that they name: Each of the 4 sequences of 2048 tokens (token t belongs to sequence t // 2048) is cut into one to three contiguous documents; positions count 0, 1, 2, ... from each document's first token. One document of each sequence begins within the sequence's first half of 256 tokens and ends within its last half of 256 tokens. One sequence is a single document.
All inputs are finite; a program needn't handle non-finite values.
Results may differ from the reference program's by a relative error of at most 0.017.
Values may be sent and summed in bfloat16 or wider, within the bound.
No kernel may reach another device: no remote copies, remote signals or barrier semaphores. Data moves between devices by JAX's collectives and lax.ppermute only.
A program may use at most 128 MiB of HBM per device.

```python
import jax
import jax.numpy as jnp
from jax import lax

D = 640
HEADS = 4
HD = 256
FF = 2048
WIN = 512
BLK = 256
SEQ_LEN = 2048
SEQS = 4
TOKENS = 8192
GAINS = 3072


def draw_positions(key, part):
    key = jax.random.fold_in(key, 7)
    head_key, tail_key, single_key = jax.random.split(key, 3)
    head_cut = jax.random.randint(head_key, (SEQS, 1), 0, BLK // 2, dtype=jnp.int32)
    tail_cut = SEQ_LEN - jax.random.randint(tail_key, (SEQS, 1), 0, BLK // 2, dtype=jnp.int32)
    single_seq = jax.random.randint(single_key, (), 0, SEQS, dtype=jnp.int32)
    is_single = jnp.arange(SEQS, dtype=jnp.int32)[:, None] == single_seq
    head_cut = jnp.where(is_single, 0, head_cut)
    tail_cut = jnp.where(is_single, SEQ_LEN, tail_cut)
    token_index = jnp.arange(SEQ_LEN, dtype=jnp.int32)[None, :]
    doc_first = jnp.where(token_index < head_cut, 0, jnp.where(token_index < tail_cut, head_cut, tail_cut))
    return (token_index - doc_first).reshape(SEQS * SEQ_LEN).astype(jnp.int32)


def block_levels(rng, shape, cuts, low, high):
    def one(position, blocks):
        heights = jax.random.uniform(jax.random.fold_in(jax.random.fold_in(rng, 6), position), (blocks,), jnp.float32, low / len(cuts), high / len(cuts))
        return jnp.repeat(jnp.exp(heights), shape[position] // blocks).reshape((-1,) + (1,) * (len(shape) - position - 1))

    factor_of = one(*cuts[0])
    for cut in cuts[1:]:
        factor_of = factor_of * one(*cut)
    return factor_of


def scatter_about(rng, shape, width, limit, shards=(), kind=jnp.bfloat16):
    values = width * jax.random.normal(rng, shape, jnp.float32)
    if shards:
        values = values * block_levels(rng, shape, shards, -0.22, 0.18)
    return jnp.clip(values, -limit, limit).astype(kind)


def setup_inputs(seed: int = 0) -> dict:
    arg_keys = jax.random.split(jax.random.key(seed), 12)
    tokens = scatter_about(arg_keys[0], (TOKENS, D), 1.0, 6.0, ((0, 32),))
    positions = draw_positions(jax.random.fold_in(arg_keys[11], 71), 0)
    cotangent = scatter_about(arg_keys[2], (TOKENS, D), 1.0, 6.0, ((0, 32),))
    w_query = scatter_about(arg_keys[3], (D * HEADS * HD,), D ** -0.5, 0.25, ((0, 32),))
    w_key = scatter_about(arg_keys[4], (D * HD,), D ** -0.5, 0.25, ((0, 32),))
    w_value = scatter_about(arg_keys[5], (D * HD,), D ** -0.5, 0.25, ((0, 32),))
    w_out = scatter_about(arg_keys[6], (HEADS * HD * D,), (HEADS * HD) ** -0.5, 0.1875, ((0, 32),))
    w_gate = scatter_about(arg_keys[7], (D * FF,), D ** -0.5, 0.25, ((0, 32),))
    w_up = scatter_about(arg_keys[8], (D * FF,), D ** -0.5, 0.25, ((0, 32),))
    w_down = scatter_about(arg_keys[9], (FF * D,), FF ** -0.5, 0.125, ((0, 32),))
    gains = jnp.clip(1.0 + 0.18 * jax.random.normal(arg_keys[10], (GAINS,), jnp.float32), 0.099609375, 1.8984375).astype(jnp.bfloat16)
    return {"tokens": tokens, "positions": positions, "cotangent": cotangent, "w_query": w_query, "w_key": w_key, "w_value": w_value, "w_out": w_out, "w_gate": w_gate, "w_up": w_up, "w_down": w_down, "gains": gains}


@jax.custom_vjp
def low(v):
    return lax.optimization_barrier(v.astype(jnp.bfloat16)).astype(jnp.float32)

@jax.custom_vjp
def low_back(v):
    return v

def low_keep(v):
    return (low(v), None)

def low_pass(kept, grad):
    return (grad,)

def back_keep(v):
    return (v, None)

def back_low(kept, grad):
    return (low(grad),)
low.defvjp(low_keep, low_pass)
low_back.defvjp(back_keep, back_low)
epsilon = 1e-06
lowest = -1e+30

def matmul(left_rows, right_rows):
    return jnp.dot(left_rows, right_rows, precision=lax.Precision.HIGHEST, preferred_element_type=jnp.float32)

def norm_rows(values, gain_row):
    inverse = lax.rsqrt(lax.optimization_barrier(jnp.mean(values * values, axis=-1, keepdims=True)) + epsilon)
    return values * inverse * gain_row

def rotate(values, cos_rows, sin_rows):
    middle_at = values.shape[-1] // 2
    first_half = values[..., :middle_at]
    second_half = values[..., middle_at:]
    return jnp.concatenate([first_half * cos_rows - second_half * sin_rows, second_half * cos_rows + first_half * sin_rows], axis=-1)

def attend_block(block_id, query_low, key_pad, value_pad, doc_start):
    span = min(512, SEQ_LEN)
    start = block_id * span
    query_part = lax.dynamic_slice_in_dim(query_low, start, span, 0)
    key_part = lax.dynamic_slice_in_dim(key_pad, start, span + WIN, 0)
    value_part = lax.dynamic_slice_in_dim(value_pad, start, span + WIN, 0)
    start_part = lax.dynamic_slice_in_dim(doc_start, start, span, 0)
    query_index = start + jnp.arange(span, dtype=jnp.int32)
    key_index = start - WIN + jnp.arange(span + WIN, dtype=jnp.int32)
    allowed = (key_index[None, :] <= query_index[:, None]) & (key_index[None, :] > query_index[:, None] - WIN) & (key_index[None, :] >= start_part[:, None])
    scores = low_back(jnp.einsum('qhd,kd->hqk', query_part, key_part, precision=lax.Precision.HIGHEST))
    scores = jnp.where(allowed[None], scores, lowest)
    row_max = lax.optimization_barrier(jnp.max(scores, axis=-1, keepdims=True))
    expo_rows = jnp.exp(scores - row_max)
    probs = expo_rows / lax.optimization_barrier(jnp.sum(expo_rows, axis=-1, keepdims=True))
    return jnp.einsum('hqk,kd->qhd', low(probs), value_part, precision=lax.Precision.HIGHEST)

def attention(query_low, key_low, value_low, places):
    span = min(512, SEQ_LEN)
    key_pad = jnp.pad(key_low, ((WIN, 0), (0, 0)))
    value_pad = jnp.pad(value_low, ((WIN, 0), (0, 0)))
    doc_start = jnp.arange(SEQ_LEN, dtype=jnp.int32) - places
    checked = jax.checkpoint(attend_block)
    blocks = lax.map(lambda block_id: checked(block_id, query_low, key_pad, value_pad, doc_start), jnp.arange(SEQ_LEN // span, dtype=jnp.int32))
    return blocks.reshape(SEQ_LEN, HEADS, HD)

def layer(inputs, places, weights):
    query_f, key_f, value_f, out_f, gate_f, up_f, down_f, gain_all = weights
    query_w = query_f.reshape(D, HEADS * HD)
    key_w = key_f.reshape(D, HD)
    value_w = value_f.reshape(D, HD)
    out_w = out_f.reshape(HEADS * HD, D)
    gate_w = gate_f.reshape(D, FF)
    up_w = up_f.reshape(D, FF)
    down_w = down_f.reshape(FF, D)
    attn_in_g = gain_all[0:D]
    attn_out_g = gain_all[D:2 * D]
    ffn_in_g = gain_all[2 * D:3 * D]
    ffn_out_g = gain_all[3 * D:4 * D]
    query_g = gain_all[4 * D:4 * D + HD]
    key_g = gain_all[4 * D + HD:4 * D + 2 * HD]
    normed_one = low(norm_rows(inputs, attn_in_g))
    query_raw = low_back(matmul(normed_one, query_w)).reshape(SEQ_LEN, HEADS, HD)
    key_raw = low_back(matmul(normed_one, key_w))
    value_low = low(low_back(matmul(normed_one, value_w)))
    freq_table = 10000.0 ** (-2.0 * jnp.arange(HD // 2, dtype=jnp.float32) / HD)
    angle_rows = places.astype(jnp.float32)[:, None] * freq_table[None, :]
    cos_rows = jnp.cos(angle_rows)
    sin_rows = jnp.sin(angle_rows)
    query_low = low(rotate(norm_rows(query_raw, query_g), cos_rows[:, None, :], sin_rows[:, None, :]) * HD ** (-0.5))
    key_low = low(rotate(norm_rows(key_raw, key_g), cos_rows, sin_rows))
    heads_out = attention(query_low, key_low, value_low, places)
    heads_out = low(low_back(heads_out.reshape(SEQ_LEN, HEADS * HD)))
    branch_one = norm_rows(low_back(matmul(heads_out, out_w)), attn_out_g)
    middle = inputs + branch_one
    normed_two = low(norm_rows(middle, ffn_in_g))
    gate_pre = low_back(matmul(normed_two, gate_w))
    up_pre = low_back(matmul(normed_two, up_w))
    hidden = low(jax.nn.gelu(gate_pre, approximate=True) * up_pre)
    branch_two = norm_rows(low_back(matmul(hidden, down_w)), ffn_out_g)
    return middle + branch_two

def reference(tokens, positions, cotangent, w_query, w_key, w_value, w_out, w_gate, w_up, w_down, gains):
    weights = tuple((weight_arg.astype(jnp.float32) for weight_arg in (w_query, w_key, w_value, w_out, w_gate, w_up, w_down, gains)))
    inputs = tokens.astype(jnp.float32).reshape(SEQS, SEQ_LEN, D)
    places = positions.reshape(SEQS, SEQ_LEN)
    checked_layer = jax.checkpoint(layer)

    def whole(inputs_all, weights_all):
        return lax.map(lambda seq_pair: checked_layer(seq_pair[0], seq_pair[1], weights_all), (inputs_all, places))
    outputs, pullback = jax.vjp(whole, inputs, weights)
    input_grad, weight_grads = pullback(cotangent.astype(jnp.float32).reshape(SEQS, SEQ_LEN, D))
    return (outputs.reshape(TOKENS, D).astype(jnp.bfloat16), input_grad.reshape(TOKENS, D), weight_grads[0], weight_grads[1], weight_grads[2], weight_grads[3], weight_grads[4], weight_grads[5], weight_grads[6], weight_grads[7])
```

```python
import numpy as np
import jax
import jax.numpy as jnp
from jax import lax
from jax.sharding import PartitionSpec as P

D = 640
HEADS = 4
HD = 256
FF = 2048
WIN = 512
BLK = 256
BACK = 2
AXES = ("dp", "seq")
F32 = jnp.float32
BF16 = jnp.bfloat16

epsilon = 1e-06
lowest = -1e30


def exchanged(value, bit):
    count = lax.axis_size("dp") * lax.axis_size("seq")
    return lax.ppermute(value, AXES, [(i, i ^ (1 << bit)) for i in range(count)])


def stage_orders():
    seq_bits = lax.axis_size("seq").bit_length() - 1
    low, core, high = 0, seq_bits, seq_bits + 1
    upper = list(range(seq_bits - 1, 0, -1))
    return (upper + [low, high, core], upper + [high, low, core], [low, high] + upper + [core])


def slot_shards(order):
    shards = np.zeros((1,), np.int32)
    for bit in order:
        shards = np.concatenate([shards, shards ^ (1 << bit)])
    return shards


def slot_permutation(order, me):
    shards = slot_shards(order)
    rows = D // len(shards)
    target = (jnp.asarray(shards) ^ me)[:, None] * rows + jnp.arange(rows, dtype=jnp.int32)[None, :]
    return (jnp.arange(D, dtype=jnp.int32)[:, None] == target.reshape(1, D)).astype(BF16)


def passed_along(value, axis, steps):
    count = lax.axis_size(axis)
    first, last = (max(0, -steps), min(count, count - steps))
    return lax.ppermute(value, axis, [(source, source + steps) for source in range(first, last)])


def rms_forward(values, gain_row):
    inverse = lax.rsqrt(jnp.mean(values * values, axis=-1, keepdims=True) + epsilon)
    unit_rows = values * inverse
    return (unit_rows * gain_row, unit_rows, inverse)


def rms_backward(incoming, unit_rows, inverse, gain_row):
    leading = tuple(range(incoming.ndim - 1))
    gain_grad = jnp.sum(incoming * unit_rows, axis=leading)
    scaled = incoming * gain_row
    value_grad = inverse * (
        scaled - unit_rows * jnp.mean(scaled * unit_rows, axis=-1, keepdims=True)
    )
    return (value_grad, gain_grad)


def rotate(values, cos_rows, sin_rows):
    middle_at = values.shape[-1] // 2
    first_half = values[..., :middle_at]
    second_half = values[..., middle_at:]
    return jnp.concatenate(
        [
            first_half * cos_rows - second_half * sin_rows,
            second_half * cos_rows + first_half * sin_rows,
        ],
        axis=-1,
    )


def dot(left, right, left_dim=1, right_dim=0):
    return lax.dot_general(
        left, right, (((left_dim,), (right_dim,)), ((), ())), preferred_element_type=F32
    )


def geglu(gate_in, up_in):
    return jax.nn.gelu(gate_in, approximate=True) * up_in


def gather_rows(piece, order):
    for bit in order:
        piece = jnp.concatenate([piece, exchanged(piece, bit)], axis=0)
    return piece


def gather_natural(piece, order, me):
    taken = []
    for bit in order:
        other = exchanged(piece, bit)
        mine_first = (me >> bit) & 1 == 0
        at = sum(1 for b in taken if b > bit)
        piece = jnp.stack(
            [jnp.where(mine_first, piece, other), jnp.where(mine_first, other, piece)], axis=at
        )
        taken.append(bit)
    return piece.reshape(-1, piece.shape[-1])


def reduce_rows(keep, send, order):
    bits = list(reversed(order))
    for at, bit in enumerate(bits):
        total = keep + exchanged(send, bit).astype(F32)
        if at + 1 < len(bits):
            half = total.shape[0] // 2
            keep, send = total[:half], total[half:].astype(BF16)
    return total


def reduce_natural(whole, order, me):
    count = len(order)
    total = whole.reshape((2,) * count + (-1, whole.shape[-1]))
    left = list(range(count - 1, -1, -1))
    for bit in reversed(order):
        at = left.index(bit)
        mine = (me >> bit) & 1
        keep = lax.dynamic_index_in_dim(total, mine, at, keepdims=False)
        send = lax.dynamic_index_in_dim(total, 1 - mine, at, keepdims=False).astype(BF16)
        total = keep + exchanged(send, bit).astype(F32)
        left.remove(bit)
    return total


def local(
    tokens, positions, cotangent, w_query, w_key, w_value, w_out, w_gate, w_up, w_down, gains
):
    order_a, order_b, order_c = stage_orders()
    count = 1 << len(order_a)
    rows = D // count
    me = lax.axis_index(AXES)
    gain_each = gains.shape[0]
    split_at = len(order_a) - 3
    first_bits = order_a[:split_at]

    gain_block = jnp.pad(gains[None, :], ((0, rows - 1), (0, 128 - gain_each)))
    attn_piece = jnp.concatenate(
        [
            w_query.reshape(rows, HEADS * HD),
            w_key.reshape(rows, HD),
            w_value.reshape(rows, HD),
            gain_block,
        ],
        axis=1,
    )
    attn_piece = gather_rows(attn_piece, first_bits)
    query_w = gather_rows(attn_piece[:, : HEADS * HD], order_a[split_at:])
    kvg_w = gather_rows(attn_piece[:, HEADS * HD :], order_b[split_at:])
    out_w = gather_natural(w_out.reshape(-1, D), order_c, me)
    ffn_piece = jnp.concatenate([w_gate.reshape(rows, FF), w_up.reshape(rows, FF)], axis=1)
    ffn_piece = gather_rows(ffn_piece, first_bits)
    gate_w = gather_rows(ffn_piece[:, :FF], order_a[split_at:])
    up_w = gather_rows(ffn_piece[:, FF:], order_b[split_at:])
    down_w = gather_natural(w_down.reshape(-1, D), order_c, me)

    perm_a = slot_permutation(order_a, me)
    perm_b = slot_permutation(order_b, me)
    slot_of = jnp.arange(D, dtype=jnp.int32) // rows
    owner = jnp.asarray(slot_shards(order_b))[slot_of] ^ me
    gain_pick = (
        (owner[None, :] == jnp.arange(count, dtype=jnp.int32)[:, None])
        & (jnp.arange(D, dtype=jnp.int32) % rows == 0)[None, :]
    )
    gain_all = dot(gain_pick.astype(BF16), kvg_w[:, 2 * HD :])[:, :gain_each].reshape(-1)
    attn_in_g, attn_out_g, ffn_in_g, ffn_out_g = (gain_all[i * D : (i + 1) * D] for i in range(4))
    query_g, key_g = gain_all[4 * D : 4 * D + HD], gain_all[4 * D + HD :]
    kv_w = kvg_w[:, : 2 * HD]

    inputs = tokens.astype(F32)
    norm_one, unit_one, inv_one = rms_forward(inputs, attn_in_g)
    normed_one = norm_one.astype(BF16)
    normed_one_a = dot(normed_one, perm_a).astype(BF16)
    normed_one_b = dot(normed_one, perm_b).astype(BF16)
    query_raw = dot(normed_one_a, query_w).reshape(BLK, HEADS, HD)
    kv_raw = dot(normed_one_b, kv_w)
    key_raw = kv_raw[:, :HD]
    value_low = kv_raw[:, HD:].astype(BF16)
    freq_table = 10000.0 ** (-2.0 * jnp.arange(HD // 2, dtype=F32) / HD)
    angle_rows = positions.astype(F32)[:, None] * freq_table[None, :]
    cos_rows = jnp.cos(angle_rows)
    sin_rows = jnp.sin(angle_rows)
    query_scale = HD ** (-0.5)
    query_norm, query_unit, query_inv = rms_forward(query_raw, query_g)
    query_low = (
        rotate(query_norm, cos_rows[:, None, :], sin_rows[:, None, :]) * query_scale
    ).astype(BF16)
    key_norm, key_unit, key_inv = rms_forward(key_raw, key_g)
    key_low = rotate(key_norm, cos_rows, sin_rows).astype(BF16)
    kv_low = jnp.concatenate([key_low, value_low], axis=1)
    earlier = [passed_along(kv_low, "seq", back_step) for back_step in range(BACK, 0, -1)]
    keys_all = jnp.concatenate([e[:, :HD] for e in earlier] + [key_low], axis=0)
    values_all = jnp.concatenate([e[:, HD:] for e in earlier] + [value_low], axis=0)
    block_index = lax.axis_index("seq")
    query_index = block_index * BLK + jnp.arange(BLK, dtype=jnp.int32)
    key_index = block_index * BLK - BACK * BLK + jnp.arange((BACK + 1) * BLK, dtype=jnp.int32)
    doc_start = query_index - positions
    allowed = (
        (key_index[None, :] <= query_index[:, None])
        & (key_index[None, :] > query_index[:, None] - WIN)
        & (key_index[None, :] >= doc_start[:, None])
    )
    raw_scores = jnp.einsum("qhd,kd->hqk", query_low, keys_all, preferred_element_type=F32)
    scores = jnp.where(allowed[None], raw_scores, lowest)
    row_max = jnp.max(scores, axis=-1, keepdims=True)
    expo_rows = jnp.exp(scores - row_max)
    row_total = jnp.sum(expo_rows, axis=-1, keepdims=True)
    probs = expo_rows / row_total
    probs_low = probs.astype(BF16)
    heads_out = (
        jnp.einsum("hqk,kd->qhd", probs_low, values_all, preferred_element_type=F32)
        .reshape(BLK, HEADS * HD)
        .astype(BF16)
    )
    attn_proj = dot(heads_out, out_w)
    branch_one, branch_unit, branch_inv = rms_forward(attn_proj, attn_out_g)
    middle = inputs + branch_one
    norm_two, unit_two, inv_two = rms_forward(middle, ffn_in_g)
    normed_two = norm_two.astype(BF16)
    normed_two_a = dot(normed_two, perm_a).astype(BF16)
    normed_two_b = dot(normed_two, perm_b).astype(BF16)
    gate_pre = dot(normed_two_a, gate_w)
    up_pre = dot(normed_two_b, up_w)
    hidden = geglu(gate_pre, up_pre).astype(BF16)
    ffn_proj = dot(hidden, down_w)
    branch_two, ffn_unit, ffn_inv = rms_forward(ffn_proj, ffn_out_g)
    layer_out = (middle + branch_two).astype(BF16)

    out_grad = cotangent.astype(F32)
    ffn_grad, ffn_out_gg = rms_backward(out_grad, ffn_unit, ffn_inv, ffn_out_g)
    ffn_grad_low = ffn_grad.astype(BF16)
    down_sum = reduce_natural(dot(hidden, ffn_grad_low, 0, 0), order_c, me)
    hidden_grad = dot(ffn_grad_low, down_w, 1, 1)
    activated, pullback = jax.vjp(geglu, gate_pre, up_pre)
    gate_grad, up_grad = pullback(hidden_grad)
    gate_low = gate_grad.astype(BF16)
    up_low = up_grad.astype(BF16)
    half = D // 2

    def weight_rows(permuted, incoming):
        return (
            dot(permuted[:, :half], incoming, 0, 0),
            dot(permuted[:, half:], incoming, 0, 0).astype(BF16),
        )

    gate_sum = reduce_rows(*weight_rows(normed_two_a, gate_low), order_a)
    up_sum = reduce_rows(*weight_rows(normed_two_b, up_low), order_b)

    def natural_columns(permuted, perm):
        high = permuted.astype(BF16)
        low = (permuted - high.astype(F32)).astype(BF16)
        return dot(high, perm, 1, 1) + dot(low, perm, 1, 1)

    normed_two_grad = natural_columns(dot(gate_low, gate_w, 1, 1), perm_a) + natural_columns(
        dot(up_low, up_w, 1, 1), perm_b
    )
    middle_extra, ffn_in_gg = rms_backward(normed_two_grad, unit_two, inv_two, ffn_in_g)
    middle_grad = out_grad + middle_extra
    attn_grad, attn_out_gg = rms_backward(middle_grad, branch_unit, branch_inv, attn_out_g)
    attn_grad_low = attn_grad.astype(BF16)
    out_sum = reduce_natural(dot(heads_out, attn_grad_low, 0, 0), order_c, me)
    heads_grad = dot(attn_grad_low, out_w, 1, 1).astype(BF16).reshape(BLK, HEADS, HD)
    prob_grad = jnp.einsum("qhd,kd->hqk", heads_grad, values_all, preferred_element_type=F32)
    delta_rows = jnp.sum(probs * prob_grad, axis=-1, keepdims=True)
    score_grad = (probs * (prob_grad - delta_rows)).astype(BF16)
    query_grad = jnp.einsum("hqk,kd->qhd", score_grad, keys_all, preferred_element_type=F32)
    keys_grad = jnp.einsum("hqk,qhd->kd", score_grad, query_low, preferred_element_type=F32)
    values_grad = jnp.einsum("hqk,qhd->kd", probs_low, heads_grad, preferred_element_type=F32)
    own_start = BACK * BLK
    both_grad = jnp.concatenate([keys_grad, values_grad], axis=1)
    both_total = both_grad[own_start:]
    both_low = both_grad[:own_start].astype(BF16)
    for back_step in range(1, BACK + 1):
        lower = (BACK - back_step) * BLK
        both_total = both_total + passed_along(
            both_low[lower : lower + BLK], "seq", -back_step
        ).astype(F32)
    key_total, value_total = both_total[:, :HD], both_total[:, HD:]
    key_rot = rotate(key_total, cos_rows, -sin_rows)
    key_raw_grad, key_gg = rms_backward(key_rot, key_unit, key_inv, key_g)
    kv_low_grad = jnp.concatenate([key_raw_grad, value_total], axis=1).astype(BF16)
    query_rot = rotate(query_grad * query_scale, cos_rows[:, None, :], -sin_rows[:, None, :])
    query_raw_grad, query_gg = rms_backward(query_rot, query_unit, query_inv, query_g)
    query_low_grad = query_raw_grad.reshape(BLK, HEADS * HD).astype(BF16)
    normed_one_grad = natural_columns(dot(query_low_grad, query_w, 1, 1), perm_a) + natural_columns(
        dot(kv_low_grad, kv_w, 1, 1), perm_b
    )
    input_extra, attn_in_gg = rms_backward(normed_one_grad, unit_one, inv_one, attn_in_g)
    input_grad = middle_grad + input_extra
    gains_grad = jnp.concatenate(
        [attn_in_gg, attn_out_gg, ffn_in_gg, ffn_out_gg, query_gg, key_gg], axis=0
    )
    gain_rows = lax.dot_general(
        gain_pick.astype(F32),
        jnp.pad(gains_grad.reshape(count, gain_each), ((0, 0), (0, 128 - gain_each))),
        (((0,), (0,)), ((), ())),
        precision=lax.Precision.HIGHEST,
        preferred_element_type=F32,
    )
    query_sum = reduce_rows(*weight_rows(normed_one_a, query_low_grad), order_a)
    kv_keep, kv_send = weight_rows(normed_one_b, kv_low_grad)
    kvg_sum = reduce_rows(
        jnp.concatenate([kv_keep, gain_rows[:half]], axis=1),
        jnp.concatenate([kv_send, gain_rows[half:].astype(BF16)], axis=1),
        order_b,
    )
    return (
        layer_out,
        input_grad,
        query_sum.reshape(-1),
        kvg_sum[:, :HD].reshape(-1),
        kvg_sum[:, HD : 2 * HD].reshape(-1),
        out_sum.reshape(-1),
        gate_sum.reshape(-1),
        up_sum.reshape(-1),
        down_sum.reshape(-1),
        kvg_sum[0, 2 * HD : 2 * HD + gain_each],
    )


def solution(mesh):
    rows = P(AXES, None)
    flat = P(AXES)
    return jax.shard_map(
        local,
        mesh=mesh,
        in_specs=(rows, flat, rows) + (flat,) * 8,
        out_specs=(rows, rows) + (flat,) * 8,
        check_vma=False,
    )
```

```python
import functools
import numpy as np
import jax
import jax.numpy as jnp
from jax import lax
from jax.experimental import pallas as pl
from jax.experimental.pallas import tpu as pltpu
from jax.sharding import PartitionSpec as P

D = 640
HEADS = 4
HD = 256
FF = 2048
WIN = 512
BLK = 256
BACK = 2
AXES = ("dp", "seq")
F32 = jnp.float32
BF16 = jnp.bfloat16
QW = HEADS * HD
SPAN = (BACK + 1) * BLK

PARTS = 32
MAIN = 16
DEPTH = PARTS * MAIN
HALF = DEPTH // 2
LANES = 128
ATTN_A = QW + QW // 4 + LANES
ATTN_B = 2 * HD + HD // 2 + 2 * D
FFN_A = FF + FF // 4 + 2 * D
Z_BITS = (1, 2)
LOW, CORE, HIGH = 0, 3, 4
ORDER_A = (LOW, HIGH, CORE)
ORDER_B = (HIGH, LOW, CORE)

epsilon = 1e-06
lowest = -1e30


def slot_shards(order):
    shards = np.arange(4, dtype=np.int32) << Z_BITS[0]
    for bit in order:
        shards = np.concatenate([shards, shards ^ (1 << bit)])
    return shards


SLOTS_A = slot_shards(ORDER_A)
SLOTS_B = slot_shards(ORDER_B)


def extra_bits():
    return (lax.axis_size("dp") * lax.axis_size("seq")).bit_length() - PARTS.bit_length()


def exchanged(value, mask):
    count = lax.axis_size("dp") * lax.axis_size("seq")
    return lax.ppermute(value, AXES, [(i, i ^ mask) for i in range(count)])


def exchanged_part(value, mask):
    return exchanged(value, mask << extra_bits())


def passed_along(value, axis, steps):
    count = lax.axis_size(axis)
    first, last = (max(0, -steps), min(count, count - steps))
    return lax.ppermute(value, axis, [(source, source + steps) for source in range(first, last)])


def dot(left, right, left_dim=1, right_dim=0):
    return lax.dot_general(
        left, right, (((left_dim,), (right_dim,)), ((), ())), preferred_element_type=F32
    )


def unit_of(values):
    inverse = lax.rsqrt(jnp.mean(values * values, axis=-1, keepdims=True) + epsilon)
    return values * inverse, inverse


def rms_values_grad(incoming, unit_rows, inverse, gain_row):
    scaled = incoming * gain_row
    return inverse * (scaled - unit_rows * jnp.mean(scaled * unit_rows, axis=-1, keepdims=True))


def rotate(values, cos_rows, sin_rows):
    middle_at = values.shape[-1] // 2
    first_half = values[..., :middle_at]
    second_half = values[..., middle_at:]
    return jnp.concatenate(
        [
            first_half * cos_rows - second_half * sin_rows,
            second_half * cos_rows + first_half * sin_rows,
        ],
        axis=-1,
    )


def row_sum(values):
    return jnp.sum(values, axis=0, keepdims=True)


def column(index):
    return pl.ds(index * LANES, LANES)


def pack_kernel(
    query, key, value, out, gate, up, down, gains, attn, ffn, wide, quarter
):
    def load(source):
        rows = source.shape[0]
        wide[:rows, :] = source[...].astype(F32)

    def put_main(target, at, blocks, block):
        target[:, pl.ds(at, LANES)] = wide[pl.ds(block, MAIN, stride=blocks), :].astype(BF16)

    def put_tail(row, at, blocks, block):
        quarter[4 * row : 4 * row + 4, pl.ds(at, LANES)] = wide[
            pl.ds(MAIN * blocks + block, 4, stride=blocks), :
        ]

    def put_matrix(source, target, at):
        load(source)
        blocks = source.shape[0] // 20
        for block in range(blocks):
            put_main(target, at + block * LANES, blocks, block)
            each = blocks // 4
            put_tail(block // each, block % each * LANES, blocks, block)
        width = blocks * LANES // 4
        target[:, pl.ds(at + blocks * LANES, width)] = quarter[:, :width].astype(BF16)

    def put_groups(target, at, groups):
        blocks = D // LANES
        for place, group in enumerate(groups):
            for block in range(blocks):
                target[:, pl.ds(at + place * D + block * LANES, LANES)] = wide[
                    pl.ds(group * MAIN * blocks + block, MAIN, stride=blocks), :
                ].astype(BF16)

    put_matrix(query, attn, 0)
    attn[:, pl.ds(QW + QW // 4, LANES)] = gains[...]
    for place, source in enumerate((key, value)):
        load(source)
        for block in range(2):
            put_main(attn, ATTN_A + place * HD + block * LANES, 2, block)
            put_tail(2 * place + block, 0, 2, block)
    attn[:, pl.ds(ATTN_A + 2 * HD, LANES)] = quarter[:, :LANES].astype(BF16)
    load(out)
    put_groups(attn, ATTN_A + 2 * HD + HD // 2, (0, 1))
    put_matrix(gate, ffn, 0)
    put_matrix(up, ffn, FFN_A)
    load(down)
    put_groups(ffn, FF + FF // 4, (0, 1))
    put_groups(ffn, FFN_A + FF + FF // 4, (2, 3))


def unpack_matrix(source, at, target):
    blocks = target.shape[0] // 20
    each = blocks // 4
    tail_at = at + blocks * LANES
    for block in range(blocks):
        target[pl.ds(block, MAIN, stride=blocks), :] = source[:, pl.ds(at + block * LANES, LANES)]
        row = block // each * 4
        target[pl.ds(MAIN * blocks + block, 4, stride=blocks), :] = source[
            row : row + 4, pl.ds(tail_at + block % each * LANES, LANES)
        ]


def unpack_groups(source, at, target, groups):
    blocks = D // LANES
    for place, group in enumerate(groups):
        for block in range(blocks):
            target[pl.ds(group * MAIN * blocks + block, MAIN, stride=blocks), :] = source[
                :, pl.ds(at + place * D + block * LANES, LANES)
            ]


def unpack_ffn_kernel(part_a, part_b, gate, up, down):
    unpack_matrix(part_a, 0, gate)
    unpack_matrix(part_b, 0, up)
    unpack_groups(part_a, FF + FF // 4, down, (0, 1))
    unpack_groups(part_b, FF + FF // 4, down, (2, 3))


def unpack_attn_kernel(query_part, out_part, kv_part, query, key, value, out):
    unpack_matrix(query_part, 0, query)
    unpack_groups(out_part, 0, out, (0, 1))
    for place, target in enumerate((key, value)):
        for block in range(2):
            target[pl.ds(block, MAIN, stride=2), :] = kv_part[
                :, pl.ds(place * HD + block * LANES, LANES)
            ]
            row = 4 * (2 * place + block)
            target[pl.ds(2 * MAIN + block, 4, stride=2), :] = kv_part[
                row : row + 4, pl.ds(2 * HD, LANES)
            ]


def quarter_rows(tail_rows, quarter):
    lane = lax.broadcasted_iota(jnp.int32, tail_rows.shape, 1)
    return jnp.where(lane // 4 % 4 == quarter, tail_rows, jnp.zeros_like(tail_rows))


def packed_product(rows, mine, other, main_at, tail_at, quarter, width):
    tail = quarter_rows(rows[:, DEPTH:], quarter)
    main_at, tail_at = pl.ds(main_at, width), pl.ds(tail_at, width)
    return (
        dot(rows[:, :HALF], mine[:, main_at])
        + dot(rows[:, HALF:DEPTH], other[:, main_at])
        + dot(tail[:, :HALF], mine[:, tail_at])
        + dot(tail[:, HALF:], other[:, tail_at])
    )


def packed_back(incoming, mine, other, main_at, tail_at, quarter):
    width = incoming.shape[1]
    main_at, tail_at = pl.ds(main_at, width), pl.ds(tail_at, width)
    tail = jnp.concatenate(
        [dot(incoming, mine[:, tail_at], 1, 1), dot(incoming, other[:, tail_at], 1, 1)], axis=1
    )
    return jnp.concatenate(
        [
            dot(incoming, mine[:, main_at], 1, 1),
            dot(incoming, other[:, main_at], 1, 1),
            quarter_rows(tail, quarter),
        ],
        axis=1,
    )


def packed_grad(rows, incoming, keep, send, main_at):
    grad = dot(rows, incoming, 0, 0).astype(BF16)
    main_at = pl.ds(main_at, incoming.shape[1])
    keep[:, main_at] = grad[:HALF]
    send[:, main_at] = grad[HALF:]


def natural_columns(permuted, permutation):
    high = permuted.astype(BF16)
    low = (permuted - high.astype(F32)).astype(BF16)
    return dot(high, permutation, 1, 1) + dot(low, permutation, 1, 1)


def place_groups(target, me, slots, mine, other, at, groups, count):
    for slot in range(PARTS):
        source = mine if slot < PARTS // 2 else other
        row = slot % (PARTS // 2) * MAIN
        first = (me ^ int(slots[slot])) * (count * MAIN)
        for place, group in enumerate(groups):
            rows = pl.ds(pl.multiple_of(first + group * MAIN, MAIN), MAIN)
            target[rows, :] = source[row : row + MAIN, pl.ds(at + place * D, D)]


def take_groups(whole, me, slots, keep, send, at, groups, count):
    for slot in range(PARTS):
        target = keep if slot < PARTS // 2 else send
        row = slot % (PARTS // 2) * MAIN
        first = (me ^ int(slots[slot])) * (count * MAIN)
        for place, group in enumerate(groups):
            rows = pl.ds(pl.multiple_of(first + group * MAIN, MAIN), MAIN)
            target[row : row + MAIN, pl.ds(at + place * D, D)] = whole[rows, :]


def qkv_kernel(
    tokens, gain_d, gain_h, perm_a, perm_b, mine_a, other_a, mine_b, other_b, cos, sin,
    query_low, kv_low, query_raw, key_raw, rows_a, rows_b,
):
    unit, _ = unit_of(tokens[...].astype(F32))
    normed = (unit * gain_d[0:1, :]).astype(BF16)
    rows_a[...] = dot(normed, perm_a[...]).astype(BF16)
    rows_b[...] = dot(normed, perm_b[...]).astype(BF16)
    cos_rows, sin_rows = cos[...], sin[...]
    for head in range(HEADS):
        raw = packed_product(rows_a, mine_a, other_a, head * HD, QW, head, HD)
        at = pl.ds(head * HD, HD)
        query_raw[:, at] = raw
        normed_raw = unit_of(raw)[0] * gain_h[0:1, :]
        query_low[:, at] = (rotate(normed_raw, cos_rows, sin_rows) * HD**-0.5).astype(BF16)
    kv = [
        packed_product(rows_b, mine_b, other_b, c * LANES, 2 * HD, c, LANES) for c in range(4)
    ]
    raw = jnp.concatenate(kv[:2], axis=1)
    key_raw[...] = raw
    kv_low[:, :HD] = rotate(unit_of(raw)[0] * gain_h[1:2, :], cos_rows, sin_rows).astype(BF16)
    kv_low[:, HD:] = jnp.concatenate(kv[2:], axis=1).astype(BF16)


def allowed_pairs(block_index, positions):
    query_index = block_index * BLK + lax.broadcasted_iota(jnp.int32, (BLK, SPAN), 0)
    key_index = (block_index - BACK) * BLK + lax.broadcasted_iota(jnp.int32, (BLK, SPAN), 1)
    return (
        (key_index <= query_index)
        & (key_index > query_index - WIN)
        & (key_index >= query_index - positions[...])
    )


def attend_kernel(
    where, tokens, positions, gain_d, perm_a, perm_b, mine_b, other_b, query_low, kv_all,
    heads_out, log_total, attn_proj, middle, rows_a, rows_b, out_w,
):
    place_groups(out_w, where[0], SLOTS_B, mine_b, other_b, 2 * HD + HD // 2, (0, 1), 2)
    allowed = allowed_pairs(where[1], positions)
    for head in range(HEADS):
        at = pl.ds(head * HD, HD)
        scores = dot(query_low[:, at], kv_all[:, :HD], 1, 1)
        scores = jnp.where(allowed, scores, lowest)
        row_max = jnp.max(scores, axis=-1, keepdims=True)
        expo = jnp.exp(scores - row_max)
        total = jnp.sum(expo, axis=-1, keepdims=True)
        log_total[:, column(head)] = jnp.broadcast_to(row_max + jnp.log(total), (BLK, LANES))
        probs = (expo * (1.0 / total)).astype(BF16)
        heads_out[:, at] = dot(probs, kv_all[:, HD:]).astype(BF16)
    proj = dot(heads_out[...], out_w[...])
    attn_proj[...] = proj
    mid = tokens[...].astype(F32) + unit_of(proj)[0] * gain_d[1:2, :]
    middle[...] = mid
    normed = (unit_of(mid)[0] * gain_d[2:3, :]).astype(BF16)
    rows_a[...] = dot(normed, perm_a[...]).astype(BF16)
    rows_b[...] = dot(normed, perm_b[...]).astype(BF16)


TILE = 256
TILES = FF // TILE
TANH_SCALE = float(np.sqrt(2.0 / np.pi))


def ffn_kernel(
    where, middle, cotangent, gain_d, perm_a, perm_b, rows_a, rows_b, mine_a, other_a, mine_b,
    other_b, layer_out, keep_a, send_a, keep_b, send_b, mid_grad, gain_grad,
    down_w, down_grad, gate_s, up_s, hidden_s, gate_g, up_g, back_a, back_b,
):
    me = where[0]
    down_at = FF + FF // 4
    place_groups(down_w, me, SLOTS_A, mine_a, other_a, down_at, (0, 1), 4)
    place_groups(down_w, me, SLOTS_B, mine_b, other_b, down_at, (2, 3), 4)

    def tile_places(tile):
        at = pl.multiple_of(tile * TILE, TILE)
        tail_at = pl.multiple_of(FF + tile % 2 * TILE, TILE)
        return at, tail_at, tile // 2

    @pl.loop(0, TILES)
    def forward(tile):
        at, tail_at, quarter = tile_places(tile)
        gate = packed_product(rows_a, mine_a, other_a, at, tail_at, quarter, TILE)
        up = packed_product(rows_b, mine_b, other_b, at, tail_at, quarter, TILE)
        gate_s[:, pl.ds(at, TILE)] = gate
        up_s[:, pl.ds(at, TILE)] = up
        tanh = jnp.tanh(TANH_SCALE * (gate + 0.044715 * gate * gate * gate))
        hidden_s[:, pl.ds(at, TILE)] = (0.5 * gate * (1.0 + tanh) * up).astype(BF16)

    proj = dot(hidden_s[...], down_w[...])
    mid = middle[...]
    unit, inverse = unit_of(proj)
    layer_out[...] = (mid + unit * gain_d[3:4, :]).astype(BF16)
    out_grad = cotangent[...].astype(F32)
    gain_grad[0:1, :] = row_sum(out_grad * unit)
    proj_grad = rms_values_grad(out_grad, unit, inverse, gain_d[3:4, :]).astype(BF16)
    back_a[...] = jnp.zeros_like(back_a)
    back_b[...] = jnp.zeros_like(back_b)

    @pl.loop(0, TILES)
    def backward(tile):
        at, tail_at, quarter = tile_places(tile)
        cols = pl.ds(at, TILE)
        hidden_grad = dot(proj_grad, down_w[cols, :], 1, 1)
        down_grad[cols, :] = dot(hidden_s[:, cols], proj_grad, 0, 0).astype(BF16)
        gate, up = gate_s[:, cols], up_s[:, cols]
        square = gate * gate
        tanh = jnp.tanh(TANH_SCALE * (gate + 0.044715 * gate * square))
        slope = 0.5 * (1.0 + tanh) + 0.5 * gate * (1.0 - tanh * tanh) * TANH_SCALE * (
            1.0 + 3.0 * 0.044715 * square
        )
        gate_grad = (hidden_grad * up * slope).astype(BF16)
        up_grad = (hidden_grad * (0.5 * gate * (1.0 + tanh))).astype(BF16)
        gate_g[:, cols] = gate_grad
        up_g[:, cols] = up_grad
        back_a[...] += packed_back(gate_grad, mine_a, other_a, at, tail_at, quarter)
        back_b[...] += packed_back(up_grad, mine_b, other_b, at, tail_at, quarter)
        packed_grad(rows_a[:, :DEPTH], gate_grad, keep_a, send_a, at)
        packed_grad(rows_b[:, :DEPTH], up_grad, keep_b, send_b, at)

    for rows, grad_s, keep, send in ((rows_a, gate_g, keep_a, send_a), (rows_b, up_g, keep_b, send_b)):

        @pl.loop(0, 2)
        def tails(half):
            total = jnp.zeros((DEPTH, TILE), F32)
            for quarter in range(4):
                at = pl.multiple_of(quarter * (FF // 4) + half * TILE, TILE)
                total += dot(quarter_rows(rows[:, DEPTH:], quarter), grad_s[:, pl.ds(at, TILE)], 0, 0)
            at = pl.ds(pl.multiple_of(FF + half * TILE, TILE), TILE)
            keep[:, at] = total[:HALF].astype(BF16)
            send[:, at] = total[HALF:].astype(BF16)

    take_groups(down_grad, me, SLOTS_A, keep_a, send_a, down_at, (0, 1), 4)
    take_groups(down_grad, me, SLOTS_B, keep_b, send_b, down_at, (2, 3), 4)
    normed_grad = natural_columns(back_a[...], perm_a[...]) + natural_columns(
        back_b[...], perm_b[...]
    )
    unit, inverse = unit_of(mid)
    gain_grad[1:2, :] = row_sum(normed_grad * unit)
    mid_grad[...] = out_grad + rms_values_grad(normed_grad, unit, inverse, gain_d[2:3, :])


def attend_back_kernel(
    where, mid_grad, attn_proj, positions, gain_d, gain_h, out_w, heads_out, query_low, kv_all,
    log_total, query_raw, cos, sin, rows_a, mine_a, other_a,
    kv_earlier, kv_own, query_keep, query_send, out_keep, out_send, back_a, gain_grad_d,
    gain_grad_h, out_grad_s, kv_grad, query_grad_s,
):
    incoming = mid_grad[...]
    unit, inverse = unit_of(attn_proj[...])
    gain_grad_d[0:1, :] = row_sum(incoming * unit)
    proj_grad = rms_values_grad(incoming, unit, inverse, gain_d[1:2, :]).astype(BF16)
    for head in range(HEADS):
        at = pl.ds(head * HD, HD)
        out_grad_s[at, :] = dot(heads_out[:, at], proj_grad, 0, 0).astype(BF16)
    take_groups(out_grad_s, where[0], SLOTS_B, out_keep, out_send, 0, (0, 1), 2)
    allowed = allowed_pairs(where[1], positions)
    cos_rows, sin_rows = cos[...], sin[...]
    total_a = jnp.zeros((BLK, 2 * DEPTH), F32)
    gain_total = jnp.zeros((1, HD), F32)
    keys_grad = jnp.zeros((SPAN, HD), F32)
    values_grad = jnp.zeros((SPAN, HD), F32)
    for head in range(HEADS):
        at = pl.ds(head * HD, HD)
        heads_grad = dot(proj_grad, out_w[at, :], 1, 1).astype(BF16)
        scores = dot(query_low[:, at], kv_all[:, :HD], 1, 1)
        log_rows = log_total[:, pl.ds(head * LANES, 1)]
        probs = jnp.where(allowed, jnp.exp(jnp.where(allowed, scores - log_rows, 0.0)), 0.0)
        prob_grad = dot(heads_grad, kv_all[:, HD:], 1, 1)
        delta = jnp.sum(probs * prob_grad, axis=-1, keepdims=True)
        score_grad = (probs * (prob_grad - delta)).astype(BF16)
        keys_grad += dot(score_grad, query_low[:, at], 0, 0)
        values_grad += dot(probs.astype(BF16), heads_grad, 0, 0)
        query_grad = dot(score_grad, kv_all[:, :HD]) * HD**-0.5
        query_rot = rotate(query_grad, cos_rows, -sin_rows)
        unit, inverse = unit_of(query_raw[:, at])
        gain_total += row_sum(query_rot * unit)
        raw_grad = rms_values_grad(query_rot, unit, inverse, gain_h[0:1, :]).astype(BF16)
        query_grad_s[:, at] = raw_grad
        total_a += packed_back(raw_grad, mine_a, other_a, head * HD, QW, head)
        packed_grad(rows_a[:, :DEPTH], raw_grad, query_keep, query_send, head * HD)
    gain_grad_h[0:1, :] = gain_total
    kv_grad[:, :HD] = keys_grad
    kv_grad[:, HD:] = values_grad
    kv_earlier[...] = kv_grad[: BACK * BLK, :].astype(BF16)
    kv_own[...] = kv_grad[BACK * BLK :, :]
    back_a[...] = total_a
    tail = jnp.zeros((DEPTH, HD), F32)
    for head in range(HEADS):
        tail += dot(
            quarter_rows(rows_a[:, DEPTH:], head), query_grad_s[:, pl.ds(head * HD, HD)], 0, 0
        )
    query_keep[:, pl.ds(QW, HD)] = tail[:HALF].astype(BF16)
    query_send[:, pl.ds(QW, HD)] = tail[HALF:].astype(BF16)


def input_kernel(
    tokens, mid_grad, gain_d, gain_h, perm_a, perm_b, rows_b, mine_b, other_b, kv_own, came_one,
    came_two, key_raw, cos, sin, back_a, input_grad, kv_keep, kv_send, gain_grad_d, gain_grad_h,
):
    total = kv_own[...] + came_one[...].astype(F32) + came_two[...].astype(F32)
    key_rot = rotate(total[:, :HD], cos[...], -sin[...])
    unit, inverse = unit_of(key_raw[...])
    gain_grad_h[0:1, :] = row_sum(key_rot * unit)
    key_grad = rms_values_grad(key_rot, unit, inverse, gain_h[1:2, :]).astype(BF16)
    raw_grad = jnp.concatenate([key_grad, total[:, HD:].astype(BF16)], axis=1)
    back_b = jnp.zeros((BLK, 2 * DEPTH), F32)
    tail = jnp.zeros((DEPTH, LANES), F32)
    for c in range(4):
        part = raw_grad[:, c * LANES : (c + 1) * LANES]
        back_b += packed_back(part, mine_b, other_b, c * LANES, 2 * HD, c)
        tail += dot(quarter_rows(rows_b[:, DEPTH:], c), part, 0, 0)
    packed_grad(rows_b[:, :DEPTH], raw_grad, kv_keep, kv_send, 0)
    kv_keep[:, pl.ds(2 * HD, LANES)] = tail[:HALF].astype(BF16)
    kv_send[:, pl.ds(2 * HD, LANES)] = tail[HALF:].astype(BF16)
    normed_grad = natural_columns(back_a[...], perm_a[...]) + natural_columns(
        back_b, perm_b[...]
    )
    unit, inverse = unit_of(tokens[...].astype(F32))
    gain_grad_d[0:1, :] = row_sum(normed_grad * unit)
    input_grad[...] = mid_grad[...] + rms_values_grad(
        normed_grad, unit, inverse, gain_d[0:1, :]
    )


VMEM_LIMIT = 56 * 1024 * 1024


def call(kernel, outs, args, scratch=(), scalars=0, flops=0):
    vmem = pl.BlockSpec(memory_space=pltpu.VMEM)
    shapes = [jax.ShapeDtypeStruct(shape, kind) for shape, kind in outs]
    return pl.pallas_call(
        kernel,
        out_shape=shapes,
        in_specs=[pl.BlockSpec(memory_space=pltpu.SMEM)] * scalars + [vmem] * (len(args) - scalars),
        out_specs=[vmem] * len(outs),
        scratch_shapes=[pltpu.VMEM(shape, kind) for shape, kind in scratch],
        compiler_params=pltpu.CompilerParams(vmem_limit_bytes=VMEM_LIMIT),
        cost_estimate=pl.CostEstimate(flops=int(flops), bytes_accessed=0, transcendentals=0),
    )(*args)


def together(*values):
    return lax.optimization_barrier(values)


def shared_part(flat):
    for bit in range(extra_bits()):
        other = exchanged(flat, 1 << bit)
        mine_first = (lax.axis_index(AXES) >> bit) & 1 == 0
        flat = jnp.where(
            mine_first, jnp.concatenate([flat, other]), jnp.concatenate([other, flat])
        )
    return flat


def own_part(flat):
    for bit in reversed(range(extra_bits())):
        halves = jnp.split(flat, 2)
        mine_first = (lax.axis_index(AXES) >> bit) & 1 == 0
        keep = jnp.where(mine_first, halves[0], halves[1])
        send = jnp.where(mine_first, halves[1], halves[0]).astype(BF16)
        flat = keep + exchanged(send, 1 << bit).astype(F32)
    return flat


def pieces_z(piece):
    return [piece] + [exchanged_part(piece, k << Z_BITS[0]) for k in range(1, 4)]


def gather_step(piece, bit):
    return jnp.concatenate([piece, exchanged_part(piece, 1 << bit)], axis=0)


def reduce_step(state, bit):
    keep, send = state
    total = keep.astype(F32) + exchanged_part(send, 1 << bit).astype(F32)
    half = total.shape[0] // 2
    return total[:half].astype(BF16), total[half:].astype(BF16)


def reduce_total(state, bit):
    keep, send = state
    return keep.astype(F32) + exchanged_part(send, 1 << bit).astype(F32)


def reduce_z(total, steps, result=None):
    result = total[:MAIN] if result is None else result
    for k in steps:
        piece = total[k * MAIN : (k + 1) * MAIN].astype(BF16)
        result = result + exchanged_part(piece, k << Z_BITS[0]).astype(F32)
    return result


def permutation(slots, me):
    rows = D // PARTS
    first = (jnp.asarray(slots) ^ me)[:, None] * rows
    inner = jnp.arange(MAIN, dtype=jnp.int32)[None, :]
    target = jnp.concatenate([(first + inner).reshape(-1), (first + MAIN + inner % 4).reshape(-1)])
    return (jnp.arange(D, dtype=jnp.int32)[:, None] == target[None, :]).astype(BF16)


def local(
    tokens, positions, cotangent, w_query, w_key, w_value, w_out, w_gate, w_up, w_down, gains
):
    me = lax.axis_index(AXES) >> extra_bits()
    block_index = lax.axis_index("seq")
    where = jnp.stack([me, block_index]).astype(jnp.int32)
    parts = [
        shared_part(w).reshape(-1, LANES)
        for w in (w_query, w_key, w_value, w_out, w_gate, w_up, w_down)
    ]
    gain_part = shared_part(gains)
    gain_each = gain_part.shape[0]
    gain_block = jnp.pad(gain_part[None, :], ((0, MAIN - 1), (0, LANES - gain_each)))
    attn, ffn = call(
        pack_kernel,
        [((MAIN, ATTN_A + ATTN_B), BF16), ((MAIN, 2 * FFN_A), BF16)],
        parts + [gain_block],
        [((320, LANES), F32), ((MAIN, FF // 4), F32)],
    )
    attn_z, ffn = together(jnp.concatenate(pieces_z(attn), axis=0), ffn)
    ffn_pieces = [ffn, exchanged_part(ffn, 1 << Z_BITS[0])]
    attn_a, attn_b, ffn_pieces = together(
        gather_step(attn_z[:, :ATTN_A], ORDER_A[0]),
        gather_step(attn_z[:, ATTN_A:], ORDER_B[0]),
        ffn_pieces,
    )
    ffn_pieces.append(exchanged_part(ffn_pieces[0], 2 << Z_BITS[0]))
    attn_a, attn_b, ffn_pieces = together(
        gather_step(attn_a, ORDER_A[1]), gather_step(attn_b, ORDER_B[1]), ffn_pieces
    )
    other_a = exchanged_part(attn_a, 1 << CORE)
    other_b = exchanged_part(attn_b, 1 << CORE)
    ffn_pieces.append(exchanged_part(ffn_pieces[0], 3 << Z_BITS[0]))

    perm_a = permutation(SLOTS_A, me)
    perm_b = permutation(SLOTS_B, me)
    row = jnp.arange(DEPTH, dtype=jnp.int32)

    def picked(slots):
        owner = jnp.repeat(jnp.asarray(slots), MAIN) ^ me
        same = owner[None, :] == jnp.arange(PARTS, dtype=jnp.int32)[:, None]
        return same & (row % MAIN == 0)[None, :]

    gain_pick = picked(SLOTS_A).astype(BF16)
    gain_at = QW + QW // 4
    gain_all = (
        dot(gain_pick[:, :HALF], attn_a[:, gain_at:])
        + dot(gain_pick[:, HALF:], other_a[:, gain_at:])
    )[:, :gain_each].reshape(-1)
    gain_d = gain_all[: 4 * D].reshape(4, D)
    gain_h = gain_all[4 * D :].reshape(2, HD)

    freq_table = 10000.0 ** (-2.0 * jnp.arange(HD // 2, dtype=F32) / HD)
    angle_rows = positions.astype(F32)[:, None] * freq_table[None, :]
    cos_rows = jnp.cos(angle_rows)
    sin_rows = jnp.sin(angle_rows)
    places = positions[:, None]

    rows = (BLK, 2 * DEPTH)
    query_low, kv_low, query_raw, key_raw, one_a, one_b = call(
        qkv_kernel,
        [
            ((BLK, QW), BF16),
            ((BLK, 2 * HD), BF16),
            ((BLK, QW), F32),
            ((BLK, HD), F32),
            (rows, BF16),
            (rows, BF16),
        ],
        [tokens, gain_d, gain_h, perm_a, perm_b, attn_a, other_a, attn_b, other_b]
        + [cos_rows, sin_rows],
        flops=30e9,
    )
    query_low, kv_low, ffn_z = together(query_low, kv_low, jnp.concatenate(ffn_pieces, axis=0))
    earlier = [passed_along(kv_low, "seq", back_step) for back_step in range(BACK, 0, -1)]
    kv_all, ffn_a, ffn_b = together(
        jnp.concatenate(earlier + [kv_low], axis=0),
        gather_step(ffn_z[:, :FFN_A], ORDER_A[0]),
        gather_step(ffn_z[:, FFN_A:], ORDER_B[0]),
    )
    heads_out, log_total, attn_proj, middle, two_a, two_b, out_w = call(
        attend_kernel,
        [
            ((BLK, QW), BF16),
            ((BLK, HEADS * LANES), F32),
            ((BLK, D), F32),
            ((BLK, D), F32),
            (rows, BF16),
            (rows, BF16),
            ((QW, D), BF16),
        ],
        [where, tokens, places, gain_d, perm_a, perm_b, attn_b, other_b, query_low, kv_all],
        scalars=1,
        flops=30e9,
    )
    middle, two_a, two_b, ffn_a, ffn_b = together(
        middle,
        two_a,
        two_b,
        gather_step(ffn_a, ORDER_A[1]),
        gather_step(ffn_b, ORDER_B[1]),
    )
    ffn_other_a = exchanged_part(ffn_a, 1 << CORE)
    ffn_other_b = exchanged_part(ffn_b, 1 << CORE)
    packed = ((HALF, FFN_A), BF16)
    layer_out, keep_a, send_a, keep_b, send_b, mid_grad, ffn_gg = call(
        ffn_kernel,
        [((BLK, D), BF16), packed, packed, packed, packed, ((BLK, D), F32), ((2, D), F32)],
        [where, middle, cotangent, gain_d, perm_a, perm_b, two_a, two_b]
        + [ffn_a, ffn_other_a, ffn_b, ffn_other_b],
        [
            ((FF, D), BF16),
            ((FF, D), BF16),
            ((BLK, FF), F32),
            ((BLK, FF), F32),
            ((BLK, FF), BF16),
            ((BLK, FF), BF16),
            ((BLK, FF), BF16),
            (rows, F32),
            (rows, F32),
        ],
        scalars=1,
        flops=1e6,
    )
    ffn_a = reduce_step((keep_a, send_a), CORE)
    ffn_b = reduce_step((keep_b, send_b), CORE)
    mid_grad_then, ffn_a, ffn_b = together(mid_grad, ffn_a, ffn_b)
    sixteen = ((HALF, QW + QW // 4), BF16)
    (
        kv_earlier,
        kv_own,
        query_keep,
        query_send,
        out_keep,
        out_send,
        back_a,
        attn_out_gg,
        query_gg,
    ) = call(
        attend_back_kernel,
        [
            ((BACK * BLK, 2 * HD), BF16),
            ((BLK, 2 * HD), F32),
            sixteen,
            sixteen,
            sixteen,
            sixteen,
            (rows, F32),
            ((1, D), F32),
            ((1, HD), F32),
        ],
        [where, mid_grad_then, attn_proj, places, gain_d, gain_h, out_w, heads_out, query_low]
        + [kv_all, log_total, query_raw, cos_rows, sin_rows, one_a, attn_a, other_a],
        [((QW, D), BF16), ((SPAN, 2 * HD), F32), ((BLK, QW), BF16)],
        scalars=1,
        flops=1e6,
    )
    ffn_a = reduce_step(ffn_a, ORDER_A[1])
    ffn_b = reduce_step(ffn_b, ORDER_B[1])
    kv_earlier, query_send, out_send, ffn_a, ffn_b = together(
        kv_earlier, query_send, out_send, ffn_a, ffn_b
    )
    came = [
        passed_along(kv_earlier[(BACK - step) * BLK : (BACK - step + 1) * BLK], "seq", -step)
        for step in range(1, BACK + 1)
    ]
    query_state = reduce_step((query_keep, query_send), CORE)
    out_state = reduce_step((out_keep, out_send), CORE)
    ffn_a = reduce_total(ffn_a, ORDER_A[0])
    ffn_b = reduce_total(ffn_b, ORDER_B[0])
    came, query_state, out_state, ffn_a, ffn_b = together(
        came, query_state, out_state, ffn_a, ffn_b
    )
    input_grad, kv_keep, kv_send, attn_in_gg, key_gg = call(
        input_kernel,
        [
            ((BLK, D), F32),
            ((HALF, 2 * HD + LANES), BF16),
            ((HALF, 2 * HD + LANES), BF16),
            ((1, D), F32),
            ((1, HD), F32),
        ],
        [tokens, mid_grad, gain_d, gain_h, perm_a, perm_b, one_b, attn_b, other_b]
        + [kv_own]
        + came
        + [key_raw, cos_rows, sin_rows, back_a],
        flops=1e6,
    )
    query_state = reduce_step(query_state, ORDER_A[1])
    out_state = reduce_step(out_state, ORDER_B[1])
    ffn = [reduce_z(total, (1, 2)) for total in (ffn_a, ffn_b)]
    kv_keep, kv_send, query_state, out_state, ffn = together(
        kv_keep, kv_send, query_state, out_state, ffn
    )
    gains_grad = jnp.concatenate(
        [attn_in_gg[0], attn_out_gg[0], ffn_gg[1], ffn_gg[0], query_gg[0], key_gg[0]]
    )
    gain_rows = lax.dot_general(
        picked(SLOTS_B).astype(F32),
        jnp.pad(gains_grad.reshape(PARTS, gain_each), ((0, 0), (0, LANES - gain_each))),
        (((0,), (0,)), ((), ())),
        precision=lax.Precision.HIGHEST,
        preferred_element_type=F32,
    ).astype(BF16)
    kv_state = (
        jnp.concatenate([kv_keep, gain_rows[:HALF]], axis=1),
        jnp.concatenate([kv_send, gain_rows[HALF:]], axis=1),
    )
    kv_state = reduce_step(reduce_step(kv_state, CORE), ORDER_B[1])
    query_total = reduce_total(query_state, ORDER_A[0])
    out_total = reduce_total(out_state, ORDER_B[0])
    ffn = [reduce_z(total, (3,), result) for total, result in zip((ffn_a, ffn_b), ffn)]
    kv_state, query_total, out_total, ffn = together(kv_state, query_total, out_total, ffn)
    kv_total = reduce_total(kv_state, ORDER_B[0])
    query_sum = reduce_z(query_total, (1, 2, 3))
    out_sum = reduce_z(out_total, (1, 2, 3))
    kv_total, query_sum, out_sum = together(kv_total, query_sum, out_sum)
    kv_sum = reduce_z(kv_total, (1, 2, 3))
    flat = [((160, LANES), F32), ((40, LANES), F32), ((320, LANES), F32)]
    grad_gate, grad_up, grad_down = call(unpack_ffn_kernel, [flat[2]] * 3, ffn)
    grad_query, grad_key, grad_value, grad_out = call(
        unpack_attn_kernel, [flat[0], flat[1], flat[1], flat[0]], [query_sum, out_sum, kv_sum]
    )
    return (
        layer_out,
        input_grad,
        *(
            own_part(grad.reshape(-1))
            for grad in (
                grad_query,
                grad_key,
                grad_value,
                grad_out,
                grad_gate,
                grad_up,
                grad_down,
                kv_sum[0, 2 * HD + LANES : 2 * HD + LANES + gain_each],
            )
        ),
    )


def solution(mesh):
    rows = P(AXES, None)
    flat = P(AXES)
    return jax.shard_map(
        local,
        mesh=mesh,
        in_specs=(rows, flat, rows) + (flat,) * 8,
        out_specs=(rows, rows) + (flat,) * 8,
        check_vma=False,
    )
```

```python
import functools
import numpy as np
import jax
import jax.numpy as jnp
from jax import lax
from jax.experimental import pallas as pl
from jax.experimental.pallas import tpu as pltpu
from jax.sharding import PartitionSpec as P

D = 640
HEADS = 4
HD = 256
FF = 2048
WIN = 512
BLK = 256
BACK = 2
AXES = ("dp", "seq")
F32 = jnp.float32
BF16 = jnp.bfloat16
QW = HEADS * HD
SPAN = (BACK + 1) * BLK

PARTS = 32
MAIN = 16
DEPTH = PARTS * MAIN
HALF = DEPTH // 2
LANES = 128
ATTN_A = QW + QW // 4 + LANES
ATTN_B = 2 * HD + HD // 2 + 2 * D
FFN_A = FF + FF // 4 + 2 * D
Z_BITS = (1, 2)
LOW, CORE, HIGH = 0, 3, 4
ORDER_A = (LOW, HIGH, CORE)
ORDER_B = (HIGH, LOW, CORE)

epsilon = 1e-06
lowest = -1e30


def slot_shards(order):
    shards = np.arange(4, dtype=np.int32) << Z_BITS[0]
    for bit in order:
        shards = np.concatenate([shards, shards ^ (1 << bit)])
    return shards


SLOTS_A = slot_shards(ORDER_A)
SLOTS_B = slot_shards(ORDER_B)


def extra_bits():
    return (lax.axis_size("dp") * lax.axis_size("seq")).bit_length() - PARTS.bit_length()


def exchanged(value, mask):
    count = lax.axis_size("dp") * lax.axis_size("seq")
    return lax.ppermute(value, AXES, [(i, i ^ mask) for i in range(count)])


def exchanged_part(value, mask):
    return exchanged(value, mask << extra_bits())


def passed_along(value, axis, steps):
    count = lax.axis_size(axis)
    first, last = (max(0, -steps), min(count, count - steps))
    return lax.ppermute(value, axis, [(source, source + steps) for source in range(first, last)])


def dot(left, right, left_dim=1, right_dim=0):
    return lax.dot_general(
        left, right, (((left_dim,), (right_dim,)), ((), ())), preferred_element_type=F32
    )


def unit_of(values):
    inverse = lax.rsqrt(jnp.mean(values * values, axis=-1, keepdims=True) + epsilon)
    return values * inverse, inverse


def rms_values_grad(incoming, unit_rows, inverse, gain_row):
    scaled = incoming * gain_row
    return inverse * (scaled - unit_rows * jnp.mean(scaled * unit_rows, axis=-1, keepdims=True))


def rotate(values, cos_rows, sin_rows):
    middle_at = values.shape[-1] // 2
    first_half = values[..., :middle_at]
    second_half = values[..., middle_at:]
    return jnp.concatenate(
        [
            first_half * cos_rows - second_half * sin_rows,
            second_half * cos_rows + first_half * sin_rows,
        ],
        axis=-1,
    )


def row_sum(values):
    return jnp.sum(values, axis=0, keepdims=True)


def column(index):
    return pl.ds(index * LANES, LANES)


def pack_kernel(
    query, key, value, out, gate, up, down, gains, attn, ffn, wide, quarter
):
    def load(source):
        rows = source.shape[0]
        wide[:rows, :] = source[...].astype(F32)

    def put_main(target, at, blocks, block):
        target[:, pl.ds(at, LANES)] = wide[pl.ds(block, MAIN, stride=blocks), :].astype(BF16)

    def put_tail(row, at, blocks, block):
        quarter[4 * row : 4 * row + 4, pl.ds(at, LANES)] = wide[
            pl.ds(MAIN * blocks + block, 4, stride=blocks), :
        ]

    def put_matrix(source, target, at):
        load(source)
        blocks = source.shape[0] // 20
        for block in range(blocks):
            put_main(target, at + block * LANES, blocks, block)
            each = blocks // 4
            put_tail(block // each, block % each * LANES, blocks, block)
        width = blocks * LANES // 4
        target[:, pl.ds(at + blocks * LANES, width)] = quarter[:, :width].astype(BF16)

    def put_groups(target, at, groups):
        blocks = D // LANES
        for place, group in enumerate(groups):
            for block in range(blocks):
                target[:, pl.ds(at + place * D + block * LANES, LANES)] = wide[
                    pl.ds(group * MAIN * blocks + block, MAIN, stride=blocks), :
                ].astype(BF16)

    put_matrix(query, attn, 0)
    attn[:, pl.ds(QW + QW // 4, LANES)] = gains[...]
    for place, source in enumerate((key, value)):
        load(source)
        for block in range(2):
            put_main(attn, ATTN_A + place * HD + block * LANES, 2, block)
            put_tail(2 * place + block, 0, 2, block)
    attn[:, pl.ds(ATTN_A + 2 * HD, LANES)] = quarter[:, :LANES].astype(BF16)
    load(out)
    put_groups(attn, ATTN_A + 2 * HD + HD // 2, (0, 1))
    put_matrix(gate, ffn, 0)
    put_matrix(up, ffn, FFN_A)
    load(down)
    put_groups(ffn, FF + FF // 4, (0, 1))
    put_groups(ffn, FFN_A + FF + FF // 4, (2, 3))


def unpack_matrix(source, at, target):
    blocks = target.shape[0] // 20
    each = blocks // 4
    tail_at = at + blocks * LANES
    for block in range(blocks):
        target[pl.ds(block, MAIN, stride=blocks), :] = source[:, pl.ds(at + block * LANES, LANES)]
        row = block // each * 4
        target[pl.ds(MAIN * blocks + block, 4, stride=blocks), :] = source[
            row : row + 4, pl.ds(tail_at + block % each * LANES, LANES)
        ]


def unpack_groups(source, at, target, groups):
    blocks = D // LANES
    for place, group in enumerate(groups):
        for block in range(blocks):
            target[pl.ds(group * MAIN * blocks + block, MAIN, stride=blocks), :] = source[
                :, pl.ds(at + place * D + block * LANES, LANES)
            ]


def unpack_ffn_kernel(part, gate, up, down):
    unpack_matrix(part, 0, gate)
    unpack_matrix(part, FFN_A, up)
    unpack_groups(part, FF + FF // 4, down, (0, 1))
    unpack_groups(part, FFN_A + FF + FF // 4, down, (2, 3))


def unpack_attn_kernel(part, query, key, value, out):
    unpack_matrix(part, 0, query)
    unpack_groups(part, QW + QW // 4, out, (0, 1))
    kv_at = QW + QW // 4 + 2 * D
    for place, target in enumerate((key, value)):
        for block in range(2):
            target[pl.ds(block, MAIN, stride=2), :] = part[
                :, pl.ds(kv_at + place * HD + block * LANES, LANES)
            ]
            row = 4 * (2 * place + block)
            target[pl.ds(2 * MAIN + block, 4, stride=2), :] = part[
                row : row + 4, pl.ds(kv_at + 2 * HD, LANES)
            ]


def quarter_mask(shape, dim, quarter):
    index = lax.broadcasted_iota(jnp.int32, shape, dim)
    return (index // 4 % 4 == quarter).astype(F32)


def quarter_rows(tail_rows, quarter):
    return tail_rows * quarter_mask((1, DEPTH), 1, quarter).astype(tail_rows.dtype)


def quarter_rows_t(tail_rows, quarter):
    return tail_rows * quarter_mask((DEPTH, 1), 0, quarter).astype(tail_rows.dtype)


def packed_product(rows, mine, other, main_at, tail_at, quarter, width):
    tail = quarter_rows(rows[:, DEPTH:], quarter)
    main_at, tail_at = pl.ds(main_at, width), pl.ds(tail_at, width)
    return (
        dot(rows[:, :HALF], mine[:, main_at])
        + dot(rows[:, HALF:DEPTH], other[:, main_at])
        + dot(tail[:, :HALF], mine[:, tail_at])
        + dot(tail[:, HALF:], other[:, tail_at])
    )


def packed_back(incoming, mine, other, main_at, tail_at, quarter):
    width = incoming.shape[1]
    main_at, tail_at = pl.ds(main_at, width), pl.ds(tail_at, width)
    tail = jnp.concatenate(
        [dot(incoming, mine[:, tail_at], 1, 1), dot(incoming, other[:, tail_at], 1, 1)], axis=1
    )
    return jnp.concatenate(
        [
            dot(incoming, mine[:, main_at], 1, 1),
            dot(incoming, other[:, main_at], 1, 1),
            quarter_rows(tail, quarter),
        ],
        axis=1,
    )


def packed_grad(rows_t, incoming, keep, send, main_at):
    grad = dot(rows_t, incoming).astype(BF16)
    main_at = pl.ds(main_at, incoming.shape[1])
    keep[:, main_at] = grad[:HALF]
    send[:, main_at] = grad[HALF:]


def natural_columns(permuted, permutation):
    high = permuted.astype(BF16)
    low = (permuted - high.astype(F32)).astype(BF16)
    return dot(high, permutation, 1, 1) + dot(low, permutation, 1, 1)


def place_groups(target, me, slots, mine, other, at, groups, count):
    for slot in range(PARTS):
        source = mine if slot < PARTS // 2 else other
        row = slot % (PARTS // 2) * MAIN
        first = (me ^ int(slots[slot])) * (count * MAIN)
        for place, group in enumerate(groups):
            rows = pl.ds(pl.multiple_of(first + group * MAIN, MAIN), MAIN)
            target[rows, :] = source[row : row + MAIN, pl.ds(at + place * D, D)]


def take_groups(whole, me, slots, keep, send, at, groups, count):
    for slot in range(PARTS):
        target = keep if slot < PARTS // 2 else send
        row = slot % (PARTS // 2) * MAIN
        first = (me ^ int(slots[slot])) * (count * MAIN)
        for place, group in enumerate(groups):
            rows = pl.ds(pl.multiple_of(first + group * MAIN, MAIN), MAIN)
            target[row : row + MAIN, pl.ds(at + place * D, D)] = whole[rows, :]


GAIN_SPANS = tuple((i * D, D) for i in range(4)) + ((4 * D, HD), (4 * D + HD, HD))
GAINS = 4 * D + 2 * HD
GAIN_EACH = GAINS // PARTS


def gain_fold():
    lane = np.arange(GAINS)[:, None] % GAIN_EACH == np.arange(LANES)[None, :]
    return jnp.asarray(lane, BF16)


def gain_holders(owners, span):
    entry = span[0] + lax.broadcasted_iota(jnp.int32, (PARTS, span[1]), 1)
    first = owners[...] * GAIN_EACH
    return (entry >= first) & (entry < first + GAIN_EACH)


def slot_first_rows():
    row = lax.broadcasted_iota(jnp.int32, (PARTS, DEPTH), 1)
    return (row == MAIN * lax.broadcasted_iota(jnp.int32, (PARTS, DEPTH), 0)).astype(BF16)


def qkv_kernel(
    tokens, owners, fold, perm_a, perm_b, mine_a, other_a, mine_b, other_b, cos, sin,
    query_low, kv_low, query_raw, key_raw, rows_a, rows_b, gain_d, gain_h,
):
    first_rows = slot_first_rows()
    gain_at = pl.ds(QW + QW // 4, LANES)
    gain_rows = (
        dot(first_rows[:, :HALF], mine_a[:, gain_at])
        + dot(first_rows[:, HALF:], other_a[:, gain_at])
    ).astype(BF16)
    for place, span in enumerate(GAIN_SPANS):
        spread = dot(gain_rows, fold[span[0] : span[0] + span[1], :], 1, 1)
        total = row_sum(jnp.where(gain_holders(owners, span), spread, 0.0))
        if place < 4:
            gain_d[place : place + 1, :] = total
        else:
            gain_h[place - 4 : place - 3, :] = total
    unit, _ = unit_of(tokens[...].astype(F32))
    normed = (unit * gain_d[0:1, :]).astype(BF16)
    rows_a[...] = dot(normed, perm_a[...]).astype(BF16)
    rows_b[...] = dot(normed, perm_b[...]).astype(BF16)
    cos_rows, sin_rows = cos[...], sin[...]
    for head in range(HEADS):
        raw = packed_product(rows_a, mine_a, other_a, head * HD, QW, head, HD)
        at = pl.ds(head * HD, HD)
        query_raw[:, at] = raw
        normed_raw = unit_of(raw)[0] * gain_h[0:1, :]
        query_low[:, at] = (rotate(normed_raw, cos_rows, sin_rows) * HD**-0.5).astype(BF16)
    kv = [
        packed_product(rows_b, mine_b, other_b, c * LANES, 2 * HD, c, LANES) for c in range(4)
    ]
    raw = jnp.concatenate(kv[:2], axis=1)
    key_raw[...] = raw
    kv_low[:, :HD] = rotate(unit_of(raw)[0] * gain_h[1:2, :], cos_rows, sin_rows).astype(BF16)
    kv_low[:, HD:] = jnp.concatenate(kv[2:], axis=1).astype(BF16)


def allowed_pairs(block_index, positions):
    query_index = block_index * BLK + lax.broadcasted_iota(jnp.int32, (BLK, SPAN), 0)
    key_index = (block_index - BACK) * BLK + lax.broadcasted_iota(jnp.int32, (BLK, SPAN), 1)
    return (
        (key_index <= query_index)
        & (key_index > query_index - WIN)
        & (key_index >= query_index - positions[...])
    )


def attend_kernel(
    where, tokens, positions, gain_d, perm_a, perm_b, mine_b, other_b, query_low, kv_all,
    heads_out, log_total, attn_proj, middle, rows_a, rows_b, out_w,
):
    place_groups(out_w, where[0], SLOTS_B, mine_b, other_b, 2 * HD + HD // 2, (0, 1), 2)
    allowed = allowed_pairs(where[1], positions)
    for head in range(HEADS):
        at = pl.ds(head * HD, HD)
        scores = dot(query_low[:, at], kv_all[:, :HD], 1, 1)
        scores = jnp.where(allowed, scores, lowest)
        row_max = jnp.max(scores, axis=-1, keepdims=True)
        expo = jnp.exp(scores - row_max)
        total = jnp.sum(expo, axis=-1, keepdims=True)
        log_total[:, column(head)] = jnp.broadcast_to(row_max + jnp.log(total), (BLK, LANES))
        probs = (expo * (1.0 / total)).astype(BF16)
        heads_out[:, at] = dot(probs, kv_all[:, HD:]).astype(BF16)
    proj = dot(heads_out[...], out_w[...])
    attn_proj[...] = proj
    mid = tokens[...].astype(F32) + unit_of(proj)[0] * gain_d[1:2, :]
    middle[...] = mid
    normed = (unit_of(mid)[0] * gain_d[2:3, :]).astype(BF16)
    rows_a[...] = dot(normed, perm_a[...]).astype(BF16)
    rows_b[...] = dot(normed, perm_b[...]).astype(BF16)


TILE = 256
TILES = FF // TILE
TANH_SCALE = float(np.sqrt(2.0 / np.pi))


def ffn_pieces_in(pieces, weights, sems, spans):
    copies = [
        [
            pltpu.make_async_copy(
                piece.at[:, pl.ds(*span)],
                weights[at // 4].at[pl.ds(at % 4 * (DEPTH // 4), DEPTH // 4), pl.ds(*span)],
                sems.at[8 * place + at],
            )
            for at, piece in enumerate(pieces)
        ]
        for place, span in enumerate(spans)
    ]
    for group in copies:
        for copy in group:
            copy.start()
    return copies


def halves(weights):
    return weights.at[pl.ds(0, HALF)], weights.at[pl.ds(HALF, HALF)]


def ffn_kernel(
    where, middle, cotangent, gain_d, rows_a, rows_b, a_0, a_1, a_2, a_3, b_0, b_1, b_2, b_3,
    layer_out, keep_a, send_a, keep_b, send_b, gate_g, up_g, gain_grad,
    weights_a, weights_b, down_w, down_grad, active_s, slope_s, hidden_s, rows_at, rows_bt, sems,
):
    me = where[0]
    down_at = FF + FF // 4
    spans = ((FF, FF // 4), (0, FF // 2), (FF // 2, FF // 2), (down_at, 2 * D))
    tail_in, first_in, second_in, down_in = ffn_pieces_in(
        (a_0, a_1, a_2, a_3, b_0, b_1, b_2, b_3), (weights_a, weights_b), sems, spans
    )
    rows_at[...] = rows_a[...].T
    rows_bt[...] = rows_b[...].T
    mine_a, other_a = halves(weights_a)
    mine_b, other_b = halves(weights_b)

    def forward(tile):
        at = pl.multiple_of(tile * TILE, TILE)
        tail_at = pl.multiple_of(FF + tile % 2 * TILE, TILE)
        gate = packed_product(rows_a, mine_a, other_a, at, tail_at, tile // 2, TILE)
        up = packed_product(rows_b, mine_b, other_b, at, tail_at, tile // 2, TILE)
        cols = pl.ds(at, TILE)
        square = gate * gate
        tanh = jnp.tanh(TANH_SCALE * (gate + 0.044715 * gate * square))
        active = 0.5 * gate * (1.0 + tanh)
        slope = 0.5 * (1.0 + tanh) + 0.5 * gate * (1.0 - tanh * tanh) * TANH_SCALE * (
            1.0 + 3.0 * 0.044715 * square
        )
        active_s[:, cols] = active
        slope_s[:, cols] = up * slope
        hidden_s[:, cols] = (active * up).astype(BF16)

    for copy in tail_in + first_in:
        copy.wait()
    pl.loop(0, TILES // 2)(forward)
    for copy in second_in:
        copy.wait()
    pl.loop(TILES // 2, TILES)(forward)
    for copy in down_in:
        copy.wait()
    place_groups(down_w, me, SLOTS_A, mine_a, other_a, down_at, (0, 1), 4)
    place_groups(down_w, me, SLOTS_B, mine_b, other_b, down_at, (2, 3), 4)
    proj = dot(hidden_s[...], down_w[...])
    unit, inverse = unit_of(proj)
    layer_out[...] = (middle[...] + unit * gain_d[3:4, :]).astype(BF16)
    out_grad = cotangent[...].astype(F32)
    gain_grad[0:1, :] = row_sum(out_grad * unit)
    proj_grad = rms_values_grad(out_grad, unit, inverse, gain_d[3:4, :]).astype(BF16)

    @pl.loop(0, TILES)
    def backward(tile):
        at = pl.multiple_of(tile * TILE, TILE)
        cols = pl.ds(at, TILE)
        hidden_grad = dot(proj_grad, down_w[cols, :], 1, 1)
        down_grad[cols, :] = dot(hidden_s[:, cols], proj_grad, 0, 0).astype(BF16)
        gate_grad = (hidden_grad * slope_s[:, cols]).astype(BF16)
        up_grad = (hidden_grad * active_s[:, cols]).astype(BF16)
        gate_g[:, cols] = gate_grad
        up_g[:, cols] = up_grad
        packed_grad(rows_at[:DEPTH, :], gate_grad, keep_a, send_a, at)
        packed_grad(rows_bt[:DEPTH, :], up_grad, keep_b, send_b, at)

    width = FF // 4
    for rows_t, grad_s, keep, send in (
        (rows_at, gate_g, keep_a, send_a),
        (rows_bt, up_g, keep_b, send_b),
    ):
        tail_grad = jnp.zeros((DEPTH, width), F32)
        for quarter in range(4):
            part = grad_s[:, pl.ds(quarter * width, width)]
            tail_grad += dot(quarter_rows_t(rows_t[DEPTH:, :], quarter), part)
        keep[:, pl.ds(FF, width)] = tail_grad[:HALF].astype(BF16)
        send[:, pl.ds(FF, width)] = tail_grad[HALF:].astype(BF16)
    take_groups(down_grad, me, SLOTS_A, keep_a, send_a, down_at, (0, 1), 4)
    take_groups(down_grad, me, SLOTS_B, keep_b, send_b, down_at, (2, 3), 4)


def ffn_back_kernel(
    middle, cotangent, gain_d, perm_a, perm_b, gate_g, up_g, a_0, a_1, a_2, a_3, b_0, b_1, b_2,
    b_3, mid_grad, gain_grad, weights_a, weights_b, sems,
):
    (copies,) = ffn_pieces_in(
        (a_0, a_1, a_2, a_3, b_0, b_1, b_2, b_3),
        (weights_a, weights_b),
        sems,
        ((0, FF + FF // 4),),
    )
    width = FF // 4
    normed_grad = jnp.zeros((BLK, D), F32)
    for at, grad_s, weights, perm in ((0, gate_g, weights_a, perm_a), (4, up_g, weights_b, perm_b)):
        for copy in copies[at : at + 4]:
            copy.wait()
        tail_back = jnp.zeros((BLK, DEPTH), F32)
        for quarter in range(4):
            part = grad_s[:, pl.ds(quarter * width, width)]
            tail_back += quarter_rows(dot(part, weights[:, pl.ds(FF, width)], 1, 1), quarter)
        back = jnp.concatenate([dot(grad_s[...], weights[:, :FF], 1, 1), tail_back], axis=1)
        normed_grad += natural_columns(back, perm[...])
    unit, inverse = unit_of(middle[...])
    gain_grad[0:1, :] = row_sum(normed_grad * unit)
    mid_grad[...] = cotangent[...].astype(F32) + rms_values_grad(
        normed_grad, unit, inverse, gain_d[2:3, :]
    )


def attend_back_kernel(
    where, mid_grad, attn_proj, positions, gain_d, gain_h, out_w, heads_out, query_low, kv_all,
    log_total, query_raw, cos, sin, rows_a, mine_a, other_a,
    kv_earlier, kv_own, query_keep, query_send, out_keep, out_send, back_a, gain_grad_d,
    gain_grad_h, out_grad_s, kv_grad, query_grad_s, rows_t,
):
    incoming = mid_grad[...]
    unit, inverse = unit_of(attn_proj[...])
    gain_grad_d[0:1, :] = row_sum(incoming * unit)
    proj_grad = rms_values_grad(incoming, unit, inverse, gain_d[1:2, :]).astype(BF16)
    for head in range(HEADS):
        at = pl.ds(head * HD, HD)
        out_grad_s[at, :] = dot(heads_out[:, at], proj_grad, 0, 0).astype(BF16)
    take_groups(out_grad_s, where[0], SLOTS_B, out_keep, out_send, 0, (0, 1), 2)
    allowed = allowed_pairs(where[1], positions)
    cos_rows, sin_rows = cos[...], sin[...]
    rows_t[...] = rows_a[...].T
    total_a = jnp.zeros((BLK, 2 * DEPTH), F32)
    gain_total = jnp.zeros((1, HD), F32)
    keys_grad = jnp.zeros((SPAN, HD), F32)
    values_grad = jnp.zeros((SPAN, HD), F32)
    for head in range(HEADS):
        at = pl.ds(head * HD, HD)
        heads_grad = dot(proj_grad, out_w[at, :], 1, 1).astype(BF16)
        scores = dot(query_low[:, at], kv_all[:, :HD], 1, 1)
        log_rows = log_total[:, pl.ds(head * LANES, 1)]
        probs = jnp.where(allowed, jnp.exp(jnp.where(allowed, scores - log_rows, 0.0)), 0.0)
        prob_grad = dot(heads_grad, kv_all[:, HD:], 1, 1)
        delta = jnp.sum(probs * prob_grad, axis=-1, keepdims=True)
        score_grad = (probs * (prob_grad - delta)).astype(BF16)
        keys_grad += dot(score_grad, query_low[:, at], 0, 0)
        values_grad += dot(probs.astype(BF16), heads_grad, 0, 0)
        query_grad = dot(score_grad, kv_all[:, :HD]) * HD**-0.5
        query_rot = rotate(query_grad, cos_rows, -sin_rows)
        unit, inverse = unit_of(query_raw[:, at])
        gain_total += row_sum(query_rot * unit)
        raw_grad = rms_values_grad(query_rot, unit, inverse, gain_h[0:1, :]).astype(BF16)
        query_grad_s[:, at] = raw_grad
        total_a += packed_back(raw_grad, mine_a, other_a, head * HD, QW, head)
        packed_grad(rows_t[:DEPTH, :], raw_grad, query_keep, query_send, head * HD)
    gain_grad_h[0:1, :] = gain_total
    kv_grad[:, :HD] = keys_grad
    kv_grad[:, HD:] = values_grad
    kv_earlier[...] = kv_grad[: BACK * BLK, :].astype(BF16)
    kv_own[...] = kv_grad[BACK * BLK :, :]
    back_a[...] = total_a
    tail = jnp.zeros((DEPTH, HD), F32)
    for head in range(HEADS):
        tail += dot(
            quarter_rows_t(rows_t[DEPTH:, :], head), query_grad_s[:, pl.ds(head * HD, HD)]
        )
    query_keep[:, pl.ds(QW, HD)] = tail[:HALF].astype(BF16)
    query_send[:, pl.ds(QW, HD)] = tail[HALF:].astype(BF16)


def input_kernel(
    tokens, mid_grad, gain_d, gain_h, perm_a, perm_b, rows_b, mine_b, other_b, kv_own, came_one,
    came_two, key_raw, cos, sin, back_a, owners, fold, out_gg, ffn_out_gg, ffn_in_gg, query_gg,
    input_grad, kv_keep, kv_send, rows_t,
):
    total = kv_own[...] + came_one[...].astype(F32) + came_two[...].astype(F32)
    key_rot = rotate(total[:, :HD], cos[...], -sin[...])
    unit, inverse = unit_of(key_raw[...])
    key_gg = row_sum(key_rot * unit)
    key_grad = rms_values_grad(key_rot, unit, inverse, gain_h[1:2, :]).astype(BF16)
    raw_grad = jnp.concatenate([key_grad, total[:, HD:].astype(BF16)], axis=1)
    rows_t[...] = rows_b[...].T
    back_b = jnp.zeros((BLK, 2 * DEPTH), F32)
    tail = jnp.zeros((DEPTH, LANES), F32)
    for c in range(4):
        part = raw_grad[:, c * LANES : (c + 1) * LANES]
        back_b += packed_back(part, mine_b, other_b, c * LANES, 2 * HD, c)
        tail += dot(quarter_rows_t(rows_t[DEPTH:, :], c), part)
    packed_grad(rows_t[:DEPTH, :], raw_grad, kv_keep, kv_send, 0)
    kv_keep[:, pl.ds(2 * HD, LANES)] = tail[:HALF].astype(BF16)
    kv_send[:, pl.ds(2 * HD, LANES)] = tail[HALF:].astype(BF16)
    normed_grad = natural_columns(back_a[...], perm_a[...]) + natural_columns(
        back_b, perm_b[...]
    )
    unit, inverse = unit_of(tokens[...].astype(F32))
    in_gg = row_sum(normed_grad * unit)
    gain_grads = (in_gg, out_gg[...], ffn_in_gg[...], ffn_out_gg[...], query_gg[...], key_gg)
    gain_rows = jnp.zeros((PARTS, LANES), F32)
    for grad, span in zip(gain_grads, GAIN_SPANS):
        held = jnp.where(gain_holders(owners, span), grad, 0.0).astype(BF16)
        gain_rows += dot(held, fold[span[0] : span[0] + span[1], :])
    gain_rows = dot(slot_first_rows(), gain_rows.astype(BF16), 0, 0).astype(BF16)
    gain_at = pl.ds(2 * HD + LANES, LANES)
    kv_keep[:, gain_at] = gain_rows[:HALF]
    kv_send[:, gain_at] = gain_rows[HALF:]
    input_grad[...] = mid_grad[...] + rms_values_grad(
        normed_grad, unit, inverse, gain_d[0:1, :]
    )


VMEM_LIMIT = 56 * 1024 * 1024


def call(kernel, outs, args, scratch=(), scalars=0, left=0, flops=1e6):
    vmem = pl.BlockSpec(memory_space=pltpu.VMEM)
    shapes = [jax.ShapeDtypeStruct(shape, kind) for shape, kind in outs]
    places = [pl.BlockSpec(memory_space=pltpu.SMEM)] * scalars
    places += [vmem] * (len(args) - scalars - left) + [pl.BlockSpec(memory_space=pl.ANY)] * left
    buffers = [pltpu.VMEM(shape, kind) for shape, kind in scratch]
    if left:
        buffers.append(pltpu.SemaphoreType.DMA((4 * left,)))
    return pl.pallas_call(
        kernel,
        out_shape=shapes,
        in_specs=places,
        out_specs=[vmem] * len(outs),
        scratch_shapes=buffers,
        compiler_params=pltpu.CompilerParams(vmem_limit_bytes=VMEM_LIMIT),
        cost_estimate=pl.CostEstimate(flops=int(flops), bytes_accessed=0, transcendentals=0),
    )(*args)


def together(*values):
    return lax.optimization_barrier(values)


def loosely(*values):
    return values


def shared_part(flat):
    for bit in range(extra_bits()):
        other = exchanged(flat, 1 << bit)
        mine_first = (lax.axis_index(AXES) >> bit) & 1 == 0
        flat = jnp.where(
            mine_first, jnp.concatenate([flat, other]), jnp.concatenate([other, flat])
        )
    return flat


def own_part(flat):
    for bit in reversed(range(extra_bits())):
        halves = jnp.split(flat, 2)
        mine_first = (lax.axis_index(AXES) >> bit) & 1 == 0
        keep = jnp.where(mine_first, halves[0], halves[1])
        send = jnp.where(mine_first, halves[1], halves[0]).astype(BF16)
        flat = keep + exchanged(send, 1 << bit).astype(F32)
    return flat


def pieces_z(piece):
    return [piece] + [exchanged_part(piece, k << Z_BITS[0]) for k in range(1, 4)]


def stacked(*pieces):
    return jnp.concatenate(pieces, axis=0)


def added(keep, came):
    return keep.astype(F32) + came.astype(F32)


def halved(total):
    half = total.shape[0] // 2
    return total[:half].astype(BF16), total[half:].astype(BF16)


def sent_z(total, k):
    return exchanged_part(total[k * MAIN : (k + 1) * MAIN].astype(BF16), k << Z_BITS[0])


def permutation(slots, me):
    rows = D // PARTS
    first = (jnp.asarray(slots) ^ me)[:, None] * rows
    inner = jnp.arange(MAIN, dtype=jnp.int32)[None, :]
    target = jnp.concatenate([(first + inner).reshape(-1), (first + MAIN + inner % 4).reshape(-1)])
    return (jnp.arange(D, dtype=jnp.int32)[:, None] == target[None, :]).astype(BF16)


def local(
    tokens, positions, cotangent, w_query, w_key, w_value, w_out, w_gate, w_up, w_down, gains
):
    me = lax.axis_index(AXES) >> extra_bits()
    block_index = lax.axis_index("seq")
    where = jnp.stack([me, block_index]).astype(jnp.int32)
    parts = [
        shared_part(w).reshape(-1, LANES)
        for w in (w_query, w_key, w_value, w_out, w_gate, w_up, w_down)
    ]
    gain_part = shared_part(gains)
    gain_each = gain_part.shape[0]
    gain_block = jnp.pad(gain_part[None, :], ((0, MAIN - 1), (0, LANES - gain_each)))
    attn, ffn = call(
        pack_kernel,
        [((MAIN, ATTN_A + ATTN_B), BF16), ((MAIN, 2 * FFN_A), BF16)],
        parts + [gain_block],
        [((320, LANES), F32), ((MAIN, FF // 4), F32)],
    )
    pieces, ffn = together(pieces_z(attn), ffn)
    attn_z = stacked(*pieces)
    attn_a, attn_b = attn_z[:, :ATTN_A], attn_z[:, ATTN_A:]
    ffn_two = exchanged_part(ffn, 2 << Z_BITS[0])
    next_a, next_b = exchanged_part(attn_a, 1 << ORDER_A[0]), exchanged_part(attn_b, 1 << ORDER_B[0])
    next_a, next_b, ffn_two, ffn = loosely(next_a, next_b, ffn_two, ffn)
    attn_a, attn_b = stacked(attn_a, next_a), stacked(attn_b, next_b)
    ffn_one = exchanged_part(ffn, 1 << Z_BITS[0])
    ffn_three = exchanged_part(ffn, 3 << Z_BITS[0])
    next_a, next_b = exchanged_part(attn_a, 1 << ORDER_A[1]), exchanged_part(attn_b, 1 << ORDER_B[1])
    next_a, next_b, ffn_one, ffn_three = loosely(next_a, next_b, ffn_one, ffn_three)
    attn_a, attn_b = stacked(attn_a, next_a), stacked(attn_b, next_b)
    other_a = exchanged_part(attn_a, 1 << CORE)
    other_b = exchanged_part(attn_b, 1 << CORE)
    ffn_z = stacked(ffn, ffn_one, ffn_two, ffn_three)
    ffn_a, ffn_b = ffn_z[:, :FFN_A], ffn_z[:, FFN_A:]
    next_a, next_b = exchanged_part(ffn_a, 1 << ORDER_A[0]), exchanged_part(ffn_b, 1 << ORDER_B[0])

    perm_a = permutation(SLOTS_A, me)
    perm_b = permutation(SLOTS_B, me)
    owners_a = (jnp.asarray(SLOTS_A) ^ me)[:, None]
    owners_b = (jnp.asarray(SLOTS_B) ^ me)[:, None]
    fold = gain_fold()

    freq_table = 10000.0 ** (-2.0 * jnp.arange(HD // 2, dtype=F32) / HD)
    angle_rows = positions.astype(F32)[:, None] * freq_table[None, :]
    cos_rows = jnp.cos(angle_rows)
    sin_rows = jnp.sin(angle_rows)
    places = positions[:, None]

    rows = (BLK, 2 * DEPTH)
    query_low, kv_low, query_raw, key_raw, one_a, one_b, gain_d, gain_h = call(
        qkv_kernel,
        [
            ((BLK, QW), BF16),
            ((BLK, 2 * HD), BF16),
            ((BLK, QW), F32),
            ((BLK, HD), F32),
            (rows, BF16),
            (rows, BF16),
            ((4, D), F32),
            ((2, HD), F32),
        ],
        [tokens, owners_a, fold, perm_a, perm_b, attn_a, other_a, attn_b, other_b]
        + [cos_rows, sin_rows],
        flops=9e9,
    )
    query_low, kv_low, next_a, next_b = loosely(query_low, kv_low, next_a, next_b)
    ffn_a, ffn_b = stacked(ffn_a, next_a), stacked(ffn_b, next_b)
    earlier = [passed_along(kv_low, "seq", back_step) for back_step in range(BACK, 0, -1)]
    kv_all = jnp.concatenate(earlier + [kv_low], axis=0)
    heads_out, log_total, attn_proj, middle, two_a, two_b, out_w = call(
        attend_kernel,
        [
            ((BLK, QW), BF16),
            ((BLK, HEADS * LANES), F32),
            ((BLK, D), F32),
            ((BLK, D), F32),
            (rows, BF16),
            (rows, BF16),
            ((QW, D), BF16),
        ],
        [where, tokens, places, gain_d, perm_a, perm_b, attn_b, other_b, query_low, kv_all],
        scalars=1,
        flops=9e9,
    )
    next_a, next_b = exchanged_part(ffn_a, 1 << ORDER_A[1]), exchanged_part(ffn_b, 1 << ORDER_B[1])
    other_ffn_a, other_ffn_b = exchanged_part(ffn_a, 1 << CORE), exchanged_part(ffn_b, 1 << CORE)
    middle, two_a, two_b, next_a, next_b, other_ffn_a, other_ffn_b = loosely(
        middle, two_a, two_b, next_a, next_b, other_ffn_a, other_ffn_b
    )
    ffn_all = [ffn_a, next_a, other_ffn_a, exchanged_part(next_a, 1 << CORE)]
    ffn_all += [ffn_b, next_b, other_ffn_b, exchanged_part(next_b, 1 << CORE)]
    packed = ((HALF, FFN_A), BF16)
    whole = ((DEPTH, FFN_A), BF16)
    gate_up = ((DEPTH, FF + FF // 4), BF16)
    wide = ((BLK, FF), BF16)
    layer_out, keep_a, send_a, keep_b, send_b, gate_g, up_g, ffn_out_gg = call(
        ffn_kernel,
        [((BLK, D), BF16), packed, packed, packed, packed, wide, wide, ((1, D), F32)],
        [where, middle, cotangent, gain_d, two_a, two_b] + ffn_all,
        [
            whole,
            whole,
            ((FF, D), BF16),
            ((FF, D), BF16),
            ((BLK, FF), F32),
            ((BLK, FF), F32),
            wide,
            ((2 * DEPTH, BLK), BF16),
            ((2 * DEPTH, BLK), BF16),
        ],
        scalars=1,
        left=8,
    )
    mid_grad, ffn_in_gg = call(
        ffn_back_kernel,
        [((BLK, D), F32), ((1, D), F32)],
        [middle, cotangent, gain_d, perm_a, perm_b, gate_g, up_g] + ffn_all,
        [gate_up, gate_up],
        left=8,
    )
    came_a, came_b = exchanged_part(send_a, 1 << CORE), exchanged_part(send_b, 1 << CORE)
    mid_grad, came_a, came_b = together(mid_grad, came_a, came_b)
    keep_a, send_a = halved(added(keep_a, came_a))
    keep_b, send_b = halved(added(keep_b, came_b))
    cut = FF + FF // 4
    came_a = exchanged_part(send_a[:, :cut], 1 << ORDER_A[1])
    came_b = exchanged_part(send_b[:, :cut], 1 << ORDER_B[1])
    sixteen = ((HALF, QW + QW // 4), BF16)
    (
        kv_earlier,
        kv_own,
        query_keep,
        query_send,
        out_keep,
        out_send,
        back_a,
        attn_out_gg,
        query_gg,
    ) = call(
        attend_back_kernel,
        [
            ((BACK * BLK, 2 * HD), BF16),
            ((BLK, 2 * HD), F32),
            sixteen,
            sixteen,
            sixteen,
            sixteen,
            (rows, F32),
            ((1, D), F32),
            ((1, HD), F32),
        ],
        [where, mid_grad, attn_proj, places, gain_d, gain_h, out_w, heads_out, query_low]
        + [kv_all, log_total, query_raw, cos_rows, sin_rows, one_a, attn_a, other_a],
        [((QW, D), BF16), ((SPAN, 2 * HD), F32), ((BLK, QW), BF16), ((2 * DEPTH, BLK), BF16)],
        scalars=1,
        flops=7e9,
    )
    kv_earlier, query_send, out_send, came_a, came_b = together(
        kv_earlier, query_send, out_send, came_a, came_b
    )
    came_a = [came_a, exchanged_part(send_a[:, cut:], 1 << ORDER_A[1])]
    came_b = [came_b, exchanged_part(send_b[:, cut:], 1 << ORDER_B[1])]
    came = [
        passed_along(kv_earlier[(BACK - step) * BLK : (BACK - step + 1) * BLK], "seq", -step)
        for step in range(1, BACK + 1)
    ]
    keep_a, send_a = halved(added(keep_a, jnp.concatenate(came_a, axis=1)))
    keep_b, send_b = halved(added(keep_b, jnp.concatenate(came_b, axis=1)))
    came_a = exchanged_part(send_a, 1 << ORDER_A[0])
    came_b = exchanged_part(send_b, 1 << ORDER_B[0])
    came_query = exchanged_part(query_send, 1 << CORE)
    came_out = exchanged_part(out_send, 1 << CORE)
    came, came_a, came_b, came_query, came_out = loosely(
        came, came_a, came_b, came_query, came_out
    )
    ffn_total = jnp.concatenate([added(keep_a, came_a), added(keep_b, came_b)], axis=1)
    query_keep, query_send = halved(added(query_keep, came_query))
    ffn_two = sent_z(ffn_total, 2)
    came_query = exchanged_part(query_send, 1 << ORDER_A[1])
    kv_width = 2 * HD + 2 * LANES
    input_grad, kv_keep, kv_send = call(
        input_kernel,
        [((BLK, D), F32), ((HALF, kv_width), BF16), ((HALF, kv_width), BF16)],
        [tokens, mid_grad, gain_d, gain_h, perm_a, perm_b, one_b, attn_b, other_b, kv_own]
        + came
        + [key_raw, cos_rows, sin_rows, back_a, owners_b, fold]
        + [attn_out_gg, ffn_out_gg, ffn_in_gg, query_gg],
        [((2 * DEPTH, BLK), BF16)],
        flops=5e9,
    )
    kv_send, ffn_two, came_query = loosely(kv_send, ffn_two, came_query)
    came_kv = exchanged_part(kv_send, 1 << CORE)
    ffn_one = sent_z(ffn_total, 1)
    came_kv, ffn_one = loosely(came_kv, ffn_one)
    rest_keep, rest_send = halved(
        jnp.concatenate([added(out_keep, came_out), added(kv_keep, came_kv)], axis=1)
    )
    query_keep, query_send = halved(added(query_keep, came_query))
    came_query = exchanged_part(query_send, 1 << ORDER_A[0])
    came_rest = exchanged_part(rest_send, 1 << ORDER_B[1])
    ffn_three = sent_z(ffn_total, 3)
    came_query, came_rest, ffn_three = loosely(came_query, came_rest, ffn_three)
    rest_keep, rest_send = halved(added(rest_keep, came_rest))
    came_rest = exchanged_part(rest_send, 1 << ORDER_B[0])
    (came_rest,) = loosely(came_rest)
    attn_total = jnp.concatenate(
        [added(query_keep, came_query), added(rest_keep, came_rest)], axis=1
    )
    attn_came = loosely(*(sent_z(attn_total, k) for k in range(1, 4)))
    ffn_sum = ffn_total[:MAIN] + sum(c.astype(F32) for c in (ffn_one, ffn_two, ffn_three))
    attn_sum = attn_total[:MAIN] + sum(c.astype(F32) for c in attn_came)
    flat = [((160, LANES), F32), ((40, LANES), F32), ((320, LANES), F32)]
    grad_gate, grad_up, grad_down = call(unpack_ffn_kernel, [flat[2]] * 3, [ffn_sum])
    grad_query, grad_key, grad_value, grad_out = call(
        unpack_attn_kernel, [flat[0], flat[1], flat[1], flat[0]], [attn_sum]
    )
    return (
        layer_out,
        input_grad,
        *(
            own_part(grad.reshape(-1))
            for grad in (
                grad_query,
                grad_key,
                grad_value,
                grad_out,
                grad_gate,
                grad_up,
                grad_down,
                attn_sum[0, QW + QW // 4 + 2 * D + 2 * HD + LANES :][:gain_each],
            )
        ),
    )


def solution(mesh):
    rows = P(AXES, None)
    flat = P(AXES)
    return jax.shard_map(
        local,
        mesh=mesh,
        in_specs=(rows, flat, rows) + (flat,) * 8,
        out_specs=(rows, rows) + (flat,) * 8,
        check_vma=False,
    )
```

```python
import functools
import numpy as np
import jax
import jax.numpy as jnp
from jax import lax
from jax.experimental import pallas as pl
from jax.experimental.pallas import tpu as pltpu
from jax.sharding import PartitionSpec as P

D = 640
HEADS = 4
HD = 256
FF = 2048
WIN = 512
BLK = 256
BACK = 2
AXES = ("dp", "seq")
F32 = jnp.float32
BF16 = jnp.bfloat16
QW = HEADS * HD
SPAN = (BACK + 1) * BLK

PARTS = 32
MAIN = 16
DEPTH = PARTS * MAIN
HALF = DEPTH // 2
KV_WIDTH = 2 * HD + HD // 2
LANES = 128
ATTN_A = QW + QW // 4 + LANES
ATTN_B = 2 * HD + HD // 2 + 2 * D
FFN_A = FF + FF // 4 + 2 * D
Z_BITS = (1, 2)
LOW, CORE, HIGH = 0, 3, 4
ORDER_A = (LOW, HIGH, CORE)
ORDER_B = (HIGH, LOW, CORE)

GAIN_SPANS = tuple((i * D, D) for i in range(4)) + ((4 * D, HD), (4 * D + HD, HD))
GAINS = 4 * D + 2 * HD
GAIN_EACH = GAINS // PARTS

epsilon = 1e-06
lowest = -1e30


def slot_shards(order):
    shards = np.arange(4, dtype=np.int32) << Z_BITS[0]
    for bit in order:
        shards = np.concatenate([shards, shards ^ (1 << bit)])
    return shards


SLOTS_A = slot_shards(ORDER_A)
SLOTS_B = slot_shards(ORDER_B)


def extra_bits():
    return (lax.axis_size("dp") * lax.axis_size("seq")).bit_length() - PARTS.bit_length()


def exchanged(value, mask):
    count = lax.axis_size("dp") * lax.axis_size("seq")
    return lax.ppermute(value, AXES, [(i, i ^ mask) for i in range(count)])


def exchanged_part(value, mask):
    return exchanged(value, mask << extra_bits())


def passed_along(value, axis, steps):
    count = lax.axis_size(axis)
    first, last = (max(0, -steps), min(count, count - steps))
    return lax.ppermute(value, axis, [(source, source + steps) for source in range(first, last)])


def dot(left, right, left_dim=1, right_dim=0):
    return lax.dot_general(
        left, right, (((left_dim,), (right_dim,)), ((), ())), preferred_element_type=F32
    )


def unit_of(values):
    inverse = lax.rsqrt(jnp.mean(values * values, axis=-1, keepdims=True) + epsilon)
    return values * inverse, inverse


def rms_values_grad(incoming, unit_rows, inverse, gain_row):
    scaled = incoming * gain_row
    return inverse * (scaled - unit_rows * jnp.mean(scaled * unit_rows, axis=-1, keepdims=True))


def rotate(values, cos_rows, sin_rows):
    middle_at = values.shape[-1] // 2
    first_half = values[..., :middle_at]
    second_half = values[..., middle_at:]
    return jnp.concatenate(
        [
            first_half * cos_rows - second_half * sin_rows,
            second_half * cos_rows + first_half * sin_rows,
        ],
        axis=-1,
    )


def row_sum(values):
    return jnp.sum(values, axis=0, keepdims=True)


def column(index):
    return pl.ds(index * LANES, LANES)


def pack_kernel(
    query, key, value, out, gate, up, down, gains, attn, ffn, wide, quarter
):
    def load(source):
        rows = source.shape[0]
        wide[:rows, :] = source[...].astype(F32)

    def put_main(target, at, blocks, block):
        target[:, pl.ds(at, LANES)] = wide[pl.ds(block, MAIN, stride=blocks), :].astype(BF16)

    def put_tail(row, at, blocks, block):
        quarter[4 * row : 4 * row + 4, pl.ds(at, LANES)] = wide[
            pl.ds(MAIN * blocks + block, 4, stride=blocks), :
        ]

    def put_matrix(source, target, at):
        load(source)
        blocks = source.shape[0] // 20
        for block in range(blocks):
            put_main(target, at + block * LANES, blocks, block)
            each = blocks // 4
            put_tail(block // each, block % each * LANES, blocks, block)
        width = blocks * LANES // 4
        target[:, pl.ds(at + blocks * LANES, width)] = quarter[:, :width].astype(BF16)

    def put_groups(target, at, groups):
        blocks = D // LANES
        for place, group in enumerate(groups):
            for block in range(blocks):
                target[:, pl.ds(at + place * D + block * LANES, LANES)] = wide[
                    pl.ds(group * MAIN * blocks + block, MAIN, stride=blocks), :
                ].astype(BF16)

    put_matrix(query, attn, 0)
    attn[:, pl.ds(QW + QW // 4, LANES)] = jnp.zeros((MAIN, LANES), BF16)
    attn[:, pl.ds(QW + QW // 4, GAIN_EACH)] = jnp.broadcast_to(gains[...], (MAIN, GAIN_EACH))
    for place, source in enumerate((key, value)):
        load(source)
        for block in range(2):
            put_main(attn, ATTN_A + 2 * D + place * HD + block * LANES, 2, block)
            put_tail(2 * place + block, 0, 2, block)
    attn[:, pl.ds(ATTN_A + 2 * D + 2 * HD, LANES)] = quarter[:, :LANES].astype(BF16)
    load(out)
    put_groups(attn, ATTN_A, (0, 1))
    put_matrix(gate, ffn, 0)
    put_matrix(up, ffn, FFN_A)
    load(down)
    put_groups(ffn, FF + FF // 4, (0, 1))
    put_groups(ffn, FFN_A + FF + FF // 4, (2, 3))


def unpack_matrix(source, at, target):
    blocks = target.shape[0] // 20
    each = blocks // 4
    tail_at = at + blocks * LANES
    for block in range(blocks):
        target[pl.ds(block, MAIN, stride=blocks), :] = source[:, pl.ds(at + block * LANES, LANES)]
        row = block // each * 4
        target[pl.ds(MAIN * blocks + block, 4, stride=blocks), :] = source[
            row : row + 4, pl.ds(tail_at + block % each * LANES, LANES)
        ]


def unpack_groups(source, at, target, groups):
    blocks = D // LANES
    for place, group in enumerate(groups):
        for block in range(blocks):
            target[pl.ds(group * MAIN * blocks + block, MAIN, stride=blocks), :] = source[
                :, pl.ds(at + place * D + block * LANES, LANES)
            ]


def unpack_ffn_kernel(own, one, two, three, gate, up, down, part):
    part[...] = sum(came[...].astype(F32) for came in (one, two, three)) + own[...]
    unpack_matrix(part, 0, gate)
    unpack_matrix(part, FFN_A, up)
    unpack_groups(part, FF + FF // 4, down, (0, 1))
    unpack_groups(part, FFN_A + FF + FF // 4, down, (2, 3))


def unpack_attn_kernel(own, one, two, three, query, key, value, out, gains, part):
    part[...] = sum(came[...].astype(F32) for came in (one, two, three)) + own[...]
    gains[...] = part[0:1, pl.ds(QW + QW // 4 + 2 * D + KV_WIDTH, GAIN_EACH)]
    unpack_matrix(part, 0, query)
    unpack_groups(part, QW + QW // 4, out, (0, 1))
    kv_at = QW + QW // 4 + 2 * D
    for place, target in enumerate((key, value)):
        for block in range(2):
            target[pl.ds(block, MAIN, stride=2), :] = part[
                :, pl.ds(kv_at + place * HD + block * LANES, LANES)
            ]
            row = 4 * (2 * place + block)
            target[pl.ds(2 * MAIN + block, 4, stride=2), :] = part[
                row : row + 4, pl.ds(kv_at + 2 * HD, LANES)
            ]


def quarter_mask(shape, dim, quarter):
    index = lax.broadcasted_iota(jnp.int32, shape, dim)
    return (index // 4 % 4 == quarter).astype(F32)


def quarter_rows(tail_rows, quarter):
    return tail_rows * quarter_mask((1, DEPTH), 1, quarter).astype(tail_rows.dtype)


def quarter_rows_t(tail_rows, quarter):
    return tail_rows * quarter_mask((DEPTH, 1), 0, quarter).astype(tail_rows.dtype)


def packed_product(rows, mine, other, main_at, tail_at, quarter, width):
    tail = quarter_rows(rows[:, DEPTH:], quarter)
    main_at, tail_at = pl.ds(main_at, width), pl.ds(tail_at, width)
    return (
        dot(rows[:, :HALF], mine[:, main_at])
        + dot(rows[:, HALF:DEPTH], other[:, main_at])
        + dot(tail[:, :HALF], mine[:, tail_at])
        + dot(tail[:, HALF:], other[:, tail_at])
    )


def packed_back(incoming, mine, other, main_at, tail_at, quarter):
    width = incoming.shape[1]
    main_at, tail_at = pl.ds(main_at, width), pl.ds(tail_at, width)
    tail = jnp.concatenate(
        [dot(incoming, mine[:, tail_at], 1, 1), dot(incoming, other[:, tail_at], 1, 1)], axis=1
    )
    return jnp.concatenate(
        [
            dot(incoming, mine[:, main_at], 1, 1),
            dot(incoming, other[:, main_at], 1, 1),
            quarter_rows(tail, quarter),
        ],
        axis=1,
    )


def packed_grad(rows_t, incoming, keep, send, main_at):
    grad = dot(rows_t, incoming).astype(BF16)
    main_at = pl.ds(main_at, incoming.shape[1])
    keep[:, main_at] = grad[:HALF]
    send[:, main_at] = grad[HALF:]


def permutation(columns):
    natural = lax.broadcasted_iota(jnp.int32, (D, 2 * DEPTH), 0)
    return (natural == columns[...]).astype(F32).astype(BF16)


def natural_columns(permuted, permutation):
    high = permuted.astype(BF16)
    low = (permuted - high.astype(F32)).astype(BF16)
    return dot(high, permutation, 1, 1) + dot(low, permutation, 1, 1)


def place_groups(target, me, slots, mine, other, at, groups, count):
    for slot in range(PARTS):
        source = mine if slot < PARTS // 2 else other
        row = slot % (PARTS // 2) * MAIN
        first = (me ^ int(slots[slot])) * (count * MAIN)
        for place, group in enumerate(groups):
            rows = pl.ds(pl.multiple_of(first + group * MAIN, MAIN), MAIN)
            target[rows, :] = source[row : row + MAIN, pl.ds(at + place * D, D)]


def take_groups(whole, me, slots, keep, send, at, groups, count):
    for slot in range(PARTS):
        target = keep if slot < PARTS // 2 else send
        row = slot % (PARTS // 2) * MAIN
        first = (me ^ int(slots[slot])) * (count * MAIN)
        for place, group in enumerate(groups):
            rows = pl.ds(pl.multiple_of(first + group * MAIN, MAIN), MAIN)
            target[row : row + MAIN, pl.ds(at + place * D, D)] = whole[rows, :]


def gain_fold():
    lane = np.arange(GAINS)[:, None] % GAIN_EACH == np.arange(LANES)[None, :]
    return jnp.asarray(lane, BF16)


def gain_holders(owners, span):
    entry = span[0] + lax.broadcasted_iota(jnp.int32, (PARTS, span[1]), 1)
    first = owners[...] * GAIN_EACH
    return (entry >= first) & (entry < first + GAIN_EACH)


def slot_first_rows():
    row = lax.broadcasted_iota(jnp.int32, (PARTS, DEPTH), 1)
    return (row == MAIN * lax.broadcasted_iota(jnp.int32, (PARTS, DEPTH), 0)).astype(BF16)


def qkv_kernel(
    tokens, owners, fold, columns_a, columns_b, mine_a, other_a, mine_b, other_b, cos, sin,
    query_low, kv_low, query_raw, key_raw, rows_a, rows_b, gain_d, gain_h,
):
    first_rows = slot_first_rows()
    gain_at = pl.ds(QW + QW // 4, LANES)
    gain_rows = (
        dot(first_rows[:, :HALF], mine_a[:, gain_at])
        + dot(first_rows[:, HALF:], other_a[:, gain_at])
    ).astype(BF16)
    for place, span in enumerate(GAIN_SPANS):
        spread = dot(gain_rows, fold[span[0] : span[0] + span[1], :], 1, 1)
        total = row_sum(jnp.where(gain_holders(owners, span), spread, 0.0))
        if place < 4:
            gain_d[place : place + 1, :] = total
        else:
            gain_h[place - 4 : place - 3, :] = total
    unit, _ = unit_of(tokens[...].astype(F32))
    normed = (unit * gain_d[0:1, :]).astype(BF16)
    rows_a[...] = dot(normed, permutation(columns_a)).astype(BF16)
    rows_b[...] = dot(normed, permutation(columns_b)).astype(BF16)
    cos_rows, sin_rows = cos[...], sin[...]
    for head in range(HEADS):
        raw = packed_product(rows_a, mine_a, other_a, head * HD, QW, head, HD)
        at = pl.ds(head * HD, HD)
        query_raw[:, at] = raw
        normed_raw = unit_of(raw)[0] * gain_h[0:1, :]
        query_low[:, at] = (rotate(normed_raw, cos_rows, sin_rows) * HD**-0.5).astype(BF16)
    kv = [
        packed_product(rows_b, mine_b, other_b, c * LANES, 2 * HD, c, LANES) for c in range(4)
    ]
    raw = jnp.concatenate(kv[:2], axis=1)
    key_raw[...] = raw
    kv_low[:, :HD] = rotate(unit_of(raw)[0] * gain_h[1:2, :], cos_rows, sin_rows).astype(BF16)
    kv_low[:, HD:] = jnp.concatenate(kv[2:], axis=1).astype(BF16)


def allowed_pairs(block_index, positions):
    query_index = block_index * BLK + lax.broadcasted_iota(jnp.int32, (BLK, SPAN), 0)
    key_index = (block_index - BACK) * BLK + lax.broadcasted_iota(jnp.int32, (BLK, SPAN), 1)
    return (
        (key_index <= query_index)
        & (key_index > query_index - WIN)
        & (key_index >= query_index - positions[...])
    )


def attend_kernel(
    where, tokens, positions, gain_d, columns_a, columns_b, mine_b, other_b, query_low, kv_two,
    kv_one, kv_low, heads_out, log_total, attn_proj, middle, rows_a, rows_b, out_w, kv_all,
):
    for place, block in enumerate((kv_two, kv_one, kv_low)):
        kv_all[place * BLK : (place + 1) * BLK, :] = block[...]
    place_groups(out_w, where[0], SLOTS_B, mine_b, other_b, 0, (0, 1), 2)
    allowed = allowed_pairs(where[1], positions)
    for head in range(HEADS):
        at = pl.ds(head * HD, HD)
        scores = dot(query_low[:, at], kv_all[:, :HD], 1, 1)
        scores = jnp.where(allowed, scores, lowest)
        row_max = jnp.max(scores, axis=-1, keepdims=True)
        expo = jnp.exp(scores - row_max)
        total = jnp.sum(expo, axis=-1, keepdims=True)
        log_total[:, column(head)] = jnp.broadcast_to(row_max + jnp.log(total), (BLK, LANES))
        probs = (expo * (1.0 / total)).astype(BF16)
        heads_out[:, at] = dot(probs, kv_all[:, HD:]).astype(BF16)
    proj = dot(heads_out[...], out_w[...])
    attn_proj[...] = proj
    mid = tokens[...].astype(F32) + unit_of(proj)[0] * gain_d[1:2, :]
    middle[...] = mid
    normed = (unit_of(mid)[0] * gain_d[2:3, :]).astype(BF16)
    rows_a[...] = dot(normed, permutation(columns_a)).astype(BF16)
    rows_b[...] = dot(normed, permutation(columns_b)).astype(BF16)


TILE = 256
TILES = FF // TILE
TANH_SCALE = float(np.sqrt(2.0 / np.pi))


def ffn_pieces_in(pieces, weights, sems, spans):
    copies = [
        [
            pltpu.make_async_copy(
                piece.at[:, pl.ds(*span)],
                weights[at // 4].at[pl.ds(at % 4 * (DEPTH // 4), DEPTH // 4), pl.ds(*span)],
                sems.at[8 * place + at],
            )
            for at, piece in enumerate(pieces)
        ]
        for place, span in enumerate(spans)
    ]
    for group in copies:
        for copy in group:
            copy.start()
    return copies


def halves(weights):
    return weights.at[pl.ds(0, HALF)], weights.at[pl.ds(HALF, HALF)]


def ffn_kernel(
    where, middle, cotangent, gain_d, rows_a, rows_b, a_0, a_1, a_2, a_3, b_0, b_1, b_2, b_3,
    layer_out, gain_grad, keep_a_out, send_a_out, keep_b_out, send_b_out, gate_out, up_out,
    keep_a, send_a, keep_b, send_b, gate_g, up_g, weights_a, weights_b, down_w, down_grad, active_s, slope_s, hidden_s, rows_at, rows_bt, sems,
):
    me = where[0]
    down_at = FF + FF // 4
    spans = ((FF, FF // 4), (0, FF // 2), (FF // 2, FF // 2), (down_at, 2 * D))
    tail_in, first_in, second_in, down_in = ffn_pieces_in(
        (a_0, a_1, a_2, a_3, b_0, b_1, b_2, b_3), (weights_a, weights_b), sems, spans
    )
    rows_at[...] = rows_a[...].T
    rows_bt[...] = rows_b[...].T
    leaving = []

    def leave(at, width, pairs):
        for source, target in pairs:
            cols = pl.ds(at, width)
            copy = pltpu.make_async_copy(
                source.at[:, cols], target.at[:, cols], sems.at[32 + len(leaving)]
            )
            copy.start()
            leaving.append(copy)

    sums = ((send_a, send_a_out), (send_b, send_b_out), (keep_a, keep_a_out), (keep_b, keep_b_out))
    mine_a, other_a = halves(weights_a)
    mine_b, other_b = halves(weights_b)

    def forward(tile):
        at = pl.multiple_of(tile * TILE, TILE)
        tail_at = pl.multiple_of(FF + tile % 2 * TILE, TILE)
        gate = packed_product(rows_a, mine_a, other_a, at, tail_at, tile // 2, TILE)
        up = packed_product(rows_b, mine_b, other_b, at, tail_at, tile // 2, TILE)
        cols = pl.ds(at, TILE)
        square = gate * gate
        tanh = jnp.tanh(TANH_SCALE * (gate + 0.044715 * gate * square))
        active = 0.5 * gate * (1.0 + tanh)
        slope = 0.5 * (1.0 + tanh) + 0.5 * gate * (1.0 - tanh * tanh) * TANH_SCALE * (
            1.0 + 3.0 * 0.044715 * square
        )
        active_s[:, cols] = active
        slope_s[:, cols] = up * slope
        hidden_s[:, cols] = (active * up).astype(BF16)

    for copy in tail_in + first_in:
        copy.wait()
    pl.loop(0, TILES // 2, unroll=True)(forward)
    for copy in second_in:
        copy.wait()
    pl.loop(TILES // 2, TILES, unroll=True)(forward)
    for copy in down_in:
        copy.wait()
    place_groups(down_w, me, SLOTS_A, mine_a, other_a, down_at, (0, 1), 4)
    place_groups(down_w, me, SLOTS_B, mine_b, other_b, down_at, (2, 3), 4)
    proj = dot(hidden_s[...], down_w[...])
    unit, inverse = unit_of(proj)
    layer_out[...] = (middle[...] + unit * gain_d[3:4, :]).astype(BF16)
    out_grad = cotangent[...].astype(F32)
    gain_grad[0:1, :] = row_sum(out_grad * unit)
    proj_grad = rms_values_grad(out_grad, unit, inverse, gain_d[3:4, :]).astype(BF16)

    for tile in range(TILES):
        at = tile * TILE
        cols = pl.ds(at, TILE)
        hidden_grad = dot(proj_grad, down_w[cols, :], 1, 1)
        down_grad[cols, :] = dot(hidden_s[:, cols], proj_grad, 0, 0).astype(BF16)
        gate_grad = (hidden_grad * slope_s[:, cols]).astype(BF16)
        up_grad = (hidden_grad * active_s[:, cols]).astype(BF16)
        gate_g[:, cols] = gate_grad
        up_g[:, cols] = up_grad
        packed_grad(rows_at[:DEPTH, :], gate_grad, keep_a, send_a, at)
        packed_grad(rows_bt[:DEPTH, :], up_grad, keep_b, send_b, at)
        if tile % 2:
            leave(at - TILE, 2 * TILE, sums + ((gate_g, gate_out), (up_g, up_out)))

    width = FF // 4
    for rows_t, grad_s, keep, send in (
        (rows_at, gate_g, keep_a, send_a),
        (rows_bt, up_g, keep_b, send_b),
    ):
        tail_grad = jnp.zeros((DEPTH, width), F32)
        for quarter in range(4):
            part = grad_s[:, pl.ds(quarter * width, width)]
            tail_grad += dot(quarter_rows_t(rows_t[DEPTH:, :], quarter), part)
        keep[:, pl.ds(FF, width)] = tail_grad[:HALF].astype(BF16)
        send[:, pl.ds(FF, width)] = tail_grad[HALF:].astype(BF16)
    leave(FF, width, sums)
    take_groups(down_grad, me, SLOTS_A, keep_a, send_a, down_at, (0, 1), 4)
    take_groups(down_grad, me, SLOTS_B, keep_b, send_b, down_at, (2, 3), 4)
    leave(down_at, 2 * D, sums)
    for copy in leaving:
        copy.wait()


def ffn_back_kernel(
    middle, cotangent, gain_d, columns_a, columns_b, gate_in, up_in, a_0, a_1, a_2, a_3, b_0, b_1,
    b_2, b_3, mid_grad, gain_grad, gate_g, up_g, weights_a, weights_b, sems,
):
    (copies,) = ffn_pieces_in(
        (a_0, a_1, a_2, a_3, b_0, b_1, b_2, b_3),
        (weights_a, weights_b),
        sems,
        ((0, FF + FF // 4),),
    )
    grads_in = [
        pltpu.make_async_copy(gate_in, gate_g, sems.at[8]),
        pltpu.make_async_copy(up_in, up_g, sems.at[9]),
    ]
    for copy in grads_in:
        copy.start()
    for copy in grads_in:
        copy.wait()
    width = FF // 4
    normed_grad = jnp.zeros((BLK, D), F32)
    for at, grad_s, weights, columns in ((0, gate_g, weights_a, columns_a), (4, up_g, weights_b, columns_b)):
        for copy in copies[at : at + 4]:
            copy.wait()
        tail_back = jnp.zeros((BLK, DEPTH), F32)
        for quarter in range(4):
            part = grad_s[:, pl.ds(quarter * width, width)]
            tail_back += quarter_rows(dot(part, weights[:, pl.ds(FF, width)], 1, 1), quarter)
        back = jnp.concatenate([dot(grad_s[...], weights[:, :FF], 1, 1), tail_back], axis=1)
        normed_grad += natural_columns(back, permutation(columns))
    unit, inverse = unit_of(middle[...])
    gain_grad[0:1, :] = row_sum(normed_grad * unit)
    mid_grad[...] = cotangent[...].astype(F32) + rms_values_grad(
        normed_grad, unit, inverse, gain_d[2:3, :]
    )


def attend_back_kernel(
    where, mid_grad, attn_proj, positions, gain_d, gain_h, out_w, heads_out, query_low, kv_all,
    log_total, query_raw, cos, sin, rows_a, mine_a, other_a,
    kv_earlier, kv_own, query_keep, query_send, out_keep, out_send, back_a, gain_grad_d,
    gain_grad_h, out_grad_s, kv_grad, query_grad_s, rows_t,
):
    incoming = mid_grad[...]
    unit, inverse = unit_of(attn_proj[...])
    gain_grad_d[0:1, :] = row_sum(incoming * unit)
    proj_grad = rms_values_grad(incoming, unit, inverse, gain_d[1:2, :]).astype(BF16)
    for head in range(HEADS):
        at = pl.ds(head * HD, HD)
        out_grad_s[at, :] = dot(heads_out[:, at], proj_grad, 0, 0).astype(BF16)
    take_groups(out_grad_s, where[0], SLOTS_B, out_keep, out_send, 0, (0, 1), 2)
    allowed = allowed_pairs(where[1], positions)
    cos_rows, sin_rows = cos[...], sin[...]
    rows_t[...] = rows_a[...].T
    total_a = jnp.zeros((BLK, 2 * DEPTH), F32)
    gain_total = jnp.zeros((1, HD), F32)
    keys_grad = jnp.zeros((SPAN, HD), F32)
    values_grad = jnp.zeros((SPAN, HD), F32)
    for head in range(HEADS):
        at = pl.ds(head * HD, HD)
        heads_grad = dot(proj_grad, out_w[at, :], 1, 1).astype(BF16)
        scores = dot(query_low[:, at], kv_all[:, :HD], 1, 1)
        log_rows = log_total[:, pl.ds(head * LANES, 1)]
        probs = jnp.where(allowed, jnp.exp(jnp.where(allowed, scores - log_rows, 0.0)), 0.0)
        prob_grad = dot(heads_grad, kv_all[:, HD:], 1, 1)
        delta = jnp.sum(probs * prob_grad, axis=-1, keepdims=True)
        score_grad = (probs * (prob_grad - delta)).astype(BF16)
        keys_grad += dot(score_grad, query_low[:, at], 0, 0)
        values_grad += dot(probs.astype(BF16), heads_grad, 0, 0)
        query_grad = dot(score_grad, kv_all[:, :HD]) * HD**-0.5
        query_rot = rotate(query_grad, cos_rows, -sin_rows)
        unit, inverse = unit_of(query_raw[:, at])
        gain_total += row_sum(query_rot * unit)
        raw_grad = rms_values_grad(query_rot, unit, inverse, gain_h[0:1, :]).astype(BF16)
        query_grad_s[:, at] = raw_grad
        total_a += packed_back(raw_grad, mine_a, other_a, head * HD, QW, head)
        packed_grad(rows_t[:DEPTH, :], raw_grad, query_keep, query_send, head * HD)
    gain_grad_h[0:1, :] = gain_total
    kv_grad[:, :HD] = keys_grad
    kv_grad[:, HD:] = values_grad
    kv_earlier[...] = kv_grad[: BACK * BLK, :].astype(BF16)
    kv_own[...] = kv_grad[BACK * BLK :, :]
    back_a[...] = total_a
    tail = jnp.zeros((DEPTH, HD), F32)
    for head in range(HEADS):
        tail += dot(
            quarter_rows_t(rows_t[DEPTH:, :], head), query_grad_s[:, pl.ds(head * HD, HD)]
        )
    query_keep[:, pl.ds(QW, HD)] = tail[:HALF].astype(BF16)
    query_send[:, pl.ds(QW, HD)] = tail[HALF:].astype(BF16)


def input_kernel(
    tokens, mid_grad, gain_d, gain_h, columns_a, columns_b, rows_b, mine_b, other_b, kv_own, came_one,
    came_two, key_raw, cos, sin, back_a, owners, fold, out_gg, ffn_out_gg, ffn_in_gg, query_gg,
    input_grad, kv_keep, kv_send, rows_t,
):
    total = kv_own[...] + came_one[...].astype(F32) + came_two[...].astype(F32)
    key_rot = rotate(total[:, :HD], cos[...], -sin[...])
    unit, inverse = unit_of(key_raw[...])
    key_gg = row_sum(key_rot * unit)
    key_grad = rms_values_grad(key_rot, unit, inverse, gain_h[1:2, :]).astype(BF16)
    raw_grad = jnp.concatenate([key_grad, total[:, HD:].astype(BF16)], axis=1)
    rows_t[...] = rows_b[...].T
    back_b = jnp.zeros((BLK, 2 * DEPTH), F32)
    tail = jnp.zeros((DEPTH, LANES), F32)
    for c in range(4):
        part = raw_grad[:, c * LANES : (c + 1) * LANES]
        back_b += packed_back(part, mine_b, other_b, c * LANES, 2 * HD, c)
        tail += dot(quarter_rows_t(rows_t[DEPTH:, :], c), part)
    packed_grad(rows_t[:DEPTH, :], raw_grad, kv_keep, kv_send, 0)
    kv_keep[:, pl.ds(2 * HD, LANES)] = tail[:HALF].astype(BF16)
    kv_send[:, pl.ds(2 * HD, LANES)] = tail[HALF:].astype(BF16)
    normed_grad = natural_columns(back_a[...], permutation(columns_a)) + natural_columns(
        back_b, permutation(columns_b)
    )
    unit, inverse = unit_of(tokens[...].astype(F32))
    in_gg = row_sum(normed_grad * unit)
    gain_grads = (in_gg, out_gg[...], ffn_in_gg[...], ffn_out_gg[...], query_gg[...], key_gg)
    gain_rows = jnp.zeros((PARTS, LANES), F32)
    for grad, span in zip(gain_grads, GAIN_SPANS):
        held = jnp.where(gain_holders(owners, span), grad, 0.0).astype(BF16)
        gain_rows += dot(held, fold[span[0] : span[0] + span[1], :])
    gain_rows = dot(slot_first_rows(), gain_rows.astype(BF16), 0, 0).astype(BF16)
    gain_at = pl.ds(2 * HD + LANES, LANES)
    kv_keep[:, gain_at] = gain_rows[:HALF]
    kv_send[:, gain_at] = gain_rows[HALF:]
    input_grad[...] = mid_grad[...] + rms_values_grad(
        normed_grad, unit, inverse, gain_d[0:1, :]
    )


VMEM_LIMIT = 56 * 1024 * 1024


def call(kernel, outs, args, scratch=(), scalars=0, left=0, outs_left=0, sems=0, windows=(), flops=1e6):
    vmem = pl.BlockSpec(memory_space=pltpu.VMEM)
    stays = pl.BlockSpec(memory_space=pl.ANY)
    shapes = [jax.ShapeDtypeStruct(shape, kind) for shape, kind in outs]
    places = [pl.BlockSpec(memory_space=pltpu.SMEM)] * scalars
    places += [vmem] * (len(args) - scalars - left) + [stays] * left
    for at, width, block in windows:
        rows = args[at].shape[0]
        places[at] = pl.BlockSpec((rows, width), functools.partial(lambda block, step: (0, block), block))
    buffers = [pltpu.VMEM(shape, kind) for shape, kind in scratch]
    if sems:
        buffers.append(pltpu.SemaphoreType.DMA((sems,)))
    return pl.pallas_call(
        kernel,
        out_shape=shapes,
        grid=(1,) if windows else (),
        in_specs=places,
        out_specs=[vmem] * (len(outs) - outs_left) + [stays] * outs_left,
        scratch_shapes=buffers,
        compiler_params=pltpu.CompilerParams(vmem_limit_bytes=VMEM_LIMIT),
        cost_estimate=pl.CostEstimate(flops=int(flops), bytes_accessed=0, transcendentals=0),
    )(*args)


def together(*values):
    return lax.optimization_barrier(values)


def shared_part(flat):
    for bit in range(extra_bits()):
        other = exchanged(flat, 1 << bit)
        mine_first = (lax.axis_index(AXES) >> bit) & 1 == 0
        flat = jnp.where(
            mine_first, jnp.concatenate([flat, other]), jnp.concatenate([other, flat])
        )
    return flat


def own_part(flat):
    for bit in reversed(range(extra_bits())):
        halves = jnp.split(flat, 2)
        mine_first = (lax.axis_index(AXES) >> bit) & 1 == 0
        keep = jnp.where(mine_first, halves[0], halves[1])
        send = jnp.where(mine_first, halves[1], halves[0]).astype(BF16)
        flat = keep + exchanged(send, 1 << bit).astype(F32)
    return flat


def pieces_z(piece):
    return [piece] + [exchanged_part(piece, k << Z_BITS[0]) for k in range(1, 4)]


def stacked(*pieces):
    return jnp.concatenate(pieces, axis=0)


def added(keep, came):
    return keep.astype(F32) + came.astype(F32)


def halved(total):
    half = total.shape[0] // 2
    return total[:half].astype(BF16), total[half:].astype(BF16)


def sent_z(total, k):
    return exchanged_part(total[k * MAIN : (k + 1) * MAIN].astype(BF16), k << Z_BITS[0])


def gathered_columns(slots, me):
    first = (jnp.asarray(slots) ^ me)[:, None] * (D // PARTS)
    inner = jnp.arange(MAIN, dtype=jnp.int32)[None, :]
    return jnp.concatenate([(first + inner).reshape(-1), (first + MAIN + inner % 4).reshape(-1)])[
        None, :
    ]


def local(
    tokens, positions, cotangent, w_query, w_key, w_value, w_out, w_gate, w_up, w_down, gains
):
    me = lax.axis_index(AXES) >> extra_bits()
    block_index = lax.axis_index("seq")
    where = jnp.stack([me, block_index]).astype(jnp.int32)
    parts = [
        shared_part(w).reshape(-1, LANES)
        for w in (w_query, w_key, w_value, w_out, w_gate, w_up, w_down)
    ]
    gain_part = shared_part(gains)
    gain_each = gain_part.shape[0]
    attn, ffn = call(
        pack_kernel,
        [((MAIN, ATTN_A + ATTN_B), BF16), ((MAIN, 2 * FFN_A), BF16)],
        parts + [gain_part[None, :]],
        [((320, LANES), F32), ((MAIN, FF // 4), F32)],
    )
    columns_a = gathered_columns(SLOTS_A, me)
    columns_b = gathered_columns(SLOTS_B, me)
    owners_a = (jnp.asarray(SLOTS_A) ^ me)[:, None]
    owners_b = (jnp.asarray(SLOTS_B) ^ me)[:, None]
    fold = gain_fold()

    freq_table = 10000.0 ** (-2.0 * jnp.arange(HD // 2, dtype=F32) / HD)
    angle_rows = positions.astype(F32)[:, None] * freq_table[None, :]
    cos_rows = jnp.cos(angle_rows)
    sin_rows = jnp.sin(angle_rows)
    places = positions[:, None]
    small = (where, places, cos_rows, sin_rows, columns_a, columns_b, owners_a, owners_b)
    pieces, ffn, small = together(pieces_z(attn), ffn, small)
    where, places, cos_rows, sin_rows, columns_a, columns_b, owners_a, owners_b = small
    attn_z = stacked(*pieces)
    attn_a, attn_b = attn_z[:, :ATTN_A], attn_z[:, ATTN_A:]
    ffn_two = exchanged_part(ffn, 2 << Z_BITS[0])
    next_a, next_b = exchanged_part(attn_a, 1 << ORDER_A[0]), exchanged_part(attn_b, 1 << ORDER_B[0])
    attn_a, attn_b = stacked(attn_a, next_a), stacked(attn_b, next_b)
    ffn_one = exchanged_part(ffn, 1 << Z_BITS[0])
    ffn_three = exchanged_part(ffn, 3 << Z_BITS[0])
    next_a, next_b = exchanged_part(attn_a, 1 << ORDER_A[1]), exchanged_part(attn_b, 1 << ORDER_B[1])
    attn_a, attn_b = stacked(attn_a, next_a), stacked(attn_b, next_b)
    other_a = exchanged_part(attn_a, 1 << CORE)
    other_b = exchanged_part(attn_b, 1 << CORE)
    ffn_z = stacked(ffn, ffn_one, ffn_two, ffn_three)
    ffn_a, ffn_b = ffn_z[:, :FFN_A], ffn_z[:, FFN_A:]
    next_a, next_b = exchanged_part(ffn_a, 1 << ORDER_A[0]), exchanged_part(ffn_b, 1 << ORDER_B[0])

    rows = (BLK, 2 * DEPTH)
    query_low, kv_low, query_raw, key_raw, one_a, one_b, gain_d, gain_h = call(
        qkv_kernel,
        [
            ((BLK, QW), BF16),
            ((BLK, 2 * HD), BF16),
            ((BLK, QW), F32),
            ((BLK, HD), F32),
            (rows, BF16),
            (rows, BF16),
            ((4, D), F32),
            ((2, HD), F32),
        ],
        [tokens, owners_a, fold, columns_a, columns_b, attn_a, other_a, attn_b, other_b]
        + [cos_rows, sin_rows],
        windows=[(7, KV_WIDTH, 2), (8, KV_WIDTH, 2)],
        flops=9e9,
    )
    ffn_a, ffn_b = stacked(ffn_a, next_a), stacked(ffn_b, next_b)
    earlier = [passed_along(kv_low, "seq", back_step) for back_step in range(BACK, 0, -1)]
    heads_out, log_total, attn_proj, middle, two_a, two_b, out_w, kv_all = call(
        attend_kernel,
        [
            ((BLK, QW), BF16),
            ((BLK, HEADS * LANES), F32),
            ((BLK, D), F32),
            ((BLK, D), F32),
            (rows, BF16),
            (rows, BF16),
            ((QW, D), BF16),
            ((SPAN, 2 * HD), BF16),
        ],
        [where, tokens, places, gain_d, columns_a, columns_b, attn_b, other_b, query_low]
        + earlier
        + [kv_low],
        windows=[(6, 2 * D, 0), (7, 2 * D, 0)],
        scalars=1,
        flops=9e9,
    )
    next_a, next_b = exchanged_part(ffn_a, 1 << ORDER_A[1]), exchanged_part(ffn_b, 1 << ORDER_B[1])
    other_ffn_a, other_ffn_b = exchanged_part(ffn_a, 1 << CORE), exchanged_part(ffn_b, 1 << CORE)
    ffn_all = [ffn_a, next_a, other_ffn_a, exchanged_part(next_a, 1 << CORE)]
    ffn_all += [ffn_b, next_b, other_ffn_b, exchanged_part(next_b, 1 << CORE)]
    packed = ((HALF, FFN_A), BF16)
    whole = ((DEPTH, FFN_A), BF16)
    gate_up = ((DEPTH, FF + FF // 4), BF16)
    wide = ((BLK, FF), BF16)
    layer_out, ffn_out_gg, keep_a, send_a, keep_b, send_b, gate_g, up_g = call(
        ffn_kernel,
        [((BLK, D), BF16), ((1, D), F32), packed, packed, packed, packed, wide, wide],
        [where, middle, cotangent, gain_d, two_a, two_b] + ffn_all,
        [
            packed,
            packed,
            packed,
            packed,
            wide,
            wide,
            whole,
            whole,
            ((FF, D), BF16),
            ((FF, D), BF16),
            ((BLK, FF), F32),
            ((BLK, FF), F32),
            wide,
            ((2 * DEPTH, BLK), BF16),
            ((2 * DEPTH, BLK), BF16),
        ],
        scalars=1,
        left=8,
        outs_left=6,
        sems=32 + 34,
    )
    mid_grad, ffn_in_gg = call(
        ffn_back_kernel,
        [((BLK, D), F32), ((1, D), F32)],
        [middle, cotangent, gain_d, columns_a, columns_b, gate_g, up_g] + ffn_all,
        [wide, wide, gate_up, gate_up],
        left=10,
        sems=10,
    )
    came_a, came_b = exchanged_part(send_a, 1 << CORE), exchanged_part(send_b, 1 << CORE)
    mid_grad, came_a, came_b = together(mid_grad, came_a, came_b)
    keep_a, send_a = halved(added(keep_a, came_a))
    keep_b, send_b = halved(added(keep_b, came_b))
    cut = FF + FF // 4
    came_a = exchanged_part(send_a[:, :cut], 1 << ORDER_A[1])
    came_b = exchanged_part(send_b[:, :cut], 1 << ORDER_B[1])
    sixteen = ((HALF, QW + QW // 4), BF16)
    (
        kv_earlier,
        kv_own,
        query_keep,
        query_send,
        out_keep,
        out_send,
        back_a,
        attn_out_gg,
        query_gg,
    ) = call(
        attend_back_kernel,
        [
            ((BACK * BLK, 2 * HD), BF16),
            ((BLK, 2 * HD), F32),
            sixteen,
            sixteen,
            sixteen,
            sixteen,
            (rows, F32),
            ((1, D), F32),
            ((1, HD), F32),
        ],
        [where, mid_grad, attn_proj, places, gain_d, gain_h, out_w, heads_out, query_low]
        + [kv_all, log_total, query_raw, cos_rows, sin_rows, one_a, attn_a, other_a],
        [((QW, D), BF16), ((SPAN, 2 * HD), F32), ((BLK, QW), BF16), ((2 * DEPTH, BLK), BF16)],
        windows=[(15, QW + QW // 4, 0), (16, QW + QW // 4, 0)],
        scalars=1,
        flops=7e9,
    )
    kv_earlier, query_send, out_send, came_a, came_b = together(
        kv_earlier, query_send, out_send, came_a, came_b
    )
    came_a = [came_a, exchanged_part(send_a[:, cut:], 1 << ORDER_A[1])]
    came_b = [came_b, exchanged_part(send_b[:, cut:], 1 << ORDER_B[1])]
    came = [
        passed_along(kv_earlier[(BACK - step) * BLK : (BACK - step + 1) * BLK], "seq", -step)
        for step in range(1, BACK + 1)
    ]
    keep_a, send_a = halved(added(keep_a, jnp.concatenate(came_a, axis=1)))
    keep_b, send_b = halved(added(keep_b, jnp.concatenate(came_b, axis=1)))
    came_a = exchanged_part(send_a, 1 << ORDER_A[0])
    came_b = exchanged_part(send_b, 1 << ORDER_B[0])
    came_query = exchanged_part(query_send, 1 << CORE)
    came_out = exchanged_part(out_send, 1 << CORE)
    ffn_total = jnp.concatenate([added(keep_a, came_a), added(keep_b, came_b)], axis=1)
    query_keep, query_send = halved(added(query_keep, came_query))
    came_query = exchanged_part(query_send, 1 << ORDER_A[1])
    kv_width = KV_WIDTH + LANES
    input_grad, kv_keep, kv_send = call(
        input_kernel,
        [((BLK, D), F32), ((HALF, kv_width), BF16), ((HALF, kv_width), BF16)],
        [tokens, mid_grad, gain_d, gain_h, columns_a, columns_b, one_b, attn_b, other_b, kv_own]
        + came
        + [key_raw, cos_rows, sin_rows, back_a, owners_b, fold]
        + [attn_out_gg, ffn_out_gg, ffn_in_gg, query_gg],
        [((2 * DEPTH, BLK), BF16)],
        windows=[(7, KV_WIDTH, 2), (8, KV_WIDTH, 2)],
        flops=5e9,
    )
    came_kv = exchanged_part(kv_send, 1 << CORE)
    ffn_then, _ = together(ffn_total, came_kv)
    ffn_came = [sent_z(ffn_then, k) for k in range(1, 4)]
    rest_keep, rest_send = halved(
        jnp.concatenate([added(out_keep, came_out), added(kv_keep, came_kv)], axis=1)
    )
    query_keep, query_send = halved(added(query_keep, came_query))
    came_query = exchanged_part(query_send, 1 << ORDER_A[0])
    came_rest = exchanged_part(rest_send, 1 << ORDER_B[1])
    rest_keep, rest_send = halved(added(rest_keep, came_rest))
    came_rest = exchanged_part(rest_send, 1 << ORDER_B[0])
    ffn_came, _ = together(ffn_came, came_rest)
    attn_total = jnp.concatenate(
        [added(query_keep, came_query), added(rest_keep, came_rest)], axis=1
    )
    attn_came = [sent_z(attn_total, k) for k in range(1, 4)]
    flat = [((160, LANES), F32), ((40, LANES), F32), ((320, LANES), F32)]
    grad_gate, grad_up, grad_down = call(
        unpack_ffn_kernel,
        [flat[2]] * 3,
        [ffn_total[:MAIN]] + ffn_came,
        [((MAIN, 2 * FFN_A), F32)],
    )
    grad_query, grad_key, grad_value, grad_out, grad_gains = call(
        unpack_attn_kernel,
        [flat[0], flat[1], flat[1], flat[0], ((1, GAIN_EACH), F32)],
        [attn_total[:MAIN]] + attn_came,
        [((MAIN, attn_total.shape[1]), F32)],
    )
    return (
        layer_out,
        input_grad,
        *(
            own_part(grad.reshape(-1))
            for grad in (
                grad_query,
                grad_key,
                grad_value,
                grad_out,
                grad_gate,
                grad_up,
                grad_down,
                grad_gains,
            )
        ),
    )


def solution(mesh):
    rows = P(AXES, None)
    flat = P(AXES)
    return jax.shard_map(
        local,
        mesh=mesh,
        in_specs=(rows, flat, rows) + (flat,) * 8,
        out_specs=(rows, rows) + (flat,) * 8,
        check_vma=False,
    )
```

```python
import functools
import numpy as np
import jax
import jax.numpy as jnp
from jax import lax
from jax.experimental import pallas as pl
from jax.experimental.pallas import tpu as pltpu
from jax.sharding import PartitionSpec as P

D = 640
HEADS = 4
HD = 256
FF = 2048
WIN = 512
BLK = 256
BACK = 2
AXES = ("dp", "seq")
F32 = jnp.float32
BF16 = jnp.bfloat16
QW = HEADS * HD
SPAN = (BACK + 1) * BLK

PARTS = 32
MAIN = 16
DEPTH = PARTS * MAIN
HALF = DEPTH // 2
KV_WIDTH = 2 * HD + HD // 2
LANES = 128
ATTN_A = QW + QW // 4 + LANES
ATTN_B = 2 * HD + HD // 2 + 2 * D
FFN_A = FF + FF // 4 + 2 * D
Z_BITS = (1, 2)
LOW, CORE, HIGH = 0, 3, 4
ORDER_A = (LOW, HIGH, CORE)
ORDER_B = (HIGH, LOW, CORE)

GAIN_SPANS = tuple((i * D, D) for i in range(4)) + ((4 * D, HD), (4 * D + HD, HD))
GAINS = 4 * D + 2 * HD
GAIN_EACH = GAINS // PARTS

epsilon = 1e-06
lowest = -1e30


def slot_shards(order):
    shards = np.arange(4, dtype=np.int32) << Z_BITS[0]
    for bit in order:
        shards = np.concatenate([shards, shards ^ (1 << bit)])
    return shards


SLOTS_A = slot_shards(ORDER_A)
SLOTS_B = slot_shards(ORDER_B)


def extra_bits():
    return (lax.axis_size("dp") * lax.axis_size("seq")).bit_length() - PARTS.bit_length()


def exchanged(value, mask):
    count = lax.axis_size("dp") * lax.axis_size("seq")
    return lax.ppermute(value, AXES, [(i, i ^ mask) for i in range(count)])


def exchanged_part(value, mask):
    return exchanged(value, mask << extra_bits())


def passed_along(value, axis, steps):
    count = lax.axis_size(axis)
    first, last = (max(0, -steps), min(count, count - steps))
    return lax.ppermute(value, axis, [(source, source + steps) for source in range(first, last)])


def dot(left, right, left_dim=1, right_dim=0):
    return lax.dot_general(
        left, right, (((left_dim,), (right_dim,)), ((), ())), preferred_element_type=F32
    )


def unit_of(values):
    inverse = lax.rsqrt(jnp.mean(values * values, axis=-1, keepdims=True) + epsilon)
    return values * inverse, inverse


def rms_values_grad(incoming, unit_rows, inverse, gain_row):
    scaled = incoming * gain_row
    return inverse * (scaled - unit_rows * jnp.mean(scaled * unit_rows, axis=-1, keepdims=True))


def rotate(values, cos_rows, sin_rows):
    middle_at = values.shape[-1] // 2
    first_half = values[..., :middle_at]
    second_half = values[..., middle_at:]
    return jnp.concatenate(
        [
            first_half * cos_rows - second_half * sin_rows,
            second_half * cos_rows + first_half * sin_rows,
        ],
        axis=-1,
    )


def row_sum(values):
    return jnp.sum(values, axis=0, keepdims=True)


def column(index):
    return pl.ds(index * LANES, LANES)


def pack_kernel(
    query, key, value, out, gate, up, down, gains, attn, ffn, wide, quarter
):
    def load(source):
        rows = source.shape[0]
        wide[:rows, :] = source[...].astype(F32)

    def put_main(target, at, blocks, block):
        target[:, pl.ds(at, LANES)] = wide[pl.ds(block, MAIN, stride=blocks), :].astype(BF16)

    def put_tail(row, at, blocks, block):
        quarter[4 * row : 4 * row + 4, pl.ds(at, LANES)] = wide[
            pl.ds(MAIN * blocks + block, 4, stride=blocks), :
        ]

    def put_matrix(source, target, at):
        load(source)
        blocks = source.shape[0] // 20
        for block in range(blocks):
            put_main(target, at + block * LANES, blocks, block)
            each = blocks // 4
            put_tail(block // each, block % each * LANES, blocks, block)
        width = blocks * LANES // 4
        target[:, pl.ds(at + blocks * LANES, width)] = quarter[:, :width].astype(BF16)

    def put_groups(target, at, groups):
        blocks = D // LANES
        for place, group in enumerate(groups):
            for block in range(blocks):
                target[:, pl.ds(at + place * D + block * LANES, LANES)] = wide[
                    pl.ds(group * MAIN * blocks + block, MAIN, stride=blocks), :
                ].astype(BF16)

    put_matrix(query, attn, 0)
    attn[:, pl.ds(QW + QW // 4, LANES)] = jnp.zeros((MAIN, LANES), BF16)
    attn[:, pl.ds(QW + QW // 4, GAIN_EACH)] = jnp.broadcast_to(gains[...], (MAIN, GAIN_EACH))
    for place, source in enumerate((key, value)):
        load(source)
        for block in range(2):
            put_main(attn, ATTN_A + 2 * D + place * HD + block * LANES, 2, block)
            put_tail(2 * place + block, 0, 2, block)
    attn[:, pl.ds(ATTN_A + 2 * D + 2 * HD, LANES)] = quarter[:, :LANES].astype(BF16)
    load(out)
    put_groups(attn, ATTN_A, (0, 1))
    put_matrix(gate, ffn, 0)
    put_matrix(up, ffn, FFN_A)
    load(down)
    put_groups(ffn, FF + FF // 4, (0, 1))
    put_groups(ffn, FFN_A + FF + FF // 4, (2, 3))


def unpack_matrix(source, at, target):
    blocks = target.shape[0] // 20
    each = blocks // 4
    tail_at = at + blocks * LANES
    for block in range(blocks):
        target[pl.ds(block, MAIN, stride=blocks), :] = source[:, pl.ds(at + block * LANES, LANES)]
        row = block // each * 4
        target[pl.ds(MAIN * blocks + block, 4, stride=blocks), :] = source[
            row : row + 4, pl.ds(tail_at + block % each * LANES, LANES)
        ]


def unpack_groups(source, at, target, groups):
    blocks = D // LANES
    for place, group in enumerate(groups):
        for block in range(blocks):
            target[pl.ds(group * MAIN * blocks + block, MAIN, stride=blocks), :] = source[
                :, pl.ds(at + place * D + block * LANES, LANES)
            ]


def unpack_ffn_kernel(own, one, two, three, gate, up, down, part):
    part[...] = sum(came[...].astype(F32) for came in (one, two, three)) + own[...]
    unpack_matrix(part, 0, gate)
    unpack_matrix(part, FFN_A, up)
    unpack_groups(part, FF + FF // 4, down, (0, 1))
    unpack_groups(part, FFN_A + FF + FF // 4, down, (2, 3))


def unpack_attn_kernel(own, one, two, three, query, key, value, out, gains, part):
    part[...] = sum(came[...].astype(F32) for came in (one, two, three)) + own[...]
    gains[...] = part[0:1, pl.ds(QW + QW // 4 + 2 * D + KV_WIDTH, GAIN_EACH)]
    unpack_matrix(part, 0, query)
    unpack_groups(part, QW + QW // 4, out, (0, 1))
    kv_at = QW + QW // 4 + 2 * D
    for place, target in enumerate((key, value)):
        for block in range(2):
            target[pl.ds(block, MAIN, stride=2), :] = part[
                :, pl.ds(kv_at + place * HD + block * LANES, LANES)
            ]
            row = 4 * (2 * place + block)
            target[pl.ds(2 * MAIN + block, 4, stride=2), :] = part[
                row : row + 4, pl.ds(kv_at + 2 * HD, LANES)
            ]


def quarter_mask(shape, dim, quarter):
    index = lax.broadcasted_iota(jnp.int32, shape, dim)
    return (index // 4 % 4 == quarter).astype(F32)


def quarter_rows(tail_rows, quarter):
    return tail_rows * quarter_mask((1, DEPTH), 1, quarter).astype(tail_rows.dtype)


def quarter_rows_t(tail_rows, quarter):
    return tail_rows * quarter_mask((DEPTH, 1), 0, quarter).astype(tail_rows.dtype)


def packed_product(rows, mine, other, main_at, tail_at, quarter, width):
    tail = quarter_rows(rows[:, DEPTH:], quarter)
    main_at, tail_at = pl.ds(main_at, width), pl.ds(tail_at, width)
    return (
        dot(rows[:, :HALF], mine[:, main_at])
        + dot(rows[:, HALF:DEPTH], other[:, main_at])
        + dot(tail[:, :HALF], mine[:, tail_at])
        + dot(tail[:, HALF:], other[:, tail_at])
    )


def packed_back(incoming, mine, other, main_at, tail_at, quarter):
    width = incoming.shape[1]
    main_at, tail_at = pl.ds(main_at, width), pl.ds(tail_at, width)
    tail = jnp.concatenate(
        [dot(incoming, mine[:, tail_at], 1, 1), dot(incoming, other[:, tail_at], 1, 1)], axis=1
    )
    return jnp.concatenate(
        [
            dot(incoming, mine[:, main_at], 1, 1),
            dot(incoming, other[:, main_at], 1, 1),
            quarter_rows(tail, quarter),
        ],
        axis=1,
    )


def packed_grad(rows_t, incoming, keep, send, main_at):
    grad = dot(rows_t, incoming).astype(BF16)
    main_at = pl.ds(main_at, incoming.shape[1])
    keep[:, main_at] = grad[:HALF]
    send[:, main_at] = grad[HALF:]


def permutation(columns):
    natural = lax.broadcasted_iota(jnp.int32, (D, 2 * DEPTH), 0)
    return (natural == columns[...]).astype(F32).astype(BF16)


def natural_columns(permuted, permutation):
    return dot(permuted.astype(BF16), permutation, 1, 1)


def place_groups(target, me, slots, mine, other, at, groups, count):
    for slot in range(PARTS):
        source = mine if slot < PARTS // 2 else other
        row = slot % (PARTS // 2) * MAIN
        first = (me ^ int(slots[slot])) * (count * MAIN)
        for place, group in enumerate(groups):
            rows = pl.ds(pl.multiple_of(first + group * MAIN, MAIN), MAIN)
            target[rows, :] = source[row : row + MAIN, pl.ds(at + place * D, D)]


def take_groups(whole, me, slots, keep, send, at, groups, count):
    for slot in range(PARTS):
        target = keep if slot < PARTS // 2 else send
        row = slot % (PARTS // 2) * MAIN
        first = (me ^ int(slots[slot])) * (count * MAIN)
        for place, group in enumerate(groups):
            rows = pl.ds(pl.multiple_of(first + group * MAIN, MAIN), MAIN)
            target[row : row + MAIN, pl.ds(at + place * D, D)] = whole[rows, :]


def gain_fold():
    lane = np.arange(GAINS)[:, None] % GAIN_EACH == np.arange(LANES)[None, :]
    return jnp.asarray(lane, BF16)


def gain_holders(owners, span):
    entry = span[0] + lax.broadcasted_iota(jnp.int32, (PARTS, span[1]), 1)
    first = owners[...] * GAIN_EACH
    return (entry >= first) & (entry < first + GAIN_EACH)


def slot_first_rows():
    row = lax.broadcasted_iota(jnp.int32, (PARTS, DEPTH), 1)
    return (row == MAIN * lax.broadcasted_iota(jnp.int32, (PARTS, DEPTH), 0)).astype(BF16)


def qkv_kernel(
    tokens, owners, fold, columns_a, columns_b, mine_a, other_a, mine_b, other_b, cos, sin,
    query_low, kv_low, query_raw, key_raw, rows_a, rows_b, gain_d, gain_h,
):
    first_rows = slot_first_rows()
    gain_at = pl.ds(QW + QW // 4, LANES)
    gain_rows = (
        dot(first_rows[:, :HALF], mine_a[:, gain_at])
        + dot(first_rows[:, HALF:], other_a[:, gain_at])
    ).astype(BF16)
    for place, span in enumerate(GAIN_SPANS):
        spread = dot(gain_rows, fold[span[0] : span[0] + span[1], :], 1, 1)
        total = row_sum(jnp.where(gain_holders(owners, span), spread, 0.0))
        if place < 4:
            gain_d[place : place + 1, :] = total
        else:
            gain_h[place - 4 : place - 3, :] = total
    unit, _ = unit_of(tokens[...].astype(F32))
    normed = (unit * gain_d[0:1, :]).astype(BF16)
    rows_a[...] = dot(normed, permutation(columns_a)).astype(BF16)
    rows_b[...] = dot(normed, permutation(columns_b)).astype(BF16)
    cos_rows, sin_rows = cos[...], sin[...]
    for head in range(HEADS):
        raw = packed_product(rows_a, mine_a, other_a, head * HD, QW, head, HD)
        at = pl.ds(head * HD, HD)
        query_raw[:, at] = raw
        normed_raw = unit_of(raw)[0] * gain_h[0:1, :]
        query_low[:, at] = (rotate(normed_raw, cos_rows, sin_rows) * HD**-0.5).astype(BF16)
    kv = [
        packed_product(rows_b, mine_b, other_b, c * LANES, 2 * HD, c, LANES) for c in range(4)
    ]
    raw = jnp.concatenate(kv[:2], axis=1)
    key_raw[...] = raw
    kv_low[:, :HD] = rotate(unit_of(raw)[0] * gain_h[1:2, :], cos_rows, sin_rows).astype(BF16)
    kv_low[:, HD:] = jnp.concatenate(kv[2:], axis=1).astype(BF16)


def allowed_pairs(block_index, positions):
    query_index = block_index * BLK + lax.broadcasted_iota(jnp.int32, (BLK, SPAN), 0)
    key_index = (block_index - BACK) * BLK + lax.broadcasted_iota(jnp.int32, (BLK, SPAN), 1)
    return (
        (key_index <= query_index)
        & (key_index > query_index - WIN)
        & (key_index >= query_index - positions[...])
    )


def attend_kernel(
    where, tokens, positions, gain_d, columns_a, columns_b, mine_b, other_b, query_low, kv_two,
    kv_one, kv_low, heads_out, log_total, attn_proj, middle, rows_a, rows_b, out_w, kv_all,
):
    for place, block in enumerate((kv_two, kv_one, kv_low)):
        kv_all[place * BLK : (place + 1) * BLK, :] = block[...]
    place_groups(out_w, where[0], SLOTS_B, mine_b, other_b, 0, (0, 1), 2)
    allowed = allowed_pairs(where[1], positions)
    for head in range(HEADS):
        at = pl.ds(head * HD, HD)
        scores = dot(query_low[:, at], kv_all[:, :HD], 1, 1)
        scores = jnp.where(allowed, scores, lowest)
        row_max = jnp.max(scores, axis=-1, keepdims=True)
        expo = jnp.exp(scores - row_max)
        total = jnp.sum(expo, axis=-1, keepdims=True)
        log_total[:, column(head)] = jnp.broadcast_to(row_max + jnp.log(total), (BLK, LANES))
        probs = (expo * (1.0 / total)).astype(BF16)
        heads_out[:, at] = dot(probs, kv_all[:, HD:]).astype(BF16)
    proj = dot(heads_out[...], out_w[...])
    attn_proj[...] = proj
    mid = tokens[...].astype(F32) + unit_of(proj)[0] * gain_d[1:2, :]
    middle[...] = mid
    normed = (unit_of(mid)[0] * gain_d[2:3, :]).astype(BF16)
    rows_a[...] = dot(normed, permutation(columns_a)).astype(BF16)
    rows_b[...] = dot(normed, permutation(columns_b)).astype(BF16)


TILE = 256
TILES = FF // TILE
TANH_SCALE = float(np.sqrt(2.0 / np.pi))


def ffn_pieces_in(pieces, weights, sems, spans):
    copies = [
        [
            pltpu.make_async_copy(
                piece.at[:, pl.ds(*span)],
                weights[at // 4].at[pl.ds(at % 4 * (DEPTH // 4), DEPTH // 4), pl.ds(*span)],
                sems.at[8 * place + at],
            )
            for at, piece in enumerate(pieces)
        ]
        for place, span in enumerate(spans)
    ]
    for group in copies:
        for copy in group:
            copy.start()
    return copies


def halves(weights):
    return weights.at[pl.ds(0, HALF)], weights.at[pl.ds(HALF, HALF)]


def ffn_kernel(
    where, middle, cotangent, gain_d, rows_a, rows_b, a_0, a_1, a_2, a_3, b_0, b_1, b_2, b_3,
    layer_out, gain_grad, keep_a_out, send_a_out, keep_b_out, send_b_out, gate_out, up_out,
    keep_a, send_a, keep_b, send_b, gate_g, up_g, weights_a, weights_b, down_w, down_grad, active_s, slope_s, hidden_s, rows_at, rows_bt, sems,
):
    me = where[0]
    down_at = FF + FF // 4
    spans = ((FF, FF // 4), (0, FF // 2), (FF // 2, FF // 2), (down_at, 2 * D))
    tail_in, first_in, second_in, down_in = ffn_pieces_in(
        (a_0, a_1, a_2, a_3, b_0, b_1, b_2, b_3), (weights_a, weights_b), sems, spans
    )
    rows_at[...] = rows_a[...].T
    rows_bt[...] = rows_b[...].T
    leaving = []

    def leave(at, width, pairs):
        for source, target in pairs:
            cols = pl.ds(at, width)
            copy = pltpu.make_async_copy(
                source.at[:, cols], target.at[:, cols], sems.at[32 + len(leaving)]
            )
            copy.start()
            leaving.append(copy)

    sums = ((send_a, send_a_out), (send_b, send_b_out), (keep_a, keep_a_out), (keep_b, keep_b_out))
    mine_a, other_a = halves(weights_a)
    mine_b, other_b = halves(weights_b)

    def forward(tile):
        at = pl.multiple_of(tile * TILE, TILE)
        tail_at = pl.multiple_of(FF + tile % 2 * TILE, TILE)
        gate = packed_product(rows_a, mine_a, other_a, at, tail_at, tile // 2, TILE)
        up = packed_product(rows_b, mine_b, other_b, at, tail_at, tile // 2, TILE)
        cols = pl.ds(at, TILE)
        square = gate * gate
        tanh = jnp.tanh(TANH_SCALE * (gate + 0.044715 * gate * square))
        active = 0.5 * gate * (1.0 + tanh)
        slope = 0.5 * (1.0 + tanh) + 0.5 * gate * (1.0 - tanh * tanh) * TANH_SCALE * (
            1.0 + 3.0 * 0.044715 * square
        )
        active_s[:, cols] = active
        slope_s[:, cols] = up * slope
        hidden_s[:, cols] = (active * up).astype(BF16)

    for copy in tail_in + first_in:
        copy.wait()
    pl.loop(0, TILES // 2, unroll=True)(forward)
    for copy in second_in:
        copy.wait()
    pl.loop(TILES // 2, TILES, unroll=True)(forward)
    for copy in down_in:
        copy.wait()
    place_groups(down_w, me, SLOTS_A, mine_a, other_a, down_at, (0, 1), 4)
    place_groups(down_w, me, SLOTS_B, mine_b, other_b, down_at, (2, 3), 4)
    proj = dot(hidden_s[...], down_w[...])
    unit, inverse = unit_of(proj)
    layer_out[...] = (middle[...] + unit * gain_d[3:4, :]).astype(BF16)
    out_grad = cotangent[...].astype(F32)
    gain_grad[0:1, :] = row_sum(out_grad * unit)
    proj_grad = rms_values_grad(out_grad, unit, inverse, gain_d[3:4, :]).astype(BF16)

    for tile in range(TILES):
        at = tile * TILE
        cols = pl.ds(at, TILE)
        hidden_grad = dot(proj_grad, down_w[cols, :], 1, 1)
        down_grad[cols, :] = dot(hidden_s[:, cols], proj_grad, 0, 0).astype(BF16)
        gate_grad = (hidden_grad * slope_s[:, cols]).astype(BF16)
        up_grad = (hidden_grad * active_s[:, cols]).astype(BF16)
        gate_g[:, cols] = gate_grad
        up_g[:, cols] = up_grad
        packed_grad(rows_at[:DEPTH, :], gate_grad, keep_a, send_a, at)
        packed_grad(rows_bt[:DEPTH, :], up_grad, keep_b, send_b, at)
        if tile % 2:
            leave(at - TILE, 2 * TILE, sums + ((gate_g, gate_out), (up_g, up_out)))

    width = FF // 4
    for rows_t, grad_s, keep, send in (
        (rows_at, gate_g, keep_a, send_a),
        (rows_bt, up_g, keep_b, send_b),
    ):
        tail_grad = jnp.zeros((DEPTH, width), F32)
        for quarter in range(4):
            part = grad_s[:, pl.ds(quarter * width, width)]
            tail_grad += dot(quarter_rows_t(rows_t[DEPTH:, :], quarter), part)
        keep[:, pl.ds(FF, width)] = tail_grad[:HALF].astype(BF16)
        send[:, pl.ds(FF, width)] = tail_grad[HALF:].astype(BF16)
    leave(FF, width, sums)
    take_groups(down_grad, me, SLOTS_A, keep_a, send_a, down_at, (0, 1), 4)
    take_groups(down_grad, me, SLOTS_B, keep_b, send_b, down_at, (2, 3), 4)
    leave(down_at, 2 * D, sums)
    for copy in leaving:
        copy.wait()


def ffn_back_kernel(
    middle, cotangent, gain_d, columns_a, columns_b, gate_in, up_in, a_0, a_1, a_2, a_3, b_0, b_1,
    b_2, b_3, mid_grad, gain_grad, gate_g, up_g, weights_a, weights_b, sems,
):
    (copies,) = ffn_pieces_in(
        (a_0, a_1, a_2, a_3, b_0, b_1, b_2, b_3),
        (weights_a, weights_b),
        sems,
        ((0, FF + FF // 4),),
    )
    grads_in = [
        pltpu.make_async_copy(gate_in, gate_g, sems.at[8]),
        pltpu.make_async_copy(up_in, up_g, sems.at[9]),
    ]
    for copy in grads_in:
        copy.start()
    for copy in grads_in:
        copy.wait()
    width = FF // 4
    normed_grad = jnp.zeros((BLK, D), F32)
    for at, grad_s, weights, columns in ((0, gate_g, weights_a, columns_a), (4, up_g, weights_b, columns_b)):
        for copy in copies[at : at + 4]:
            copy.wait()
        tail_back = jnp.zeros((BLK, DEPTH), F32)
        for quarter in range(4):
            part = grad_s[:, pl.ds(quarter * width, width)]
            tail_back += quarter_rows(dot(part, weights[:, pl.ds(FF, width)], 1, 1), quarter)
        back = jnp.concatenate([dot(grad_s[...], weights[:, :FF], 1, 1), tail_back], axis=1)
        normed_grad += natural_columns(back, permutation(columns))
    unit, inverse = unit_of(middle[...])
    gain_grad[0:1, :] = row_sum(normed_grad * unit)
    mid_grad[...] = cotangent[...].astype(F32) + rms_values_grad(
        normed_grad, unit, inverse, gain_d[2:3, :]
    )


def attend_back_kernel(
    where, mid_grad, attn_proj, positions, gain_d, gain_h, out_w, heads_out, query_low, kv_all,
    log_total, query_raw, cos, sin, rows_a, mine_a, other_a,
    kv_earlier, kv_own, query_keep, query_send, out_keep, out_send, back_a, gain_grad_d,
    gain_grad_h, out_grad_s, kv_grad, query_grad_s, rows_t,
):
    incoming = mid_grad[...]
    unit, inverse = unit_of(attn_proj[...])
    gain_grad_d[0:1, :] = row_sum(incoming * unit)
    proj_grad = rms_values_grad(incoming, unit, inverse, gain_d[1:2, :]).astype(BF16)
    for head in range(HEADS):
        at = pl.ds(head * HD, HD)
        out_grad_s[at, :] = dot(heads_out[:, at], proj_grad, 0, 0).astype(BF16)
    take_groups(out_grad_s, where[0], SLOTS_B, out_keep, out_send, 0, (0, 1), 2)
    allowed = allowed_pairs(where[1], positions)
    cos_rows, sin_rows = cos[...], sin[...]
    rows_t[...] = rows_a[...].T
    total_a = jnp.zeros((BLK, 2 * DEPTH), F32)
    gain_total = jnp.zeros((1, HD), F32)
    keys_grad = jnp.zeros((SPAN, HD), F32)
    values_grad = jnp.zeros((SPAN, HD), F32)
    for head in range(HEADS):
        at = pl.ds(head * HD, HD)
        heads_grad = dot(proj_grad, out_w[at, :], 1, 1).astype(BF16)
        scores = dot(query_low[:, at], kv_all[:, :HD], 1, 1)
        log_rows = log_total[:, pl.ds(head * LANES, 1)]
        probs = jnp.where(allowed, jnp.exp(jnp.where(allowed, scores - log_rows, 0.0)), 0.0)
        prob_grad = dot(heads_grad, kv_all[:, HD:], 1, 1)
        delta = jnp.sum(probs * prob_grad, axis=-1, keepdims=True)
        score_grad = (probs * (prob_grad - delta)).astype(BF16)
        keys_grad += dot(score_grad, query_low[:, at], 0, 0)
        values_grad += dot(probs.astype(BF16), heads_grad, 0, 0)
        query_grad = dot(score_grad, kv_all[:, :HD]) * HD**-0.5
        query_rot = rotate(query_grad, cos_rows, -sin_rows)
        unit, inverse = unit_of(query_raw[:, at])
        gain_total += row_sum(query_rot * unit)
        raw_grad = rms_values_grad(query_rot, unit, inverse, gain_h[0:1, :]).astype(BF16)
        query_grad_s[:, at] = raw_grad
        total_a += packed_back(raw_grad, mine_a, other_a, head * HD, QW, head)
        packed_grad(rows_t[:DEPTH, :], raw_grad, query_keep, query_send, head * HD)
    gain_grad_h[0:1, :] = gain_total
    kv_grad[:, :HD] = keys_grad
    kv_grad[:, HD:] = values_grad
    kv_earlier[...] = kv_grad[: BACK * BLK, :].astype(BF16)
    kv_own[...] = kv_grad[BACK * BLK :, :]
    back_a[...] = total_a
    tail = jnp.zeros((DEPTH, HD), F32)
    for head in range(HEADS):
        tail += dot(
            quarter_rows_t(rows_t[DEPTH:, :], head), query_grad_s[:, pl.ds(head * HD, HD)]
        )
    query_keep[:, pl.ds(QW, HD)] = tail[:HALF].astype(BF16)
    query_send[:, pl.ds(QW, HD)] = tail[HALF:].astype(BF16)


def input_kernel(
    tokens, mid_grad, gain_d, gain_h, columns_a, columns_b, rows_b, mine_b, other_b, kv_own, came_one,
    came_two, key_raw, cos, sin, back_a, owners, fold, out_gg, ffn_out_gg, ffn_in_gg, query_gg,
    input_grad, kv_keep, kv_send, rows_t,
):
    total = kv_own[...] + came_one[...].astype(F32) + came_two[...].astype(F32)
    key_rot = rotate(total[:, :HD], cos[...], -sin[...])
    unit, inverse = unit_of(key_raw[...])
    key_gg = row_sum(key_rot * unit)
    key_grad = rms_values_grad(key_rot, unit, inverse, gain_h[1:2, :]).astype(BF16)
    raw_grad = jnp.concatenate([key_grad, total[:, HD:].astype(BF16)], axis=1)
    rows_t[...] = rows_b[...].T
    back_b = jnp.zeros((BLK, 2 * DEPTH), F32)
    tail = jnp.zeros((DEPTH, LANES), F32)
    for c in range(4):
        part = raw_grad[:, c * LANES : (c + 1) * LANES]
        back_b += packed_back(part, mine_b, other_b, c * LANES, 2 * HD, c)
        tail += dot(quarter_rows_t(rows_t[DEPTH:, :], c), part)
    packed_grad(rows_t[:DEPTH, :], raw_grad, kv_keep, kv_send, 0)
    kv_keep[:, pl.ds(2 * HD, LANES)] = tail[:HALF].astype(BF16)
    kv_send[:, pl.ds(2 * HD, LANES)] = tail[HALF:].astype(BF16)
    normed_grad = natural_columns(back_a[...], permutation(columns_a)) + natural_columns(
        back_b, permutation(columns_b)
    )
    unit, inverse = unit_of(tokens[...].astype(F32))
    in_gg = row_sum(normed_grad * unit)
    gain_grads = (in_gg, out_gg[...], ffn_in_gg[...], ffn_out_gg[...], query_gg[...], key_gg)
    gain_rows = jnp.zeros((PARTS, LANES), F32)
    for grad, span in zip(gain_grads, GAIN_SPANS):
        held = jnp.where(gain_holders(owners, span), grad, 0.0).astype(BF16)
        gain_rows += dot(held, fold[span[0] : span[0] + span[1], :])
    gain_rows = dot(slot_first_rows(), gain_rows.astype(BF16), 0, 0).astype(BF16)
    gain_at = pl.ds(2 * HD + LANES, LANES)
    kv_keep[:, gain_at] = gain_rows[:HALF]
    kv_send[:, gain_at] = gain_rows[HALF:]
    input_grad[...] = mid_grad[...] + rms_values_grad(
        normed_grad, unit, inverse, gain_d[0:1, :]
    )


def call(kernel, outs, args, scratch=(), scalars=0, left=0, outs_left=0, sems=0, windows=(), flops=1e6, limit=56):
    vmem = pl.BlockSpec(memory_space=pltpu.VMEM)
    stays = pl.BlockSpec(memory_space=pl.ANY)
    shapes = [jax.ShapeDtypeStruct(shape, kind) for shape, kind in outs]
    places = [pl.BlockSpec(memory_space=pltpu.SMEM)] * scalars
    places += [vmem] * (len(args) - scalars - left) + [stays] * left
    for at, width, block in windows:
        rows = args[at].shape[0]
        places[at] = pl.BlockSpec((rows, width), functools.partial(lambda block, step: (0, block), block))
    buffers = [pltpu.VMEM(shape, kind) for shape, kind in scratch]
    if sems:
        buffers.append(pltpu.SemaphoreType.DMA((sems,)))
    return pl.pallas_call(
        kernel,
        out_shape=shapes,
        grid=(1,) if windows else (),
        in_specs=places,
        out_specs=[vmem] * (len(outs) - outs_left) + [stays] * outs_left,
        scratch_shapes=buffers,
        compiler_params=pltpu.CompilerParams(vmem_limit_bytes=limit * 1024 * 1024),
        cost_estimate=pl.CostEstimate(flops=int(flops), bytes_accessed=0, transcendentals=0),
    )(*args)


def together(*values):
    return lax.optimization_barrier(values)


def shared_part(flat):
    for bit in range(extra_bits()):
        other = exchanged(flat, 1 << bit)
        mine_first = (lax.axis_index(AXES) >> bit) & 1 == 0
        flat = jnp.where(
            mine_first, jnp.concatenate([flat, other]), jnp.concatenate([other, flat])
        )
    return flat


def own_part(flat):
    for bit in reversed(range(extra_bits())):
        halves = jnp.split(flat, 2)
        mine_first = (lax.axis_index(AXES) >> bit) & 1 == 0
        keep = jnp.where(mine_first, halves[0], halves[1])
        send = jnp.where(mine_first, halves[1], halves[0]).astype(BF16)
        flat = keep + exchanged(send, 1 << bit).astype(F32)
    return flat


def pieces_z(piece):
    return [piece] + [exchanged_part(piece, k << Z_BITS[0]) for k in range(1, 4)]


def stacked(*pieces):
    return jnp.concatenate(pieces, axis=0)


def added(keep, came):
    return keep.astype(F32) + came.astype(F32)


def halved(total):
    half = total.shape[0] // 2
    return total[:half].astype(BF16), total[half:].astype(BF16)


def sent_z(total, k):
    return exchanged_part(total[k * MAIN : (k + 1) * MAIN].astype(BF16), k << Z_BITS[0])


def gathered_columns(slots, me):
    first = (jnp.asarray(slots) ^ me)[:, None] * (D // PARTS)
    inner = jnp.arange(MAIN, dtype=jnp.int32)[None, :]
    return jnp.concatenate([(first + inner).reshape(-1), (first + MAIN + inner % 4).reshape(-1)])[
        None, :
    ]


def local(
    tokens, positions, cotangent, w_query, w_key, w_value, w_out, w_gate, w_up, w_down, gains
):
    me = lax.axis_index(AXES) >> extra_bits()
    block_index = lax.axis_index("seq")
    where = jnp.stack([me, block_index]).astype(jnp.int32)
    parts = [
        shared_part(w).reshape(-1, LANES)
        for w in (w_query, w_key, w_value, w_out, w_gate, w_up, w_down)
    ]
    gain_part = shared_part(gains)
    gain_each = gain_part.shape[0]
    attn, ffn = call(
        pack_kernel,
        [((MAIN, ATTN_A + ATTN_B), BF16), ((MAIN, 2 * FFN_A), BF16)],
        parts + [gain_part[None, :]],
        [((320, LANES), F32), ((MAIN, FF // 4), F32)],
    )
    columns_a = gathered_columns(SLOTS_A, me)
    columns_b = gathered_columns(SLOTS_B, me)
    owners_a = (jnp.asarray(SLOTS_A) ^ me)[:, None]
    owners_b = (jnp.asarray(SLOTS_B) ^ me)[:, None]
    fold = gain_fold()

    freq_table = 10000.0 ** (-2.0 * jnp.arange(HD // 2, dtype=F32) / HD)
    angle_rows = positions.astype(F32)[:, None] * freq_table[None, :]
    cos_rows = jnp.cos(angle_rows)
    sin_rows = jnp.sin(angle_rows)
    places = positions[:, None]
    small = (where, places, cos_rows, sin_rows, columns_a, columns_b, owners_a, owners_b)
    pieces, ffn, small = together(pieces_z(attn), ffn, small)
    where, places, cos_rows, sin_rows, columns_a, columns_b, owners_a, owners_b = small
    attn_z = stacked(*pieces)
    attn_a, attn_b = attn_z[:, :ATTN_A], attn_z[:, ATTN_A:]
    ffn_two = exchanged_part(ffn, 2 << Z_BITS[0])
    next_a, next_b = exchanged_part(attn_a, 1 << ORDER_A[0]), exchanged_part(attn_b, 1 << ORDER_B[0])
    attn_a, attn_b = stacked(attn_a, next_a), stacked(attn_b, next_b)
    ffn_one = exchanged_part(ffn, 1 << Z_BITS[0])
    ffn_three = exchanged_part(ffn, 3 << Z_BITS[0])
    next_a, next_b = exchanged_part(attn_a, 1 << ORDER_A[1]), exchanged_part(attn_b, 1 << ORDER_B[1])
    attn_a, attn_b = stacked(attn_a, next_a), stacked(attn_b, next_b)
    other_a = exchanged_part(attn_a, 1 << CORE)
    other_b = exchanged_part(attn_b, 1 << CORE)
    ffn_z = stacked(ffn, ffn_one, ffn_two, ffn_three)
    ffn_a, ffn_b = ffn_z[:, :FFN_A], ffn_z[:, FFN_A:]
    next_a, next_b = exchanged_part(ffn_a, 1 << ORDER_A[0]), exchanged_part(ffn_b, 1 << ORDER_B[0])

    rows = (BLK, 2 * DEPTH)
    query_low, kv_low, query_raw, key_raw, one_a, one_b, gain_d, gain_h = call(
        qkv_kernel,
        [
            ((BLK, QW), BF16),
            ((BLK, 2 * HD), BF16),
            ((BLK, QW), F32),
            ((BLK, HD), F32),
            (rows, BF16),
            (rows, BF16),
            ((4, D), F32),
            ((2, HD), F32),
        ],
        [tokens, owners_a, fold, columns_a, columns_b, attn_a, other_a, attn_b, other_b]
        + [cos_rows, sin_rows],
        windows=[(7, KV_WIDTH, 2), (8, KV_WIDTH, 2)],
        flops=9e9,
    )
    ffn_a, ffn_b = stacked(ffn_a, next_a), stacked(ffn_b, next_b)
    earlier = [passed_along(kv_low, "seq", back_step) for back_step in range(BACK, 0, -1)]
    heads_out, log_total, attn_proj, middle, two_a, two_b, out_w, kv_all = call(
        attend_kernel,
        [
            ((BLK, QW), BF16),
            ((BLK, HEADS * LANES), F32),
            ((BLK, D), F32),
            ((BLK, D), F32),
            (rows, BF16),
            (rows, BF16),
            ((QW, D), BF16),
            ((SPAN, 2 * HD), BF16),
        ],
        [where, tokens, places, gain_d, columns_a, columns_b, attn_b, other_b, query_low]
        + earlier
        + [kv_low],
        windows=[(6, 2 * D, 0), (7, 2 * D, 0)],
        scalars=1,
        flops=9e9,
    )
    next_a, next_b = exchanged_part(ffn_a, 1 << ORDER_A[1]), exchanged_part(ffn_b, 1 << ORDER_B[1])
    other_ffn_a, other_ffn_b = exchanged_part(ffn_a, 1 << CORE), exchanged_part(ffn_b, 1 << CORE)
    ffn_all = [ffn_a, next_a, other_ffn_a, exchanged_part(next_a, 1 << CORE)]
    ffn_all += [ffn_b, next_b, other_ffn_b, exchanged_part(next_b, 1 << CORE)]
    packed = ((HALF, FFN_A), BF16)
    whole = ((DEPTH, FFN_A), BF16)
    gate_up = ((DEPTH, FF + FF // 4), BF16)
    wide = ((BLK, FF), BF16)
    layer_out, ffn_out_gg, keep_a, send_a, keep_b, send_b, gate_g, up_g = call(
        ffn_kernel,
        [((BLK, D), BF16), ((1, D), F32), packed, packed, packed, packed, wide, wide],
        [where, middle, cotangent, gain_d, two_a, two_b] + ffn_all,
        [
            packed,
            packed,
            packed,
            packed,
            wide,
            wide,
            whole,
            whole,
            ((FF, D), BF16),
            ((FF, D), BF16),
            ((BLK, FF), F32),
            ((BLK, FF), F32),
            wide,
            ((2 * DEPTH, BLK), BF16),
            ((2 * DEPTH, BLK), BF16),
        ],
        scalars=1,
        left=8,
        outs_left=6,
        sems=32 + 34,
    )
    mid_grad, ffn_in_gg = call(
        ffn_back_kernel,
        [((BLK, D), F32), ((1, D), F32)],
        [middle, cotangent, gain_d, columns_a, columns_b, gate_g, up_g] + ffn_all,
        [wide, wide, gate_up, gate_up],
        left=10,
        sems=10,
    )
    came_a, came_b = exchanged_part(send_a, 1 << CORE), exchanged_part(send_b, 1 << CORE)
    mid_grad, came_a, came_b = together(mid_grad, came_a, came_b)
    keep_a, send_a = halved(added(keep_a, came_a))
    keep_b, send_b = halved(added(keep_b, came_b))
    cut = FF + FF // 4
    came_a = exchanged_part(send_a[:, :cut], 1 << ORDER_A[1])
    came_b = exchanged_part(send_b[:, :cut], 1 << ORDER_B[1])
    sixteen = ((HALF, QW + QW // 4), BF16)
    (
        kv_earlier,
        kv_own,
        query_keep,
        query_send,
        out_keep,
        out_send,
        back_a,
        attn_out_gg,
        query_gg,
    ) = call(
        attend_back_kernel,
        [
            ((BACK * BLK, 2 * HD), BF16),
            ((BLK, 2 * HD), F32),
            sixteen,
            sixteen,
            sixteen,
            sixteen,
            (rows, F32),
            ((1, D), F32),
            ((1, HD), F32),
        ],
        [where, mid_grad, attn_proj, places, gain_d, gain_h, out_w, heads_out, query_low]
        + [kv_all, log_total, query_raw, cos_rows, sin_rows, one_a, attn_a, other_a],
        [((QW, D), BF16), ((SPAN, 2 * HD), F32), ((BLK, QW), BF16), ((2 * DEPTH, BLK), BF16)],
        windows=[(15, QW + QW // 4, 0), (16, QW + QW // 4, 0)],
        scalars=1,
        flops=7e9,
    )
    kv_earlier, query_send, out_send, came_a, came_b = together(
        kv_earlier, query_send, out_send, came_a, came_b
    )
    came_a = [came_a, exchanged_part(send_a[:, cut:], 1 << ORDER_A[1])]
    came_b = [came_b, exchanged_part(send_b[:, cut:], 1 << ORDER_B[1])]
    came = [
        passed_along(kv_earlier[(BACK - step) * BLK : (BACK - step + 1) * BLK], "seq", -step)
        for step in range(1, BACK + 1)
    ]
    keep_a, send_a = halved(added(keep_a, jnp.concatenate(came_a, axis=1)))
    keep_b, send_b = halved(added(keep_b, jnp.concatenate(came_b, axis=1)))
    came_a = exchanged_part(send_a, 1 << ORDER_A[0])
    came_b = exchanged_part(send_b, 1 << ORDER_B[0])
    came_query = exchanged_part(query_send, 1 << CORE)
    came_out = exchanged_part(out_send, 1 << CORE)
    ffn_total = jnp.concatenate([added(keep_a, came_a), added(keep_b, came_b)], axis=1)
    query_keep, query_send = halved(added(query_keep, came_query))
    came_query = exchanged_part(query_send, 1 << ORDER_A[1])
    kv_width = KV_WIDTH + LANES
    input_grad, kv_keep, kv_send = call(
        input_kernel,
        [((BLK, D), F32), ((HALF, kv_width), BF16), ((HALF, kv_width), BF16)],
        [tokens, mid_grad, gain_d, gain_h, columns_a, columns_b, one_b, attn_b, other_b, kv_own]
        + came
        + [key_raw, cos_rows, sin_rows, back_a, owners_b, fold]
        + [attn_out_gg, ffn_out_gg, ffn_in_gg, query_gg],
        [((2 * DEPTH, BLK), BF16)],
        windows=[(7, KV_WIDTH, 2), (8, KV_WIDTH, 2)],
        flops=5e9,
    )
    came_kv = exchanged_part(kv_send, 1 << CORE)
    ffn_then, _ = together(ffn_total, came_kv)
    ffn_came = [sent_z(ffn_then, k) for k in range(1, 4)]
    rest_keep, rest_send = halved(
        jnp.concatenate([added(out_keep, came_out), added(kv_keep, came_kv)], axis=1)
    )
    query_keep, query_send = halved(added(query_keep, came_query))
    came_query = exchanged_part(query_send, 1 << ORDER_A[0])
    came_rest = exchanged_part(rest_send, 1 << ORDER_B[1])
    rest_keep, rest_send = halved(added(rest_keep, came_rest))
    came_rest = exchanged_part(rest_send, 1 << ORDER_B[0])
    ffn_came, _ = together(ffn_came, came_rest)
    attn_total = jnp.concatenate(
        [added(query_keep, came_query), added(rest_keep, came_rest)], axis=1
    )
    attn_came = [sent_z(attn_total, k) for k in range(1, 4)]
    flat = [((160, LANES), F32), ((40, LANES), F32), ((320, LANES), F32)]
    grad_gate, grad_up, grad_down = call(
        unpack_ffn_kernel,
        [flat[2]] * 3,
        [ffn_total[:MAIN]] + ffn_came,
        [((MAIN, 2 * FFN_A), F32)],
        limit=16,
    )
    grad_query, grad_key, grad_value, grad_out, grad_gains = call(
        unpack_attn_kernel,
        [flat[0], flat[1], flat[1], flat[0], ((1, GAIN_EACH), F32)],
        [attn_total[:MAIN]] + attn_came,
        [((MAIN, attn_total.shape[1]), F32)],
        limit=16,
    )
    return (
        layer_out,
        input_grad,
        *(
            own_part(grad.reshape(-1))
            for grad in (
                grad_query,
                grad_key,
                grad_value,
                grad_out,
                grad_gate,
                grad_up,
                grad_down,
                grad_gains,
            )
        ),
    )


def solution(mesh):
    rows = P(AXES, None)
    flat = P(AXES)
    return jax.shard_map(
        local,
        mesh=mesh,
        in_specs=(rows, flat, rows) + (flat,) * 8,
        out_specs=(rows, rows) + (flat,) * 8,
        check_vma=False,
    )
```

```python
import functools
import numpy as np
import jax
import jax.numpy as jnp
from jax import lax
from jax.experimental import pallas as pl
from jax.experimental.pallas import tpu as pltpu
from jax.sharding import PartitionSpec as P

D = 640
HEADS = 4
HD = 256
FF = 2048
WIN = 512
BLK = 256
BACK = 2
AXES = ("dp", "seq")
F32 = jnp.float32
BF16 = jnp.bfloat16
QW = HEADS * HD
SPAN = (BACK + 1) * BLK

PARTS = 32
MAIN = 16
DEPTH = PARTS * MAIN
HALF = DEPTH // 2
KV_WIDTH = 2 * HD + HD // 2
LANES = 128
ATTN_A = QW + QW // 4 + LANES
ATTN_B = 2 * HD + HD // 2 + 2 * D
FFN_A = FF + FF // 4 + 2 * D
Z_BITS = (1, 2)
LOW, CORE, HIGH = 0, 3, 4
ORDER_A = (LOW, HIGH, CORE)
ORDER_B = (HIGH, LOW, CORE)

GAIN_SPANS = tuple((i * D, D) for i in range(4)) + ((4 * D, HD), (4 * D + HD, HD))
GAINS = 4 * D + 2 * HD
GAIN_EACH = GAINS // PARTS

epsilon = 1e-06
lowest = -1e30


def slot_shards(order):
    shards = np.arange(4, dtype=np.int32) << Z_BITS[0]
    for bit in order:
        shards = np.concatenate([shards, shards ^ (1 << bit)])
    return shards


SLOTS_A = slot_shards(ORDER_A)
SLOTS_B = slot_shards(ORDER_B)


def extra_bits():
    return (lax.axis_size("dp") * lax.axis_size("seq")).bit_length() - PARTS.bit_length()


def exchanged(value, mask):
    count = lax.axis_size("dp") * lax.axis_size("seq")
    return lax.ppermute(value, AXES, [(i, i ^ mask) for i in range(count)])


def exchanged_part(value, mask):
    return exchanged(value, mask << extra_bits())


def passed_along(value, axis, steps):
    count = lax.axis_size(axis)
    first, last = (max(0, -steps), min(count, count - steps))
    return lax.ppermute(value, axis, [(source, source + steps) for source in range(first, last)])


def dot(left, right, left_dim=1, right_dim=0):
    return lax.dot_general(
        left, right, (((left_dim,), (right_dim,)), ((), ())), preferred_element_type=F32
    )


def unit_of(values):
    inverse = lax.rsqrt(jnp.mean(values * values, axis=-1, keepdims=True) + epsilon)
    return values * inverse, inverse


def rms_values_grad(incoming, unit_rows, inverse, gain_row):
    scaled = incoming * gain_row
    return inverse * (scaled - unit_rows * jnp.mean(scaled * unit_rows, axis=-1, keepdims=True))


def rotate(values, cos_rows, sin_rows):
    middle_at = values.shape[-1] // 2
    first_half = values[..., :middle_at]
    second_half = values[..., middle_at:]
    return jnp.concatenate(
        [
            first_half * cos_rows - second_half * sin_rows,
            second_half * cos_rows + first_half * sin_rows,
        ],
        axis=-1,
    )


def row_sum(values):
    return jnp.sum(values, axis=0, keepdims=True)


def column(index):
    return pl.ds(index * LANES, LANES)


def pack_kernel(
    query, key, value, out, gate, up, down, gains, attn, ffn, wide, quarter
):
    def load(source):
        rows = source.shape[0]
        wide[:rows, :] = source[...].astype(F32)

    def put_main(target, at, blocks, block):
        target[:, pl.ds(at, LANES)] = wide[pl.ds(block, MAIN, stride=blocks), :].astype(BF16)

    def put_tail(row, at, blocks, block):
        quarter[4 * row : 4 * row + 4, pl.ds(at, LANES)] = wide[
            pl.ds(MAIN * blocks + block, 4, stride=blocks), :
        ]

    def put_matrix(source, target, at):
        load(source)
        blocks = source.shape[0] // 20
        for block in range(blocks):
            put_main(target, at + block * LANES, blocks, block)
            each = blocks // 4
            put_tail(block // each, block % each * LANES, blocks, block)
        width = blocks * LANES // 4
        target[:, pl.ds(at + blocks * LANES, width)] = quarter[:, :width].astype(BF16)

    def put_groups(target, at, groups):
        blocks = D // LANES
        for place, group in enumerate(groups):
            for block in range(blocks):
                target[:, pl.ds(at + place * D + block * LANES, LANES)] = wide[
                    pl.ds(group * MAIN * blocks + block, MAIN, stride=blocks), :
                ].astype(BF16)

    put_matrix(query, attn, 0)
    attn[:, pl.ds(QW + QW // 4, LANES)] = jnp.zeros((MAIN, LANES), BF16)
    attn[:, pl.ds(QW + QW // 4, GAIN_EACH)] = jnp.broadcast_to(gains[...], (MAIN, GAIN_EACH))
    for place, source in enumerate((key, value)):
        load(source)
        for block in range(2):
            put_main(attn, ATTN_A + 2 * D + place * HD + block * LANES, 2, block)
            put_tail(2 * place + block, 0, 2, block)
    attn[:, pl.ds(ATTN_A + 2 * D + 2 * HD, LANES)] = quarter[:, :LANES].astype(BF16)
    load(out)
    put_groups(attn, ATTN_A, (0, 1))
    put_matrix(gate, ffn, 0)
    put_matrix(up, ffn, FFN_A)
    load(down)
    put_groups(ffn, FF + FF // 4, (0, 1))
    put_groups(ffn, FFN_A + FF + FF // 4, (2, 3))


def unpack_matrix(source, at, target):
    blocks = target.shape[0] // 20
    each = blocks // 4
    tail_at = at + blocks * LANES
    for block in range(blocks):
        target[pl.ds(block, MAIN, stride=blocks), :] = source[:, pl.ds(at + block * LANES, LANES)]
        row = block // each * 4
        target[pl.ds(MAIN * blocks + block, 4, stride=blocks), :] = source[
            row : row + 4, pl.ds(tail_at + block % each * LANES, LANES)
        ]


def unpack_groups(source, at, target, groups):
    blocks = D // LANES
    for place, group in enumerate(groups):
        for block in range(blocks):
            target[pl.ds(group * MAIN * blocks + block, MAIN, stride=blocks), :] = source[
                :, pl.ds(at + place * D + block * LANES, LANES)
            ]


def unpack_ffn_kernel(own, one, two, three, gate, up, down, part):
    part[...] = sum(came[...].astype(F32) for came in (one, two, three)) + own[...]
    unpack_matrix(part, 0, gate)
    unpack_matrix(part, FFN_A, up)
    unpack_groups(part, FF + FF // 4, down, (0, 1))
    unpack_groups(part, FFN_A + FF + FF // 4, down, (2, 3))


def unpack_attn_kernel(own, one, two, three, query, key, value, out, gains, part):
    part[...] = sum(came[...].astype(F32) for came in (one, two, three)) + own[...]
    gains[...] = part[0:1, pl.ds(QW + QW // 4 + 2 * D + KV_WIDTH, GAIN_EACH)]
    unpack_matrix(part, 0, query)
    unpack_groups(part, QW + QW // 4, out, (0, 1))
    kv_at = QW + QW // 4 + 2 * D
    for place, target in enumerate((key, value)):
        for block in range(2):
            target[pl.ds(block, MAIN, stride=2), :] = part[
                :, pl.ds(kv_at + place * HD + block * LANES, LANES)
            ]
            row = 4 * (2 * place + block)
            target[pl.ds(2 * MAIN + block, 4, stride=2), :] = part[
                row : row + 4, pl.ds(kv_at + 2 * HD, LANES)
            ]


def quarter_mask(shape, dim, quarter):
    index = lax.broadcasted_iota(jnp.int32, shape, dim)
    return (index // 4 % 4 == quarter).astype(F32)


def quarter_rows(tail_rows, quarter):
    return tail_rows * quarter_mask((1, DEPTH), 1, quarter).astype(tail_rows.dtype)


def quarter_rows_t(tail_rows, quarter):
    return tail_rows * quarter_mask((DEPTH, 1), 0, quarter).astype(tail_rows.dtype)


def packed_product(rows, mine, other, main_at, tail_at, quarter, width):
    tail = quarter_rows(rows[:, DEPTH:], quarter)
    main_at, tail_at = pl.ds(main_at, width), pl.ds(tail_at, width)
    return (
        dot(rows[:, :HALF], mine[:, main_at])
        + dot(rows[:, HALF:DEPTH], other[:, main_at])
        + dot(tail[:, :HALF], mine[:, tail_at])
        + dot(tail[:, HALF:], other[:, tail_at])
    )


def packed_back(incoming, mine, other, main_at, tail_at, quarter):
    width = incoming.shape[1]
    main_at, tail_at = pl.ds(main_at, width), pl.ds(tail_at, width)
    tail = jnp.concatenate(
        [dot(incoming, mine[:, tail_at], 1, 1), dot(incoming, other[:, tail_at], 1, 1)], axis=1
    )
    return jnp.concatenate(
        [
            dot(incoming, mine[:, main_at], 1, 1),
            dot(incoming, other[:, main_at], 1, 1),
            quarter_rows(tail, quarter),
        ],
        axis=1,
    )


def packed_grad(rows_t, incoming, keep, send, main_at):
    grad = dot(rows_t, incoming).astype(BF16)
    main_at = pl.ds(main_at, incoming.shape[1])
    keep[:, main_at] = grad[:HALF]
    send[:, main_at] = grad[HALF:]


def permutation(columns):
    natural = lax.broadcasted_iota(jnp.int32, (D, 2 * DEPTH), 0)
    return (natural == columns[...]).astype(F32).astype(BF16)


def natural_columns(permuted, permutation):
    return dot(permuted.astype(BF16), permutation, 1, 1)


def place_groups(target, me, slots, mine, other, at, groups, count):
    for slot in range(PARTS):
        source = mine if slot < PARTS // 2 else other
        row = slot % (PARTS // 2) * MAIN
        first = (me ^ int(slots[slot])) * (count * MAIN)
        for place, group in enumerate(groups):
            rows = pl.ds(pl.multiple_of(first + group * MAIN, MAIN), MAIN)
            target[rows, :] = source[row : row + MAIN, pl.ds(at + place * D, D)]


def take_groups(whole, me, slots, keep, send, at, groups, count):
    for slot in range(PARTS):
        target = keep if slot < PARTS // 2 else send
        row = slot % (PARTS // 2) * MAIN
        first = (me ^ int(slots[slot])) * (count * MAIN)
        for place, group in enumerate(groups):
            rows = pl.ds(pl.multiple_of(first + group * MAIN, MAIN), MAIN)
            target[row : row + MAIN, pl.ds(at + place * D, D)] = whole[rows, :]


def gain_fold():
    lane = np.arange(GAINS)[:, None] % GAIN_EACH == np.arange(LANES)[None, :]
    return jnp.asarray(lane, BF16)


def gain_holders(owners, span):
    entry = span[0] + lax.broadcasted_iota(jnp.int32, (PARTS, span[1]), 1)
    first = owners[...] * GAIN_EACH
    return (entry >= first) & (entry < first + GAIN_EACH)


def slot_first_rows():
    row = lax.broadcasted_iota(jnp.int32, (PARTS, DEPTH), 1)
    return (row == MAIN * lax.broadcasted_iota(jnp.int32, (PARTS, DEPTH), 0)).astype(BF16)


def qkv_kernel(
    tokens, owners, fold, columns_a, columns_b, mine_a, other_a, mine_b, other_b, cos, sin,
    query_low, kv_low, query_raw, key_raw, rows_a, rows_b, gain_d, gain_h,
):
    first_rows = slot_first_rows()
    gain_at = pl.ds(QW + QW // 4, LANES)
    gain_rows = (
        dot(first_rows[:, :HALF], mine_a[:, gain_at])
        + dot(first_rows[:, HALF:], other_a[:, gain_at])
    ).astype(BF16)
    for place, span in enumerate(GAIN_SPANS):
        spread = dot(gain_rows, fold[span[0] : span[0] + span[1], :], 1, 1)
        total = row_sum(jnp.where(gain_holders(owners, span), spread, 0.0))
        if place < 4:
            gain_d[place : place + 1, :] = total
        else:
            gain_h[place - 4 : place - 3, :] = total
    unit, _ = unit_of(tokens[...].astype(F32))
    normed = (unit * gain_d[0:1, :]).astype(BF16)
    rows_a[...] = dot(normed, permutation(columns_a)).astype(BF16)
    rows_b[...] = dot(normed, permutation(columns_b)).astype(BF16)
    cos_rows, sin_rows = cos[...], sin[...]
    for head in range(HEADS):
        raw = packed_product(rows_a, mine_a, other_a, head * HD, QW, head, HD)
        at = pl.ds(head * HD, HD)
        query_raw[:, at] = raw
        normed_raw = unit_of(raw)[0] * gain_h[0:1, :]
        query_low[:, at] = (rotate(normed_raw, cos_rows, sin_rows) * HD**-0.5).astype(BF16)
    kv = [
        packed_product(rows_b, mine_b, other_b, c * LANES, 2 * HD, c, LANES) for c in range(4)
    ]
    raw = jnp.concatenate(kv[:2], axis=1)
    key_raw[...] = raw
    kv_low[:, :HD] = rotate(unit_of(raw)[0] * gain_h[1:2, :], cos_rows, sin_rows).astype(BF16)
    kv_low[:, HD:] = jnp.concatenate(kv[2:], axis=1).astype(BF16)


def allowed_pairs(block_index, positions):
    query_index = block_index * BLK + lax.broadcasted_iota(jnp.int32, (BLK, SPAN), 0)
    key_index = (block_index - BACK) * BLK + lax.broadcasted_iota(jnp.int32, (BLK, SPAN), 1)
    return (
        (key_index <= query_index)
        & (key_index > query_index - WIN)
        & (key_index >= query_index - positions[...])
    )


def attend_kernel(
    where, tokens, positions, gain_d, columns_a, columns_b, mine_b, other_b, query_low, kv_two,
    kv_one, kv_low, heads_out, log_total, attn_proj, middle, rows_a, rows_b, out_w, kv_all,
):
    for place, block in enumerate((kv_two, kv_one, kv_low)):
        kv_all[place * BLK : (place + 1) * BLK, :] = block[...]
    place_groups(out_w, where[0], SLOTS_B, mine_b, other_b, 0, (0, 1), 2)
    allowed = allowed_pairs(where[1], positions)
    for head in range(HEADS):
        at = pl.ds(head * HD, HD)
        scores = dot(query_low[:, at], kv_all[:, :HD], 1, 1)
        scores = jnp.where(allowed, scores, lowest)
        row_max = jnp.max(scores, axis=-1, keepdims=True)
        expo = jnp.exp(scores - row_max)
        total = jnp.sum(expo, axis=-1, keepdims=True)
        log_total[:, column(head)] = jnp.broadcast_to(row_max + jnp.log(total), (BLK, LANES))
        probs = (expo * (1.0 / total)).astype(BF16)
        heads_out[:, at] = dot(probs, kv_all[:, HD:]).astype(BF16)
    proj = dot(heads_out[...], out_w[...])
    attn_proj[...] = proj
    mid = tokens[...].astype(F32) + unit_of(proj)[0] * gain_d[1:2, :]
    middle[...] = mid
    normed = (unit_of(mid)[0] * gain_d[2:3, :]).astype(BF16)
    rows_a[...] = dot(normed, permutation(columns_a)).astype(BF16)
    rows_b[...] = dot(normed, permutation(columns_b)).astype(BF16)


TILE = 256
TILES = FF // TILE
TANH_SCALE = float(np.sqrt(2.0 / np.pi))


def ffn_pieces_in(pieces, weights, sems, spans):
    copies = [
        [
            pltpu.make_async_copy(
                piece.at[:, pl.ds(*span)],
                weights[at // 4].at[pl.ds(at % 4 * (DEPTH // 4), DEPTH // 4), pl.ds(*span)],
                sems.at[8 * place + at],
            )
            for at, piece in enumerate(pieces)
        ]
        for place, span in enumerate(spans)
    ]
    for group in copies:
        for copy in group:
            copy.start()
    return copies


def halves(weights):
    return weights.at[pl.ds(0, HALF)], weights.at[pl.ds(HALF, HALF)]


def ffn_kernel(
    where, middle, cotangent, gain_d, rows_a, rows_b, a_0, a_1, a_2, a_3, b_0, b_1, b_2, b_3,
    layer_out, gain_grad, keep_a_out, send_a_out, keep_b_out, send_b_out, gate_out, up_out,
    keep_a, send_a, keep_b, send_b, gate_g, up_g, weights_a, weights_b, down_w, down_grad, active_s, slope_s, hidden_s, rows_at, rows_bt, sems,
):
    me = where[0]
    down_at = FF + FF // 4
    spans = ((FF, FF // 4), (0, FF // 2), (FF // 2, FF // 2), (down_at, 2 * D))
    tail_in, first_in, second_in, down_in = ffn_pieces_in(
        (a_0, a_1, a_2, a_3, b_0, b_1, b_2, b_3), (weights_a, weights_b), sems, spans
    )
    rows_at[...] = rows_a[...].T
    rows_bt[...] = rows_b[...].T
    leaving = []

    def leave(at, width, pairs):
        for source, target in pairs:
            cols = pl.ds(at, width)
            copy = pltpu.make_async_copy(
                source.at[:, cols], target.at[:, cols], sems.at[32 + len(leaving)]
            )
            copy.start()
            leaving.append(copy)

    sums = ((send_a, send_a_out), (send_b, send_b_out), (keep_a, keep_a_out), (keep_b, keep_b_out))
    mine_a, other_a = halves(weights_a)
    mine_b, other_b = halves(weights_b)

    def forward(tile):
        at = pl.multiple_of(tile * TILE, TILE)
        tail_at = pl.multiple_of(FF + tile % 2 * TILE, TILE)
        gate = packed_product(rows_a, mine_a, other_a, at, tail_at, tile // 2, TILE)
        up = packed_product(rows_b, mine_b, other_b, at, tail_at, tile // 2, TILE)
        cols = pl.ds(at, TILE)
        square = gate * gate
        tanh = jnp.tanh(TANH_SCALE * (gate + 0.044715 * gate * square))
        active = 0.5 * gate * (1.0 + tanh)
        slope = 0.5 * (1.0 + tanh) + 0.5 * gate * (1.0 - tanh * tanh) * TANH_SCALE * (
            1.0 + 3.0 * 0.044715 * square
        )
        active_s[:, cols] = active
        slope_s[:, cols] = up * slope
        hidden_s[:, cols] = (active * up).astype(BF16)

    for copy in tail_in + first_in:
        copy.wait()
    pl.loop(0, TILES // 2, unroll=True)(forward)
    for copy in second_in:
        copy.wait()
    pl.loop(TILES // 2, TILES, unroll=True)(forward)
    for copy in down_in:
        copy.wait()
    place_groups(down_w, me, SLOTS_A, mine_a, other_a, down_at, (0, 1), 4)
    place_groups(down_w, me, SLOTS_B, mine_b, other_b, down_at, (2, 3), 4)
    proj = dot(hidden_s[...], down_w[...])
    unit, inverse = unit_of(proj)
    layer_out[...] = (middle[...] + unit * gain_d[3:4, :]).astype(BF16)
    out_grad = cotangent[...].astype(F32)
    gain_grad[0:1, :] = row_sum(out_grad * unit)
    proj_grad = rms_values_grad(out_grad, unit, inverse, gain_d[3:4, :]).astype(BF16)

    for tile in range(TILES):
        at = tile * TILE
        cols = pl.ds(at, TILE)
        hidden_grad = dot(proj_grad, down_w[cols, :], 1, 1)
        down_grad[cols, :] = dot(hidden_s[:, cols], proj_grad, 0, 0).astype(BF16)
        gate_grad = (hidden_grad * slope_s[:, cols]).astype(BF16)
        up_grad = (hidden_grad * active_s[:, cols]).astype(BF16)
        gate_g[:, cols] = gate_grad
        up_g[:, cols] = up_grad
        packed_grad(rows_at[:DEPTH, :], gate_grad, keep_a, send_a, at)
        packed_grad(rows_bt[:DEPTH, :], up_grad, keep_b, send_b, at)
        if tile % 2:
            leave(at - TILE, 2 * TILE, sums + ((gate_g, gate_out), (up_g, up_out)))

    width = FF // 4
    for rows_t, grad_s, keep, send in (
        (rows_at, gate_g, keep_a, send_a),
        (rows_bt, up_g, keep_b, send_b),
    ):
        tail_grad = jnp.zeros((DEPTH, width), F32)
        for quarter in range(4):
            part = grad_s[:, pl.ds(quarter * width, width)]
            tail_grad += dot(quarter_rows_t(rows_t[DEPTH:, :], quarter), part)
        keep[:, pl.ds(FF, width)] = tail_grad[:HALF].astype(BF16)
        send[:, pl.ds(FF, width)] = tail_grad[HALF:].astype(BF16)
    leave(FF, width, sums)
    take_groups(down_grad, me, SLOTS_A, keep_a, send_a, down_at, (0, 1), 4)
    take_groups(down_grad, me, SLOTS_B, keep_b, send_b, down_at, (2, 3), 4)
    leave(down_at, 2 * D, sums)
    for copy in leaving:
        copy.wait()


def ffn_back_kernel(
    middle, cotangent, gain_d, columns_a, columns_b, gate_in, up_in, a_0, a_1, a_2, a_3, b_0, b_1,
    b_2, b_3, mid_grad, gain_grad, gate_g, up_g, weights_a, weights_b, sems,
):
    (copies,) = ffn_pieces_in(
        (a_0, a_1, a_2, a_3, b_0, b_1, b_2, b_3),
        (weights_a, weights_b),
        sems,
        ((0, FF + FF // 4),),
    )
    grads_in = [
        pltpu.make_async_copy(gate_in, gate_g, sems.at[8]),
        pltpu.make_async_copy(up_in, up_g, sems.at[9]),
    ]
    for copy in grads_in:
        copy.start()
    for copy in grads_in:
        copy.wait()
    width = FF // 4
    normed_grad = jnp.zeros((BLK, D), F32)
    for at, grad_s, weights, columns in ((0, gate_g, weights_a, columns_a), (4, up_g, weights_b, columns_b)):
        for copy in copies[at : at + 4]:
            copy.wait()
        tail_back = jnp.zeros((BLK, DEPTH), F32)
        for quarter in range(4):
            part = grad_s[:, pl.ds(quarter * width, width)]
            tail_back += quarter_rows(dot(part, weights[:, pl.ds(FF, width)], 1, 1), quarter)
        back = jnp.concatenate([dot(grad_s[...], weights[:, :FF], 1, 1), tail_back], axis=1)
        normed_grad += natural_columns(back, permutation(columns))
    unit, inverse = unit_of(middle[...])
    gain_grad[0:1, :] = row_sum(normed_grad * unit)
    mid_grad[...] = cotangent[...].astype(F32) + rms_values_grad(
        normed_grad, unit, inverse, gain_d[2:3, :]
    )


def attend_back_kernel(
    where, mid_grad, attn_proj, positions, gain_d, gain_h, out_w, heads_out, query_low, kv_all,
    log_total, query_raw, cos, sin, rows_a, mine_a, other_a,
    kv_earlier, kv_own, query_keep, query_send, out_keep, out_send, back_a, gain_grad_d,
    gain_grad_h, out_grad_s, kv_grad, query_grad_s, rows_t,
):
    incoming = mid_grad[...]
    unit, inverse = unit_of(attn_proj[...])
    gain_grad_d[0:1, :] = row_sum(incoming * unit)
    proj_grad = rms_values_grad(incoming, unit, inverse, gain_d[1:2, :]).astype(BF16)
    for head in range(HEADS):
        at = pl.ds(head * HD, HD)
        out_grad_s[at, :] = dot(heads_out[:, at], proj_grad, 0, 0).astype(BF16)
    take_groups(out_grad_s, where[0], SLOTS_B, out_keep, out_send, 0, (0, 1), 2)
    allowed = allowed_pairs(where[1], positions)
    cos_rows, sin_rows = cos[...], sin[...]
    rows_t[...] = rows_a[...].T
    total_a = jnp.zeros((BLK, 2 * DEPTH), F32)
    gain_total = jnp.zeros((1, HD), F32)
    keys_grad = jnp.zeros((SPAN, HD), F32)
    values_grad = jnp.zeros((SPAN, HD), F32)
    for head in range(HEADS):
        at = pl.ds(head * HD, HD)
        heads_grad = dot(proj_grad, out_w[at, :], 1, 1).astype(BF16)
        scores = dot(query_low[:, at], kv_all[:, :HD], 1, 1)
        log_rows = log_total[:, pl.ds(head * LANES, 1)]
        probs = jnp.where(allowed, jnp.exp(jnp.where(allowed, scores - log_rows, 0.0)), 0.0)
        prob_grad = dot(heads_grad, kv_all[:, HD:], 1, 1)
        delta = jnp.sum(probs * prob_grad, axis=-1, keepdims=True)
        score_grad = (probs * (prob_grad - delta)).astype(BF16)
        keys_grad += dot(score_grad, query_low[:, at], 0, 0)
        values_grad += dot(probs.astype(BF16), heads_grad, 0, 0)
        query_grad = dot(score_grad, kv_all[:, :HD]) * HD**-0.5
        query_rot = rotate(query_grad, cos_rows, -sin_rows)
        unit, inverse = unit_of(query_raw[:, at])
        gain_total += row_sum(query_rot * unit)
        raw_grad = rms_values_grad(query_rot, unit, inverse, gain_h[0:1, :]).astype(BF16)
        query_grad_s[:, at] = raw_grad
        total_a += packed_back(raw_grad, mine_a, other_a, head * HD, QW, head)
        packed_grad(rows_t[:DEPTH, :], raw_grad, query_keep, query_send, head * HD)
    gain_grad_h[0:1, :] = gain_total
    kv_grad[:, :HD] = keys_grad
    kv_grad[:, HD:] = values_grad
    kv_earlier[...] = kv_grad[: BACK * BLK, :].astype(BF16)
    kv_own[...] = kv_grad[BACK * BLK :, :]
    back_a[...] = total_a
    tail = jnp.zeros((DEPTH, HD), F32)
    for head in range(HEADS):
        tail += dot(
            quarter_rows_t(rows_t[DEPTH:, :], head), query_grad_s[:, pl.ds(head * HD, HD)]
        )
    query_keep[:, pl.ds(QW, HD)] = tail[:HALF].astype(BF16)
    query_send[:, pl.ds(QW, HD)] = tail[HALF:].astype(BF16)


def input_kernel(
    tokens, mid_grad, gain_d, gain_h, columns_a, columns_b, rows_b, mine_b, other_b, kv_own, came_one,
    came_two, key_raw, cos, sin, back_a, owners, fold, out_gg, ffn_out_gg, ffn_in_gg, query_gg,
    input_grad, kv_keep, kv_send, rows_t,
):
    total = kv_own[...] + came_one[...].astype(F32) + came_two[...].astype(F32)
    key_rot = rotate(total[:, :HD], cos[...], -sin[...])
    unit, inverse = unit_of(key_raw[...])
    key_gg = row_sum(key_rot * unit)
    key_grad = rms_values_grad(key_rot, unit, inverse, gain_h[1:2, :]).astype(BF16)
    raw_grad = jnp.concatenate([key_grad, total[:, HD:].astype(BF16)], axis=1)
    rows_t[...] = rows_b[...].T
    back_b = jnp.zeros((BLK, 2 * DEPTH), F32)
    tail = jnp.zeros((DEPTH, LANES), F32)
    for c in range(4):
        part = raw_grad[:, c * LANES : (c + 1) * LANES]
        back_b += packed_back(part, mine_b, other_b, c * LANES, 2 * HD, c)
        tail += dot(quarter_rows_t(rows_t[DEPTH:, :], c), part)
    packed_grad(rows_t[:DEPTH, :], raw_grad, kv_keep, kv_send, 0)
    kv_keep[:, pl.ds(2 * HD, LANES)] = tail[:HALF].astype(BF16)
    kv_send[:, pl.ds(2 * HD, LANES)] = tail[HALF:].astype(BF16)
    normed_grad = natural_columns(back_a[...], permutation(columns_a)) + natural_columns(
        back_b, permutation(columns_b)
    )
    unit, inverse = unit_of(tokens[...].astype(F32))
    in_gg = row_sum(normed_grad * unit)
    gain_grads = (in_gg, out_gg[...], ffn_in_gg[...], ffn_out_gg[...], query_gg[...], key_gg)
    gain_rows = jnp.zeros((PARTS, LANES), F32)
    for grad, span in zip(gain_grads, GAIN_SPANS):
        held = jnp.where(gain_holders(owners, span), grad, 0.0).astype(BF16)
        gain_rows += dot(held, fold[span[0] : span[0] + span[1], :])
    gain_rows = dot(slot_first_rows(), gain_rows.astype(BF16), 0, 0).astype(BF16)
    gain_at = pl.ds(2 * HD + LANES, LANES)
    kv_keep[:, gain_at] = gain_rows[:HALF]
    kv_send[:, gain_at] = gain_rows[HALF:]
    input_grad[...] = mid_grad[...] + rms_values_grad(
        normed_grad, unit, inverse, gain_d[0:1, :]
    )


def call(kernel, outs, args, scratch=(), scalars=0, left=0, outs_left=0, sems=0, windows=(), flops=1e6, limit=56):
    vmem = pl.BlockSpec(memory_space=pltpu.VMEM)
    stays = pl.BlockSpec(memory_space=pl.ANY)
    shapes = [jax.ShapeDtypeStruct(shape, kind) for shape, kind in outs]
    places = [pl.BlockSpec(memory_space=pltpu.SMEM)] * scalars
    places += [vmem] * (len(args) - scalars - left) + [stays] * left
    for at, width, block in windows:
        rows = args[at].shape[0]
        places[at] = pl.BlockSpec((rows, width), functools.partial(lambda block, step: (0, block), block))
    buffers = [pltpu.VMEM(shape, kind) for shape, kind in scratch]
    if sems:
        buffers.append(pltpu.SemaphoreType.DMA((sems,)))
    return pl.pallas_call(
        kernel,
        out_shape=shapes,
        grid=(1,) if windows else (),
        in_specs=places,
        out_specs=[vmem] * (len(outs) - outs_left) + [stays] * outs_left,
        scratch_shapes=buffers,
        compiler_params=pltpu.CompilerParams(vmem_limit_bytes=limit * 1024 * 1024),
        cost_estimate=pl.CostEstimate(flops=int(flops), bytes_accessed=0, transcendentals=0),
    )(*args)


def together(*values):
    return lax.optimization_barrier(values)


def shared_part(flat):
    for bit in range(extra_bits()):
        other = exchanged(flat, 1 << bit)
        mine_first = (lax.axis_index(AXES) >> bit) & 1 == 0
        flat = jnp.where(
            mine_first, jnp.concatenate([flat, other]), jnp.concatenate([other, flat])
        )
    return flat


def own_part(flat):
    for bit in reversed(range(extra_bits())):
        halves = jnp.split(flat, 2)
        mine_first = (lax.axis_index(AXES) >> bit) & 1 == 0
        keep = jnp.where(mine_first, halves[0], halves[1])
        send = jnp.where(mine_first, halves[1], halves[0]).astype(BF16)
        flat = keep + exchanged(send, 1 << bit).astype(F32)
    return flat


def pieces_z(piece):
    return [piece] + [exchanged_part(piece, k << Z_BITS[0]) for k in range(1, 4)]


def stacked(*pieces):
    return jnp.concatenate(pieces, axis=0)


def added(keep, came):
    return keep.astype(F32) + came.astype(F32)


def halved(total):
    half = total.shape[0] // 2
    return total[:half].astype(BF16), total[half:].astype(BF16)


def sent_z(total, k):
    return exchanged_part(total[k * MAIN : (k + 1) * MAIN].astype(BF16), k << Z_BITS[0])


def gathered_columns(slots, me):
    first = (jnp.asarray(slots) ^ me)[:, None] * (D // PARTS)
    inner = jnp.arange(MAIN, dtype=jnp.int32)[None, :]
    return jnp.concatenate([(first + inner).reshape(-1), (first + MAIN + inner % 4).reshape(-1)])[
        None, :
    ]


def local(
    tokens, positions, cotangent, w_query, w_key, w_value, w_out, w_gate, w_up, w_down, gains
):
    me = lax.axis_index(AXES) >> extra_bits()
    block_index = lax.axis_index("seq")
    where = jnp.stack([me, block_index]).astype(jnp.int32)
    parts = [
        shared_part(w).reshape(-1, LANES)
        for w in (w_query, w_key, w_value, w_out, w_gate, w_up, w_down)
    ]
    gain_part = shared_part(gains)
    gain_each = gain_part.shape[0]
    attn, ffn = call(
        pack_kernel,
        [((MAIN, ATTN_A + ATTN_B), BF16), ((MAIN, 2 * FFN_A), BF16)],
        parts + [gain_part[None, :]],
        [((320, LANES), F32), ((MAIN, FF // 4), F32)],
    )
    columns_a = gathered_columns(SLOTS_A, me)
    columns_b = gathered_columns(SLOTS_B, me)
    owners_a = (jnp.asarray(SLOTS_A) ^ me)[:, None]
    owners_b = (jnp.asarray(SLOTS_B) ^ me)[:, None]
    fold = gain_fold()

    freq_table = 10000.0 ** (-2.0 * jnp.arange(HD // 2, dtype=F32) / HD)
    angle_rows = positions.astype(F32)[:, None] * freq_table[None, :]
    cos_rows = jnp.cos(angle_rows)
    sin_rows = jnp.sin(angle_rows)
    places = positions[:, None]
    small = (where, places, cos_rows, sin_rows, columns_a, columns_b, owners_a, owners_b)
    pieces, ffn, small = together(pieces_z(attn), ffn, small)
    where, places, cos_rows, sin_rows, columns_a, columns_b, owners_a, owners_b = small
    attn_z = stacked(*pieces)
    attn_a, attn_b = attn_z[:, :ATTN_A], attn_z[:, ATTN_A:]
    ffn_two = exchanged_part(ffn, 2 << Z_BITS[0])
    next_a, next_b = exchanged_part(attn_a, 1 << ORDER_A[0]), exchanged_part(attn_b, 1 << ORDER_B[0])
    attn_a, attn_b = stacked(attn_a, next_a), stacked(attn_b, next_b)
    ffn_one = exchanged_part(ffn, 1 << Z_BITS[0])
    ffn_three = exchanged_part(ffn, 3 << Z_BITS[0])
    next_a, next_b = exchanged_part(attn_a, 1 << ORDER_A[1]), exchanged_part(attn_b, 1 << ORDER_B[1])
    attn_a, attn_b = stacked(attn_a, next_a), stacked(attn_b, next_b)
    other_a = exchanged_part(attn_a, 1 << CORE)
    other_b = exchanged_part(attn_b, 1 << CORE)
    ffn_z = stacked(ffn, ffn_one, ffn_two, ffn_three)
    ffn_a, ffn_b = ffn_z[:, :FFN_A], ffn_z[:, FFN_A:]
    next_a, next_b = exchanged_part(ffn_a, 1 << ORDER_A[0]), exchanged_part(ffn_b, 1 << ORDER_B[0])

    rows = (BLK, 2 * DEPTH)
    query_low, kv_low, query_raw, key_raw, one_a, one_b, gain_d, gain_h = call(
        qkv_kernel,
        [
            ((BLK, QW), BF16),
            ((BLK, 2 * HD), BF16),
            ((BLK, QW), F32),
            ((BLK, HD), F32),
            (rows, BF16),
            (rows, BF16),
            ((4, D), F32),
            ((2, HD), F32),
        ],
        [tokens, owners_a, fold, columns_a, columns_b, attn_a, other_a, attn_b, other_b]
        + [cos_rows, sin_rows],
        windows=[(7, KV_WIDTH, 2), (8, KV_WIDTH, 2)],
        flops=9e9,
    )
    ffn_a, ffn_b = stacked(ffn_a, next_a), stacked(ffn_b, next_b)
    earlier = [passed_along(kv_low, "seq", back_step) for back_step in range(BACK, 0, -1)]
    heads_out, log_total, attn_proj, middle, two_a, two_b, out_w, kv_all = call(
        attend_kernel,
        [
            ((BLK, QW), BF16),
            ((BLK, HEADS * LANES), F32),
            ((BLK, D), F32),
            ((BLK, D), F32),
            (rows, BF16),
            (rows, BF16),
            ((QW, D), BF16),
            ((SPAN, 2 * HD), BF16),
        ],
        [where, tokens, places, gain_d, columns_a, columns_b, attn_b, other_b, query_low]
        + earlier
        + [kv_low],
        windows=[(6, 2 * D, 0), (7, 2 * D, 0)],
        scalars=1,
        flops=9e9,
    )
    next_a, next_b = exchanged_part(ffn_a, 1 << ORDER_A[1]), exchanged_part(ffn_b, 1 << ORDER_B[1])
    other_ffn_a, other_ffn_b = exchanged_part(ffn_a, 1 << CORE), exchanged_part(ffn_b, 1 << CORE)
    ffn_all = [ffn_a, next_a, other_ffn_a, exchanged_part(next_a, 1 << CORE)]
    ffn_all += [ffn_b, next_b, other_ffn_b, exchanged_part(next_b, 1 << CORE)]
    packed = ((HALF, FFN_A), BF16)
    whole = ((DEPTH, FFN_A), BF16)
    gate_up = ((DEPTH, FF + FF // 4), BF16)
    wide = ((BLK, FF), BF16)
    layer_out, ffn_out_gg, keep_a, send_a, keep_b, send_b, gate_g, up_g = call(
        ffn_kernel,
        [((BLK, D), BF16), ((1, D), F32), packed, packed, packed, packed, wide, wide],
        [where, middle, cotangent, gain_d, two_a, two_b] + ffn_all,
        [
            packed,
            packed,
            packed,
            packed,
            wide,
            wide,
            whole,
            whole,
            ((FF, D), BF16),
            ((FF, D), BF16),
            ((BLK, FF), F32),
            ((BLK, FF), F32),
            wide,
            ((2 * DEPTH, BLK), BF16),
            ((2 * DEPTH, BLK), BF16),
        ],
        scalars=1,
        left=8,
        outs_left=6,
        sems=32 + 34,
    )
    mid_grad, ffn_in_gg = call(
        ffn_back_kernel,
        [((BLK, D), F32), ((1, D), F32)],
        [middle, cotangent, gain_d, columns_a, columns_b, gate_g, up_g] + ffn_all,
        [wide, wide, gate_up, gate_up],
        left=10,
        sems=10,
    )
    came_a, came_b = exchanged_part(send_a, 1 << CORE), exchanged_part(send_b, 1 << CORE)
    mid_grad, came_a, came_b = together(mid_grad, came_a, came_b)
    keep_a, send_a = halved(added(keep_a, came_a))
    keep_b, send_b = halved(added(keep_b, came_b))
    cut = FF + FF // 4
    came_a = exchanged_part(send_a[:, :cut], 1 << ORDER_A[1])
    came_b = exchanged_part(send_b[:, :cut], 1 << ORDER_B[1])
    sixteen = ((HALF, QW + QW // 4), BF16)
    (
        kv_earlier,
        kv_own,
        query_keep,
        query_send,
        out_keep,
        out_send,
        back_a,
        attn_out_gg,
        query_gg,
    ) = call(
        attend_back_kernel,
        [
            ((BACK * BLK, 2 * HD), BF16),
            ((BLK, 2 * HD), F32),
            sixteen,
            sixteen,
            sixteen,
            sixteen,
            (rows, F32),
            ((1, D), F32),
            ((1, HD), F32),
        ],
        [where, mid_grad, attn_proj, places, gain_d, gain_h, out_w, heads_out, query_low]
        + [kv_all, log_total, query_raw, cos_rows, sin_rows, one_a, attn_a, other_a],
        [((QW, D), BF16), ((SPAN, 2 * HD), F32), ((BLK, QW), BF16), ((2 * DEPTH, BLK), BF16)],
        windows=[(15, QW + QW // 4, 0), (16, QW + QW // 4, 0)],
        scalars=1,
        flops=7e9,
    )
    kv_earlier, query_send, out_send, came_a, came_b = together(
        kv_earlier, query_send, out_send, came_a, came_b
    )
    came_a = [came_a, exchanged_part(send_a[:, cut:], 1 << ORDER_A[1])]
    came_b = [came_b, exchanged_part(send_b[:, cut:], 1 << ORDER_B[1])]
    came = [
        passed_along(kv_earlier[(BACK - step) * BLK : (BACK - step + 1) * BLK], "seq", -step)
        for step in range(1, BACK + 1)
    ]
    keep_a, send_a = halved(added(keep_a, jnp.concatenate(came_a, axis=1)))
    keep_b, send_b = halved(added(keep_b, jnp.concatenate(came_b, axis=1)))
    came_a = exchanged_part(send_a, 1 << ORDER_A[0])
    came_b = exchanged_part(send_b, 1 << ORDER_B[0])
    came_query = exchanged_part(query_send, 1 << CORE)
    came_out = exchanged_part(out_send, 1 << CORE)
    ffn_total = jnp.concatenate([added(keep_a, came_a), added(keep_b, came_b)], axis=1)
    query_keep, query_send = halved(added(query_keep, came_query))
    came_query = exchanged_part(query_send, 1 << ORDER_A[1])
    kv_width = KV_WIDTH + LANES
    input_grad, kv_keep, kv_send = call(
        input_kernel,
        [((BLK, D), F32), ((HALF, kv_width), BF16), ((HALF, kv_width), BF16)],
        [tokens, mid_grad, gain_d, gain_h, columns_a, columns_b, one_b, attn_b, other_b, kv_own]
        + came
        + [key_raw, cos_rows, sin_rows, back_a, owners_b, fold]
        + [attn_out_gg, ffn_out_gg, ffn_in_gg, query_gg],
        [((2 * DEPTH, BLK), BF16)],
        windows=[(7, KV_WIDTH, 2), (8, KV_WIDTH, 2)],
        limit=24,
        flops=5e9,
    )
    came_kv = exchanged_part(kv_send, 1 << CORE)
    ffn_then, _ = together(ffn_total, came_kv)
    ffn_came = [sent_z(ffn_then, k) for k in range(1, 4)]
    rest_keep, rest_send = halved(
        jnp.concatenate([added(out_keep, came_out), added(kv_keep, came_kv)], axis=1)
    )
    query_keep, query_send = halved(added(query_keep, came_query))
    came_query = exchanged_part(query_send, 1 << ORDER_A[0])
    came_rest = exchanged_part(rest_send, 1 << ORDER_B[1])
    rest_keep, rest_send = halved(added(rest_keep, came_rest))
    came_rest = exchanged_part(rest_send, 1 << ORDER_B[0])
    ffn_came, _ = together(ffn_came, came_rest)
    attn_total = jnp.concatenate(
        [added(query_keep, came_query), added(rest_keep, came_rest)], axis=1
    )
    attn_came = [sent_z(attn_total, k) for k in range(1, 4)]
    flat = [((160, LANES), F32), ((40, LANES), F32), ((320, LANES), F32)]
    grad_gate, grad_up, grad_down = call(
        unpack_ffn_kernel,
        [flat[2]] * 3,
        [ffn_total[:MAIN]] + ffn_came,
        [((MAIN, 2 * FFN_A), F32)],
        limit=16,
    )
    grad_query, grad_key, grad_value, grad_out, grad_gains = call(
        unpack_attn_kernel,
        [flat[0], flat[1], flat[1], flat[0], ((1, GAIN_EACH), F32)],
        [attn_total[:MAIN]] + attn_came,
        [((MAIN, attn_total.shape[1]), F32)],
        limit=16,
    )
    return (
        layer_out,
        input_grad,
        *(
            own_part(grad.reshape(-1))
            for grad in (
                grad_query,
                grad_key,
                grad_value,
                grad_out,
                grad_gate,
                grad_up,
                grad_down,
                grad_gains,
            )
        ),
    )


def solution(mesh):
    rows = P(AXES, None)
    flat = P(AXES)
    return jax.shard_map(
        local,
        mesh=mesh,
        in_specs=(rows, flat, rows) + (flat,) * 8,
        out_specs=(rows, rows) + (flat,) * 8,
        check_vma=False,
    )
```

```python
import functools
import numpy as np
import jax
import jax.numpy as jnp
from jax import lax
from jax.experimental import pallas as pl
from jax.experimental.pallas import tpu as pltpu
from jax.sharding import PartitionSpec as P

D = 640
HEADS = 4
HD = 256
FF = 2048
WIN = 512
BLK = 256
BACK = 2
AXES = ("dp", "seq")
F32 = jnp.float32
BF16 = jnp.bfloat16
QW = HEADS * HD
SPAN = (BACK + 1) * BLK

PARTS = 32
MAIN = 16
DEPTH = PARTS * MAIN
HALF = DEPTH // 2
KV_WIDTH = 2 * HD + HD // 2
LANES = 128
ATTN_A = QW + QW // 4 + LANES
ATTN_B = 2 * HD + HD // 2 + 2 * D
FFN_A = FF + FF // 4 + 2 * D
Z_BITS = (1, 2)
LOW, CORE, HIGH = 0, 3, 4
ORDER_A = (LOW, HIGH, CORE)
ORDER_B = (HIGH, LOW, CORE)

GAIN_SPANS = tuple((i * D, D) for i in range(4)) + ((4 * D, HD), (4 * D + HD, HD))
GAINS = 4 * D + 2 * HD
GAIN_EACH = GAINS // PARTS

epsilon = 1e-06
lowest = -1e30


def slot_shards(order):
    shards = np.arange(4, dtype=np.int32) << Z_BITS[0]
    for bit in order:
        shards = np.concatenate([shards, shards ^ (1 << bit)])
    return shards


SLOTS_A = slot_shards(ORDER_A)
SLOTS_B = slot_shards(ORDER_B)


def extra_bits():
    return (lax.axis_size("dp") * lax.axis_size("seq")).bit_length() - PARTS.bit_length()


def exchanged(value, mask):
    count = lax.axis_size("dp") * lax.axis_size("seq")
    return lax.ppermute(value, AXES, [(i, i ^ mask) for i in range(count)])


def exchanged_part(value, mask):
    return exchanged(value, mask << extra_bits())


def passed_along(value, axis, steps):
    count = lax.axis_size(axis)
    first, last = (max(0, -steps), min(count, count - steps))
    return lax.ppermute(value, axis, [(source, source + steps) for source in range(first, last)])


def dot(left, right, left_dim=1, right_dim=0):
    return lax.dot_general(
        left, right, (((left_dim,), (right_dim,)), ((), ())), preferred_element_type=F32
    )


def unit_of(values):
    inverse = lax.rsqrt(jnp.mean(values * values, axis=-1, keepdims=True) + epsilon)
    return values * inverse, inverse


def rms_values_grad(incoming, unit_rows, inverse, gain_row):
    scaled = incoming * gain_row
    return inverse * (scaled - unit_rows * jnp.mean(scaled * unit_rows, axis=-1, keepdims=True))


def rotate(values, cos_rows, sin_rows):
    middle_at = values.shape[-1] // 2
    first_half = values[..., :middle_at]
    second_half = values[..., middle_at:]
    return jnp.concatenate(
        [
            first_half * cos_rows - second_half * sin_rows,
            second_half * cos_rows + first_half * sin_rows,
        ],
        axis=-1,
    )


def row_sum(values):
    return jnp.sum(values, axis=0, keepdims=True)


def column(index):
    return pl.ds(index * LANES, LANES)


def pack_kernel(
    query, key, value, out, gate, up, down, gains, attn, ffn, wide, quarter
):
    def load(source):
        rows = source.shape[0]
        wide[:rows, :] = source[...].astype(F32)

    def put_main(target, at, blocks, block):
        target[:, pl.ds(at, LANES)] = wide[pl.ds(block, MAIN, stride=blocks), :].astype(BF16)

    def put_tail(row, at, blocks, block):
        quarter[4 * row : 4 * row + 4, pl.ds(at, LANES)] = wide[
            pl.ds(MAIN * blocks + block, 4, stride=blocks), :
        ]

    def put_matrix(source, target, at):
        load(source)
        blocks = source.shape[0] // 20
        for block in range(blocks):
            put_main(target, at + block * LANES, blocks, block)
            each = blocks // 4
            put_tail(block // each, block % each * LANES, blocks, block)
        width = blocks * LANES // 4
        target[:, pl.ds(at + blocks * LANES, width)] = quarter[:, :width].astype(BF16)

    def put_groups(target, at, groups):
        blocks = D // LANES
        for place, group in enumerate(groups):
            for block in range(blocks):
                target[:, pl.ds(at + place * D + block * LANES, LANES)] = wide[
                    pl.ds(group * MAIN * blocks + block, MAIN, stride=blocks), :
                ].astype(BF16)

    put_matrix(query, attn, 0)
    attn[:, pl.ds(QW + QW // 4, LANES)] = jnp.zeros((MAIN, LANES), BF16)
    attn[:, pl.ds(QW + QW // 4, GAIN_EACH)] = jnp.broadcast_to(gains[...], (MAIN, GAIN_EACH))
    for place, source in enumerate((key, value)):
        load(source)
        for block in range(2):
            put_main(attn, ATTN_A + 2 * D + place * HD + block * LANES, 2, block)
            put_tail(2 * place + block, 0, 2, block)
    attn[:, pl.ds(ATTN_A + 2 * D + 2 * HD, LANES)] = quarter[:, :LANES].astype(BF16)
    load(out)
    put_groups(attn, ATTN_A, (0, 1))
    put_matrix(gate, ffn, 0)
    put_matrix(up, ffn, FFN_A)
    load(down)
    put_groups(ffn, FF + FF // 4, (0, 1))
    put_groups(ffn, FFN_A + FF + FF // 4, (2, 3))


def unpack_matrix(source, at, target):
    blocks = target.shape[0] // 20
    each = blocks // 4
    tail_at = at + blocks * LANES
    for block in range(blocks):
        target[pl.ds(block, MAIN, stride=blocks), :] = source[:, pl.ds(at + block * LANES, LANES)]
        row = block // each * 4
        target[pl.ds(MAIN * blocks + block, 4, stride=blocks), :] = source[
            row : row + 4, pl.ds(tail_at + block % each * LANES, LANES)
        ]


def unpack_groups(source, at, target, groups):
    blocks = D // LANES
    for place, group in enumerate(groups):
        for block in range(blocks):
            target[pl.ds(group * MAIN * blocks + block, MAIN, stride=blocks), :] = source[
                :, pl.ds(at + place * D + block * LANES, LANES)
            ]


def unpack_ffn_kernel(own, one, two, three, gate, up, down, part):
    part[...] = sum(came[...].astype(F32) for came in (one, two, three)) + own[...]
    unpack_matrix(part, 0, gate)
    unpack_matrix(part, FFN_A, up)
    unpack_groups(part, FF + FF // 4, down, (0, 1))
    unpack_groups(part, FFN_A + FF + FF // 4, down, (2, 3))


def unpack_attn_kernel(own, one, two, three, query, key, value, out, gains, part):
    part[...] = sum(came[...].astype(F32) for came in (one, two, three)) + own[...]
    gains[...] = part[0:1, pl.ds(QW + QW // 4 + 2 * D + KV_WIDTH, GAIN_EACH)]
    unpack_matrix(part, 0, query)
    unpack_groups(part, QW + QW // 4, out, (0, 1))
    kv_at = QW + QW // 4 + 2 * D
    for place, target in enumerate((key, value)):
        for block in range(2):
            target[pl.ds(block, MAIN, stride=2), :] = part[
                :, pl.ds(kv_at + place * HD + block * LANES, LANES)
            ]
            row = 4 * (2 * place + block)
            target[pl.ds(2 * MAIN + block, 4, stride=2), :] = part[
                row : row + 4, pl.ds(kv_at + 2 * HD, LANES)
            ]


def quarter_mask(shape, dim, quarter):
    index = lax.broadcasted_iota(jnp.int32, shape, dim)
    return (index // 4 % 4 == quarter).astype(F32)


def quarter_rows(tail_rows, quarter):
    return tail_rows * quarter_mask((1, DEPTH), 1, quarter).astype(tail_rows.dtype)


def quarter_rows_t(tail_rows, quarter):
    return tail_rows * quarter_mask((DEPTH, 1), 0, quarter).astype(tail_rows.dtype)


def packed_product(rows, mine, other, main_at, tail_at, quarter, width):
    tail = quarter_rows(rows[:, DEPTH:], quarter)
    main_at, tail_at = pl.ds(main_at, width), pl.ds(tail_at, width)
    return (
        dot(rows[:, :HALF], mine[:, main_at])
        + dot(rows[:, HALF:DEPTH], other[:, main_at])
        + dot(tail[:, :HALF], mine[:, tail_at])
        + dot(tail[:, HALF:], other[:, tail_at])
    )


def packed_back(incoming, mine, other, main_at, tail_at, quarter):
    width = incoming.shape[1]
    main_at, tail_at = pl.ds(main_at, width), pl.ds(tail_at, width)
    tail = jnp.concatenate(
        [dot(incoming, mine[:, tail_at], 1, 1), dot(incoming, other[:, tail_at], 1, 1)], axis=1
    )
    return jnp.concatenate(
        [
            dot(incoming, mine[:, main_at], 1, 1),
            dot(incoming, other[:, main_at], 1, 1),
            quarter_rows(tail, quarter),
        ],
        axis=1,
    )


def packed_grad(rows_t, incoming, keep, send, main_at):
    grad = dot(rows_t, incoming).astype(BF16)
    main_at = pl.ds(main_at, incoming.shape[1])
    keep[:, main_at] = grad[:HALF]
    send[:, main_at] = grad[HALF:]


def permutation(columns):
    natural = lax.broadcasted_iota(jnp.int32, (D, 2 * DEPTH), 0)
    return (natural == columns[...]).astype(F32).astype(BF16)


def natural_columns(permuted, permutation):
    return dot(permuted.astype(BF16), permutation, 1, 1)


def place_groups(target, me, slots, mine, other, at, groups, count):
    for slot in range(PARTS):
        source = mine if slot < PARTS // 2 else other
        row = slot % (PARTS // 2) * MAIN
        first = (me ^ int(slots[slot])) * (count * MAIN)
        for place, group in enumerate(groups):
            rows = pl.ds(pl.multiple_of(first + group * MAIN, MAIN), MAIN)
            target[rows, :] = source[row : row + MAIN, pl.ds(at + place * D, D)]


def take_groups(whole, me, slots, keep, send, at, groups, count):
    for slot in range(PARTS):
        target = keep if slot < PARTS // 2 else send
        row = slot % (PARTS // 2) * MAIN
        first = (me ^ int(slots[slot])) * (count * MAIN)
        for place, group in enumerate(groups):
            rows = pl.ds(pl.multiple_of(first + group * MAIN, MAIN), MAIN)
            target[row : row + MAIN, pl.ds(at + place * D, D)] = whole[rows, :]


def gain_fold():
    lane = np.arange(GAINS)[:, None] % GAIN_EACH == np.arange(LANES)[None, :]
    return jnp.asarray(lane, BF16)


def gain_holders(owners, span):
    entry = span[0] + lax.broadcasted_iota(jnp.int32, (PARTS, span[1]), 1)
    first = owners[...] * GAIN_EACH
    return (entry >= first) & (entry < first + GAIN_EACH)


def slot_first_rows():
    row = lax.broadcasted_iota(jnp.int32, (PARTS, DEPTH), 1)
    return (row == MAIN * lax.broadcasted_iota(jnp.int32, (PARTS, DEPTH), 0)).astype(BF16)


def qkv_kernel(
    tokens, owners, fold, columns_a, columns_b, mine_a, other_a, mine_b, other_b, cos, sin,
    query_low, kv_low, query_raw, key_raw, rows_a, rows_b, gain_d, gain_h,
):
    first_rows = slot_first_rows()
    gain_at = pl.ds(QW + QW // 4, LANES)
    gain_rows = (
        dot(first_rows[:, :HALF], mine_a[:, gain_at])
        + dot(first_rows[:, HALF:], other_a[:, gain_at])
    ).astype(BF16)
    for place, span in enumerate(GAIN_SPANS):
        spread = dot(gain_rows, fold[span[0] : span[0] + span[1], :], 1, 1)
        total = row_sum(jnp.where(gain_holders(owners, span), spread, 0.0))
        if place < 4:
            gain_d[place : place + 1, :] = total
        else:
            gain_h[place - 4 : place - 3, :] = total
    unit, _ = unit_of(tokens[...].astype(F32))
    normed = (unit * gain_d[0:1, :]).astype(BF16)
    rows_a[...] = dot(normed, permutation(columns_a)).astype(BF16)
    rows_b[...] = dot(normed, permutation(columns_b)).astype(BF16)
    cos_rows, sin_rows = cos[...], sin[...]
    for head in range(HEADS):
        raw = packed_product(rows_a, mine_a, other_a, head * HD, QW, head, HD)
        at = pl.ds(head * HD, HD)
        query_raw[:, at] = raw
        normed_raw = unit_of(raw)[0] * gain_h[0:1, :]
        query_low[:, at] = (rotate(normed_raw, cos_rows, sin_rows) * HD**-0.5).astype(BF16)
    kv = [
        packed_product(rows_b, mine_b, other_b, c * LANES, 2 * HD, c, LANES) for c in range(4)
    ]
    raw = jnp.concatenate(kv[:2], axis=1)
    key_raw[...] = raw
    kv_low[:, :HD] = rotate(unit_of(raw)[0] * gain_h[1:2, :], cos_rows, sin_rows).astype(BF16)
    kv_low[:, HD:] = jnp.concatenate(kv[2:], axis=1).astype(BF16)


def allowed_pairs(block_index, positions):
    query_index = block_index * BLK + lax.broadcasted_iota(jnp.int32, (BLK, SPAN), 0)
    key_index = (block_index - BACK) * BLK + lax.broadcasted_iota(jnp.int32, (BLK, SPAN), 1)
    return (
        (key_index <= query_index)
        & (key_index > query_index - WIN)
        & (key_index >= query_index - positions[...])
    )


def attend_kernel(
    where, tokens, positions, gain_d, columns_a, columns_b, mine_b, other_b, query_low, kv_two,
    kv_one, kv_low, heads_out, log_total, attn_proj, middle, rows_a, rows_b, out_w, kv_all,
):
    for place, block in enumerate((kv_two, kv_one, kv_low)):
        kv_all[place * BLK : (place + 1) * BLK, :] = block[...]
    place_groups(out_w, where[0], SLOTS_B, mine_b, other_b, 0, (0, 1), 2)
    allowed = allowed_pairs(where[1], positions)
    for head in range(HEADS):
        at = pl.ds(head * HD, HD)
        scores = dot(query_low[:, at], kv_all[:, :HD], 1, 1)
        scores = jnp.where(allowed, scores, lowest)
        row_max = jnp.max(scores, axis=-1, keepdims=True)
        expo = jnp.exp(scores - row_max)
        total = jnp.sum(expo, axis=-1, keepdims=True)
        log_total[:, column(head)] = jnp.broadcast_to(row_max + jnp.log(total), (BLK, LANES))
        probs = (expo * (1.0 / total)).astype(BF16)
        heads_out[:, at] = dot(probs, kv_all[:, HD:]).astype(BF16)
    proj = dot(heads_out[...], out_w[...])
    attn_proj[...] = proj
    mid = tokens[...].astype(F32) + unit_of(proj)[0] * gain_d[1:2, :]
    middle[...] = mid
    normed = (unit_of(mid)[0] * gain_d[2:3, :]).astype(BF16)
    rows_a[...] = dot(normed, permutation(columns_a)).astype(BF16)
    rows_b[...] = dot(normed, permutation(columns_b)).astype(BF16)


TILE = 256
TILES = FF // TILE
TANH_SCALE = float(np.sqrt(2.0 / np.pi))


def ffn_pieces_in(pieces, weights, sems, spans):
    copies = [
        [
            pltpu.make_async_copy(
                piece.at[:, pl.ds(*span)],
                weights[at // 4].at[pl.ds(at % 4 * (DEPTH // 4), DEPTH // 4), pl.ds(*span)],
                sems.at[8 * place + at],
            )
            for at, piece in enumerate(pieces)
        ]
        for place, span in enumerate(spans)
    ]
    for group in copies:
        for copy in group:
            copy.start()
    return copies


def halves(weights):
    return weights.at[pl.ds(0, HALF)], weights.at[pl.ds(HALF, HALF)]


def ffn_kernel(
    where, middle, cotangent, gain_d, rows_a, rows_b, a_0, a_1, a_2, a_3, b_0, b_1, b_2, b_3,
    layer_out, gain_grad, keep_a_out, send_a_out, keep_b_out, send_b_out, gate_out, up_out,
    keep_a, send_a, keep_b, send_b, gate_g, up_g, weights_a, weights_b, down_w, down_grad, active_s, slope_s, hidden_s, rows_at, rows_bt, sems,
):
    me = where[0]
    down_at = FF + FF // 4
    spans = ((FF, FF // 4), (0, FF // 2), (FF // 2, FF // 2), (down_at, 2 * D))
    tail_in, first_in, second_in, down_in = ffn_pieces_in(
        (a_0, a_1, a_2, a_3, b_0, b_1, b_2, b_3), (weights_a, weights_b), sems, spans
    )
    rows_at[...] = rows_a[...].T
    rows_bt[...] = rows_b[...].T
    leaving = []

    def leave(at, width, pairs):
        for source, target in pairs:
            cols = pl.ds(at, width)
            copy = pltpu.make_async_copy(
                source.at[:, cols], target.at[:, cols], sems.at[32 + len(leaving)]
            )
            copy.start()
            leaving.append(copy)

    sums = ((send_a, send_a_out), (send_b, send_b_out), (keep_a, keep_a_out), (keep_b, keep_b_out))
    mine_a, other_a = halves(weights_a)
    mine_b, other_b = halves(weights_b)

    def forward(tile):
        at = pl.multiple_of(tile * TILE, TILE)
        tail_at = pl.multiple_of(FF + tile % 2 * TILE, TILE)
        gate = packed_product(rows_a, mine_a, other_a, at, tail_at, tile // 2, TILE)
        up = packed_product(rows_b, mine_b, other_b, at, tail_at, tile // 2, TILE)
        cols = pl.ds(at, TILE)
        square = gate * gate
        tanh = jnp.tanh(TANH_SCALE * (gate + 0.044715 * gate * square))
        active = 0.5 * gate * (1.0 + tanh)
        slope = 0.5 * (1.0 + tanh) + 0.5 * gate * (1.0 - tanh * tanh) * TANH_SCALE * (
            1.0 + 3.0 * 0.044715 * square
        )
        active_s[:, cols] = active
        slope_s[:, cols] = up * slope
        hidden_s[:, cols] = (active * up).astype(BF16)

    for copy in tail_in + first_in:
        copy.wait()
    pl.loop(0, TILES // 2, unroll=True)(forward)
    for copy in second_in:
        copy.wait()
    pl.loop(TILES // 2, TILES, unroll=True)(forward)
    for copy in down_in:
        copy.wait()
    place_groups(down_w, me, SLOTS_A, mine_a, other_a, down_at, (0, 1), 4)
    place_groups(down_w, me, SLOTS_B, mine_b, other_b, down_at, (2, 3), 4)
    proj = dot(hidden_s[...], down_w[...])
    unit, inverse = unit_of(proj)
    layer_out[...] = (middle[...] + unit * gain_d[3:4, :]).astype(BF16)
    out_grad = cotangent[...].astype(F32)
    gain_grad[0:1, :] = row_sum(out_grad * unit)
    proj_grad = rms_values_grad(out_grad, unit, inverse, gain_d[3:4, :]).astype(BF16)

    for tile in range(TILES):
        at = tile * TILE
        cols = pl.ds(at, TILE)
        hidden_grad = dot(proj_grad, down_w[cols, :], 1, 1)
        down_grad[cols, :] = dot(hidden_s[:, cols], proj_grad, 0, 0).astype(BF16)
        gate_grad = (hidden_grad * slope_s[:, cols]).astype(BF16)
        up_grad = (hidden_grad * active_s[:, cols]).astype(BF16)
        gate_g[:, cols] = gate_grad
        up_g[:, cols] = up_grad
        packed_grad(rows_at[:DEPTH, :], gate_grad, keep_a, send_a, at)
        packed_grad(rows_bt[:DEPTH, :], up_grad, keep_b, send_b, at)
        if tile % 2:
            leave(at - TILE, 2 * TILE, sums + ((gate_g, gate_out), (up_g, up_out)))

    width = FF // 4
    for rows_t, grad_s, keep, send in (
        (rows_at, gate_g, keep_a, send_a),
        (rows_bt, up_g, keep_b, send_b),
    ):
        tail_grad = jnp.zeros((DEPTH, width), F32)
        for quarter in range(4):
            part = grad_s[:, pl.ds(quarter * width, width)]
            tail_grad += dot(quarter_rows_t(rows_t[DEPTH:, :], quarter), part)
        keep[:, pl.ds(FF, width)] = tail_grad[:HALF].astype(BF16)
        send[:, pl.ds(FF, width)] = tail_grad[HALF:].astype(BF16)
    leave(FF, width, sums)
    take_groups(down_grad, me, SLOTS_A, keep_a, send_a, down_at, (0, 1), 4)
    take_groups(down_grad, me, SLOTS_B, keep_b, send_b, down_at, (2, 3), 4)
    leave(down_at, 2 * D, sums)
    for copy in leaving:
        copy.wait()


def ffn_back_kernel(
    middle, cotangent, gain_d, columns_a, columns_b, gate_in, up_in, a_0, a_1, a_2, a_3, b_0, b_1,
    b_2, b_3, mid_grad, gain_grad, gate_g, up_g, weights_a, weights_b, sems,
):
    (copies,) = ffn_pieces_in(
        (a_0, a_1, a_2, a_3, b_0, b_1, b_2, b_3),
        (weights_a, weights_b),
        sems,
        ((0, FF + FF // 4),),
    )
    grads_in = [
        pltpu.make_async_copy(gate_in, gate_g, sems.at[8]),
        pltpu.make_async_copy(up_in, up_g, sems.at[9]),
    ]
    for copy in grads_in:
        copy.start()
    for copy in grads_in:
        copy.wait()
    width = FF // 4
    normed_grad = jnp.zeros((BLK, D), F32)
    for at, grad_s, weights, columns in ((0, gate_g, weights_a, columns_a), (4, up_g, weights_b, columns_b)):
        for copy in copies[at : at + 4]:
            copy.wait()
        tail_back = jnp.zeros((BLK, DEPTH), F32)
        for quarter in range(4):
            part = grad_s[:, pl.ds(quarter * width, width)]
            tail_back += quarter_rows(dot(part, weights[:, pl.ds(FF, width)], 1, 1), quarter)
        back = jnp.concatenate([dot(grad_s[...], weights[:, :FF], 1, 1), tail_back], axis=1)
        normed_grad += natural_columns(back, permutation(columns))
    unit, inverse = unit_of(middle[...])
    gain_grad[0:1, :] = row_sum(normed_grad * unit)
    mid_grad[...] = cotangent[...].astype(F32) + rms_values_grad(
        normed_grad, unit, inverse, gain_d[2:3, :]
    )


def attend_back_kernel(
    where, mid_grad, attn_proj, positions, gain_d, gain_h, out_w, heads_out, query_low, kv_all,
    log_total, query_raw, cos, sin, rows_a, mine_a, other_a,
    kv_earlier, kv_own, query_keep, query_send, out_keep, out_send, back_a, gain_grad_d,
    gain_grad_h, out_grad_s, kv_grad, query_grad_s, rows_t,
):
    incoming = mid_grad[...]
    unit, inverse = unit_of(attn_proj[...])
    gain_grad_d[0:1, :] = row_sum(incoming * unit)
    proj_grad = rms_values_grad(incoming, unit, inverse, gain_d[1:2, :]).astype(BF16)
    for head in range(HEADS):
        at = pl.ds(head * HD, HD)
        out_grad_s[at, :] = dot(heads_out[:, at], proj_grad, 0, 0).astype(BF16)
    take_groups(out_grad_s, where[0], SLOTS_B, out_keep, out_send, 0, (0, 1), 2)
    allowed = allowed_pairs(where[1], positions)
    cos_rows, sin_rows = cos[...], sin[...]
    rows_t[...] = rows_a[...].T
    total_a = jnp.zeros((BLK, 2 * DEPTH), F32)
    gain_total = jnp.zeros((1, HD), F32)
    keys_grad = jnp.zeros((SPAN, HD), F32)
    values_grad = jnp.zeros((SPAN, HD), F32)
    for head in range(HEADS):
        at = pl.ds(head * HD, HD)
        heads_grad = dot(proj_grad, out_w[at, :], 1, 1).astype(BF16)
        scores = dot(query_low[:, at], kv_all[:, :HD], 1, 1)
        log_rows = log_total[:, pl.ds(head * LANES, 1)]
        probs = jnp.where(allowed, jnp.exp(jnp.where(allowed, scores - log_rows, 0.0)), 0.0)
        prob_grad = dot(heads_grad, kv_all[:, HD:], 1, 1)
        delta = jnp.sum(probs * prob_grad, axis=-1, keepdims=True)
        score_grad = (probs * (prob_grad - delta)).astype(BF16)
        keys_grad += dot(score_grad, query_low[:, at], 0, 0)
        values_grad += dot(probs.astype(BF16), heads_grad, 0, 0)
        query_grad = dot(score_grad, kv_all[:, :HD]) * HD**-0.5
        query_rot = rotate(query_grad, cos_rows, -sin_rows)
        unit, inverse = unit_of(query_raw[:, at])
        gain_total += row_sum(query_rot * unit)
        raw_grad = rms_values_grad(query_rot, unit, inverse, gain_h[0:1, :]).astype(BF16)
        query_grad_s[:, at] = raw_grad
        total_a += packed_back(raw_grad, mine_a, other_a, head * HD, QW, head)
        packed_grad(rows_t[:DEPTH, :], raw_grad, query_keep, query_send, head * HD)
    gain_grad_h[0:1, :] = gain_total
    kv_grad[:, :HD] = keys_grad
    kv_grad[:, HD:] = values_grad
    kv_earlier[...] = kv_grad[: BACK * BLK, :].astype(BF16)
    kv_own[...] = kv_grad[BACK * BLK :, :]
    back_a[...] = total_a
    tail = jnp.zeros((DEPTH, HD), F32)
    for head in range(HEADS):
        tail += dot(
            quarter_rows_t(rows_t[DEPTH:, :], head), query_grad_s[:, pl.ds(head * HD, HD)]
        )
    query_keep[:, pl.ds(QW, HD)] = tail[:HALF].astype(BF16)
    query_send[:, pl.ds(QW, HD)] = tail[HALF:].astype(BF16)


def input_kernel(
    tokens, mid_grad, gain_d, gain_h, columns_a, columns_b, rows_b, mine_b, other_b, kv_own, came_one,
    came_two, key_raw, cos, sin, back_a, owners, fold, out_gg, ffn_out_gg, ffn_in_gg, query_gg,
    input_grad, kv_keep, kv_send, rows_t,
):
    total = kv_own[...] + came_one[...].astype(F32) + came_two[...].astype(F32)
    key_rot = rotate(total[:, :HD], cos[...], -sin[...])
    unit, inverse = unit_of(key_raw[...])
    key_gg = row_sum(key_rot * unit)
    key_grad = rms_values_grad(key_rot, unit, inverse, gain_h[1:2, :]).astype(BF16)
    raw_grad = jnp.concatenate([key_grad, total[:, HD:].astype(BF16)], axis=1)
    rows_t[...] = rows_b[...].T
    back_b = jnp.zeros((BLK, 2 * DEPTH), F32)
    tail = jnp.zeros((DEPTH, LANES), F32)
    for c in range(4):
        part = raw_grad[:, c * LANES : (c + 1) * LANES]
        back_b += packed_back(part, mine_b, other_b, c * LANES, 2 * HD, c)
        tail += dot(quarter_rows_t(rows_t[DEPTH:, :], c), part)
    packed_grad(rows_t[:DEPTH, :], raw_grad, kv_keep, kv_send, 0)
    kv_keep[:, pl.ds(2 * HD, LANES)] = tail[:HALF].astype(BF16)
    kv_send[:, pl.ds(2 * HD, LANES)] = tail[HALF:].astype(BF16)
    normed_grad = natural_columns(back_a[...], permutation(columns_a)) + natural_columns(
        back_b, permutation(columns_b)
    )
    unit, inverse = unit_of(tokens[...].astype(F32))
    in_gg = row_sum(normed_grad * unit)
    gain_grads = (in_gg, out_gg[...], ffn_in_gg[...], ffn_out_gg[...], query_gg[...], key_gg)
    gain_rows = jnp.zeros((PARTS, LANES), F32)
    for grad, span in zip(gain_grads, GAIN_SPANS):
        held = jnp.where(gain_holders(owners, span), grad, 0.0).astype(BF16)
        gain_rows += dot(held, fold[span[0] : span[0] + span[1], :])
    gain_rows = dot(slot_first_rows(), gain_rows.astype(BF16), 0, 0).astype(BF16)
    gain_at = pl.ds(2 * HD + LANES, LANES)
    kv_keep[:, gain_at] = gain_rows[:HALF]
    kv_send[:, gain_at] = gain_rows[HALF:]
    input_grad[...] = mid_grad[...] + rms_values_grad(
        normed_grad, unit, inverse, gain_d[0:1, :]
    )


def call(kernel, outs, args, scratch=(), scalars=0, left=0, outs_left=0, sems=0, windows=(), flops=1e6, limit=56):
    vmem = pl.BlockSpec(memory_space=pltpu.VMEM)
    stays = pl.BlockSpec(memory_space=pl.ANY)
    shapes = [jax.ShapeDtypeStruct(shape, kind) for shape, kind in outs]
    places = [pl.BlockSpec(memory_space=pltpu.SMEM)] * scalars
    places += [vmem] * (len(args) - scalars - left) + [stays] * left
    for at, width, block in windows:
        rows = args[at].shape[0]
        places[at] = pl.BlockSpec((rows, width), functools.partial(lambda block, step: (0, block), block))
    buffers = [pltpu.VMEM(shape, kind) for shape, kind in scratch]
    if sems:
        buffers.append(pltpu.SemaphoreType.DMA((sems,)))
    return pl.pallas_call(
        kernel,
        out_shape=shapes,
        grid=(1,) if windows else (),
        in_specs=places,
        out_specs=[vmem] * (len(outs) - outs_left) + [stays] * outs_left,
        scratch_shapes=buffers,
        compiler_params=pltpu.CompilerParams(vmem_limit_bytes=limit * 1024 * 1024),
        cost_estimate=pl.CostEstimate(flops=int(flops), bytes_accessed=0, transcendentals=0),
    )(*args)


def together(*values):
    return lax.optimization_barrier(values)


def shared_part(flat):
    for bit in range(extra_bits()):
        other = exchanged(flat, 1 << bit)
        mine_first = (lax.axis_index(AXES) >> bit) & 1 == 0
        flat = jnp.where(
            mine_first, jnp.concatenate([flat, other]), jnp.concatenate([other, flat])
        )
    return flat


def own_part(flat):
    for bit in reversed(range(extra_bits())):
        halves = jnp.split(flat, 2)
        mine_first = (lax.axis_index(AXES) >> bit) & 1 == 0
        keep = jnp.where(mine_first, halves[0], halves[1])
        send = jnp.where(mine_first, halves[1], halves[0]).astype(BF16)
        flat = keep + exchanged(send, 1 << bit).astype(F32)
    return flat


def pieces_z(piece):
    return [piece] + [exchanged_part(piece, k << Z_BITS[0]) for k in range(1, 4)]


def stacked(*pieces):
    return jnp.concatenate(pieces, axis=0)


def added(keep, came):
    return keep.astype(F32) + came.astype(F32)


def halved(total):
    half = total.shape[0] // 2
    return total[:half].astype(BF16), total[half:].astype(BF16)


def sent_z(total, k):
    return exchanged_part(total[k * MAIN : (k + 1) * MAIN].astype(BF16), k << Z_BITS[0])


def gathered_columns(slots, me):
    first = (jnp.asarray(slots) ^ me)[:, None] * (D // PARTS)
    inner = jnp.arange(MAIN, dtype=jnp.int32)[None, :]
    return jnp.concatenate([(first + inner).reshape(-1), (first + MAIN + inner % 4).reshape(-1)])[
        None, :
    ]


def local(
    tokens, positions, cotangent, w_query, w_key, w_value, w_out, w_gate, w_up, w_down, gains
):
    me = lax.axis_index(AXES) >> extra_bits()
    block_index = lax.axis_index("seq")
    where = jnp.stack([me, block_index]).astype(jnp.int32)
    parts = [
        shared_part(w).reshape(-1, LANES)
        for w in (w_query, w_key, w_value, w_out, w_gate, w_up, w_down)
    ]
    gain_part = shared_part(gains)
    gain_each = gain_part.shape[0]
    attn, ffn = call(
        pack_kernel,
        [((MAIN, ATTN_A + ATTN_B), BF16), ((MAIN, 2 * FFN_A), BF16)],
        parts + [gain_part[None, :]],
        [((320, LANES), F32), ((MAIN, FF // 4), F32)],
    )
    columns_a = gathered_columns(SLOTS_A, me)
    columns_b = gathered_columns(SLOTS_B, me)
    owners_a = (jnp.asarray(SLOTS_A) ^ me)[:, None]
    owners_b = (jnp.asarray(SLOTS_B) ^ me)[:, None]
    fold = gain_fold()

    freq_table = 10000.0 ** (-2.0 * jnp.arange(HD // 2, dtype=F32) / HD)
    angle_rows = positions.astype(F32)[:, None] * freq_table[None, :]
    cos_rows = jnp.cos(angle_rows)
    sin_rows = jnp.sin(angle_rows)
    places = positions[:, None]
    small = (where, places, cos_rows, sin_rows, columns_a, columns_b, owners_a, owners_b)
    pieces, ffn, small = together(pieces_z(attn), ffn, small)
    where, places, cos_rows, sin_rows, columns_a, columns_b, owners_a, owners_b = small
    attn_z = stacked(*pieces)
    attn_a, attn_b = attn_z[:, :ATTN_A], attn_z[:, ATTN_A:]
    ffn_two = exchanged_part(ffn, 2 << Z_BITS[0])
    next_a, next_b = exchanged_part(attn_a, 1 << ORDER_A[0]), exchanged_part(attn_b, 1 << ORDER_B[0])
    attn_a, attn_b = stacked(attn_a, next_a), stacked(attn_b, next_b)
    ffn_one = exchanged_part(ffn, 1 << Z_BITS[0])
    ffn_three = exchanged_part(ffn, 3 << Z_BITS[0])
    next_a, next_b = exchanged_part(attn_a, 1 << ORDER_A[1]), exchanged_part(attn_b, 1 << ORDER_B[1])
    attn_a, attn_b = stacked(attn_a, next_a), stacked(attn_b, next_b)
    other_a = exchanged_part(attn_a, 1 << CORE)
    other_b = exchanged_part(attn_b, 1 << CORE)
    ffn_z = stacked(ffn, ffn_one, ffn_two, ffn_three)
    ffn_a, ffn_b = ffn_z[:, :FFN_A], ffn_z[:, FFN_A:]
    next_a, next_b = exchanged_part(ffn_a, 1 << ORDER_A[0]), exchanged_part(ffn_b, 1 << ORDER_B[0])

    rows = (BLK, 2 * DEPTH)
    query_low, kv_low, query_raw, key_raw, one_a, one_b, gain_d, gain_h = call(
        qkv_kernel,
        [
            ((BLK, QW), BF16),
            ((BLK, 2 * HD), BF16),
            ((BLK, QW), F32),
            ((BLK, HD), F32),
            (rows, BF16),
            (rows, BF16),
            ((4, D), F32),
            ((2, HD), F32),
        ],
        [tokens, owners_a, fold, columns_a, columns_b, attn_a, other_a, attn_b, other_b]
        + [cos_rows, sin_rows],
        windows=[(7, KV_WIDTH, 2), (8, KV_WIDTH, 2)],
        flops=9e9,
    )
    ffn_a, ffn_b = stacked(ffn_a, next_a), stacked(ffn_b, next_b)
    earlier = [passed_along(kv_low, "seq", back_step) for back_step in range(BACK, 0, -1)]
    heads_out, log_total, attn_proj, middle, two_a, two_b, out_w, kv_all = call(
        attend_kernel,
        [
            ((BLK, QW), BF16),
            ((BLK, HEADS * LANES), F32),
            ((BLK, D), F32),
            ((BLK, D), F32),
            (rows, BF16),
            (rows, BF16),
            ((QW, D), BF16),
            ((SPAN, 2 * HD), BF16),
        ],
        [where, tokens, places, gain_d, columns_a, columns_b, attn_b, other_b, query_low]
        + earlier
        + [kv_low],
        windows=[(6, 2 * D, 0), (7, 2 * D, 0)],
        scalars=1,
        flops=9e9,
    )
    next_a, next_b = exchanged_part(ffn_a, 1 << ORDER_A[1]), exchanged_part(ffn_b, 1 << ORDER_B[1])
    other_ffn_a, other_ffn_b = exchanged_part(ffn_a, 1 << CORE), exchanged_part(ffn_b, 1 << CORE)
    ffn_all = [ffn_a, next_a, other_ffn_a, exchanged_part(next_a, 1 << CORE)]
    ffn_all += [ffn_b, next_b, other_ffn_b, exchanged_part(next_b, 1 << CORE)]
    packed = ((HALF, FFN_A), BF16)
    whole = ((DEPTH, FFN_A), BF16)
    gate_up = ((DEPTH, FF + FF // 4), BF16)
    wide = ((BLK, FF), BF16)
    layer_out, ffn_out_gg, keep_a, send_a, keep_b, send_b, gate_g, up_g = call(
        ffn_kernel,
        [((BLK, D), BF16), ((1, D), F32), packed, packed, packed, packed, wide, wide],
        [where, middle, cotangent, gain_d, two_a, two_b] + ffn_all,
        [
            packed,
            packed,
            packed,
            packed,
            wide,
            wide,
            whole,
            whole,
            ((FF, D), BF16),
            ((FF, D), BF16),
            ((BLK, FF), F32),
            ((BLK, FF), F32),
            wide,
            ((2 * DEPTH, BLK), BF16),
            ((2 * DEPTH, BLK), BF16),
        ],
        scalars=1,
        left=8,
        outs_left=6,
        sems=32 + 34,
    )
    mid_grad, ffn_in_gg = call(
        ffn_back_kernel,
        [((BLK, D), F32), ((1, D), F32)],
        [middle, cotangent, gain_d, columns_a, columns_b, gate_g, up_g] + ffn_all,
        [wide, wide, gate_up, gate_up],
        left=10,
        sems=10,
    )
    came_a, came_b = exchanged_part(send_a, 1 << CORE), exchanged_part(send_b, 1 << CORE)
    mid_grad, came_a, came_b = together(mid_grad, came_a, came_b)
    keep_a, send_a = halved(added(keep_a, came_a))
    keep_b, send_b = halved(added(keep_b, came_b))
    cut = FF + FF // 4
    came_a = exchanged_part(send_a[:, :cut], 1 << ORDER_A[1])
    came_b = exchanged_part(send_b[:, :cut], 1 << ORDER_B[1])
    sixteen = ((HALF, QW + QW // 4), BF16)
    (
        kv_earlier,
        kv_own,
        query_keep,
        query_send,
        out_keep,
        out_send,
        back_a,
        attn_out_gg,
        query_gg,
    ) = call(
        attend_back_kernel,
        [
            ((BACK * BLK, 2 * HD), BF16),
            ((BLK, 2 * HD), F32),
            sixteen,
            sixteen,
            sixteen,
            sixteen,
            (rows, F32),
            ((1, D), F32),
            ((1, HD), F32),
        ],
        [where, mid_grad, attn_proj, places, gain_d, gain_h, out_w, heads_out, query_low]
        + [kv_all, log_total, query_raw, cos_rows, sin_rows, one_a, attn_a, other_a],
        [((QW, D), BF16), ((SPAN, 2 * HD), F32), ((BLK, QW), BF16), ((2 * DEPTH, BLK), BF16)],
        windows=[(15, QW + QW // 4, 0), (16, QW + QW // 4, 0)],
        limit=24,
        scalars=1,
        flops=7e9,
    )
    kv_earlier, query_send, out_send, came_a, came_b = together(
        kv_earlier, query_send, out_send, came_a, came_b
    )
    came_a = [came_a, exchanged_part(send_a[:, cut:], 1 << ORDER_A[1])]
    came_b = [came_b, exchanged_part(send_b[:, cut:], 1 << ORDER_B[1])]
    came = [
        passed_along(kv_earlier[(BACK - step) * BLK : (BACK - step + 1) * BLK], "seq", -step)
        for step in range(1, BACK + 1)
    ]
    keep_a, send_a = halved(added(keep_a, jnp.concatenate(came_a, axis=1)))
    keep_b, send_b = halved(added(keep_b, jnp.concatenate(came_b, axis=1)))
    came_a = exchanged_part(send_a, 1 << ORDER_A[0])
    came_b = exchanged_part(send_b, 1 << ORDER_B[0])
    came_query = exchanged_part(query_send, 1 << CORE)
    came_out = exchanged_part(out_send, 1 << CORE)
    ffn_total = jnp.concatenate([added(keep_a, came_a), added(keep_b, came_b)], axis=1)
    query_keep, query_send = halved(added(query_keep, came_query))
    came_query = exchanged_part(query_send, 1 << ORDER_A[1])
    kv_width = KV_WIDTH + LANES
    input_grad, kv_keep, kv_send = call(
        input_kernel,
        [((BLK, D), F32), ((HALF, kv_width), BF16), ((HALF, kv_width), BF16)],
        [tokens, mid_grad, gain_d, gain_h, columns_a, columns_b, one_b, attn_b, other_b, kv_own]
        + came
        + [key_raw, cos_rows, sin_rows, back_a, owners_b, fold]
        + [attn_out_gg, ffn_out_gg, ffn_in_gg, query_gg],
        [((2 * DEPTH, BLK), BF16)],
        windows=[(7, KV_WIDTH, 2), (8, KV_WIDTH, 2)],
        limit=24,
        flops=5e9,
    )
    came_kv = exchanged_part(kv_send, 1 << CORE)
    ffn_then, _ = together(ffn_total, came_kv)
    ffn_came = [sent_z(ffn_then, k) for k in range(1, 4)]
    rest_keep, rest_send = halved(
        jnp.concatenate([added(out_keep, came_out), added(kv_keep, came_kv)], axis=1)
    )
    query_keep, query_send = halved(added(query_keep, came_query))
    came_query = exchanged_part(query_send, 1 << ORDER_A[0])
    came_rest = exchanged_part(rest_send, 1 << ORDER_B[1])
    rest_keep, rest_send = halved(added(rest_keep, came_rest))
    came_rest = exchanged_part(rest_send, 1 << ORDER_B[0])
    ffn_came, _ = together(ffn_came, came_rest)
    attn_total = jnp.concatenate(
        [added(query_keep, came_query), added(rest_keep, came_rest)], axis=1
    )
    attn_came = [sent_z(attn_total, k) for k in range(1, 4)]
    flat = [((160, LANES), F32), ((40, LANES), F32), ((320, LANES), F32)]
    grad_gate, grad_up, grad_down = call(
        unpack_ffn_kernel,
        [flat[2]] * 3,
        [ffn_total[:MAIN]] + ffn_came,
        [((MAIN, 2 * FFN_A), F32)],
        limit=16,
    )
    grad_query, grad_key, grad_value, grad_out, grad_gains = call(
        unpack_attn_kernel,
        [flat[0], flat[1], flat[1], flat[0], ((1, GAIN_EACH), F32)],
        [attn_total[:MAIN]] + attn_came,
        [((MAIN, attn_total.shape[1]), F32)],
        limit=16,
    )
    return (
        layer_out,
        input_grad,
        *(
            own_part(grad.reshape(-1))
            for grad in (
                grad_query,
                grad_key,
                grad_value,
                grad_out,
                grad_gate,
                grad_up,
                grad_down,
                grad_gains,
            )
        ),
    )


def solution(mesh):
    rows = P(AXES, None)
    flat = P(AXES)
    return jax.shard_map(
        local,
        mesh=mesh,
        in_specs=(rows, flat, rows) + (flat,) * 8,
        out_specs=(rows, rows) + (flat,) * 8,
        check_vma=False,
    )
```
